512 devices in a mesh: nx: 32 (over z_hi, y, x), ny: 16 (over z_lo, core).
Axes of the slice: x: 4, y: 4, z: 16 (z_hi: 2, z_lo: 8; z = z_hi * 8 + z_lo), core: 2. Of those that a mesh axis runs over, the one named last changes fastest.
Arguments:
- state: float32 [16, 1536, 6144], P(None, 'nx', 'ny'), may hold values from -6 to 6
- diffuse: float32 [16, 1536, 6144], P(None, 'nx', 'ny'), may hold values from 0.02 to 0.12
- vertical: float32 [1536, 6144], P('nx', 'ny'), may hold values from 0.1 to 2
- rows_we: float32 [3, 2, 16, 2048], P(None, None, None, 'ny'), may hold values from -6 to 6
- rows_sn: float32 [3, 2, 16, 512], P(None, None, None, 'nx'), may hold values from -6 to 6
- fill_we: float32 [2, 16, 2048], P(None, None, 'ny'), may hold values from -6 to 6
- fill_sn: float32 [2, 16, 512], P(None, None, 'nx'), may hold values from -6 to 6
- index_we: int32 [6144], P('ny'), may hold values from 0 to 2046
- weight_we: float32 [6144], P('ny'), may hold values from 0 to 1
- index_sn: int32 [1536], P('nx'), may hold values from 0 to 510
- weight_sn: float32 [1536], P('nx'), may hold values from 0 to 1
- jump: int32 [2], replicated, may hold values from -1 to 1
Outputs:
- final_state: float32 [16, 1536, 6144], P(None, 'nx', 'ny')
The draws below stay inside these ranges and needn't reach their ends.
Inputs may be any that keep to these rules, and one draw needn't show every extreme that they name: Each entry of the jump is -1, 0 or 1. index_we[j] and index_sn[i] follow the nest ratio: they are nondecreasing, and index_we[j] - j // 3 and index_sn[i] - i // 3 each stay within ±2 of one fixed offset.
All inputs are finite; a program needn't handle non-finite values.
Results may differ from the reference program's by a relative error of at most 0.00002.
Values sent between devices are 32-bit elements; how exact they have to be, the bound alone decides.
No kernel may reach another device: no remote copies, remote signals or barrier semaphores. Data moves between devices by JAX's collectives and lax.ppermute only.
A program may use at most 64 MiB of HBM per device.

```python
import math
import jax
import jax.numpy as jnp
from jax import lax

NZ = 16
STEPS = 3
NX = 1536
NY = 6144
PX = 512
PY = 2048


def plant(values, key, least, high):
    dims = values.shape
    place = [jax.random.randint(jax.random.fold_in(key, axis), (), 0, dims[axis]) for axis in range(len(dims))]
    values = values.at[tuple(place)].set(least)
    longest = dims.index(max(dims))
    place[longest] = (place[longest] + 1) % dims[longest]
    return values.at[tuple(place)].set(high)


def steps_of(own_key, extent, pieces, low, largest):
    def one(axis_at, shards_of):
        steps = jax.random.uniform(jax.random.fold_in(jax.random.fold_in(own_key, 6), axis_at), (shards_of,), jnp.float32, low / len(pieces), largest / len(pieces))
        return jnp.repeat(jnp.exp(steps), extent[axis_at] // shards_of).reshape((-1,) + (1,) * (len(extent) - axis_at - 1))

    level = one(*pieces[0])
    for cut in pieces[1:]:
        level = level * one(*cut)
    return level


def scatter_about(rng, shape, width, limit, split=(), kind=jnp.bfloat16):
    values = jax.random.normal(rng, shape, jnp.float32) * width
    if len(split) > 0:
        values = steps_of(rng, shape, split, -0.22, 0.18) * values
    return jnp.clip(values, min=-limit, max=limit).astype(kind)


def setup_inputs(seed: int = 0) -> dict:
    key_of = jax.random.split(jax.random.key(seed), 13)
    return {
        "state": scatter_about(key_of[0], (NZ, NX, NY), 1.0, 6.0, ((1, 32), (2, 16)), jnp.float32),
        "diffuse": jnp.clip(jnp.exp(math.log(0.12) - 1.7917595 * jax.random.uniform(key_of[1], (NZ, NX, NY), jnp.float32) ** steps_of(key_of[1], (NZ, NX, NY), ((1, 32), (2, 16)), -0.2, 0.2)), 0.02, 0.12),
        "vertical": jnp.clip(jnp.exp(math.log(2.0) - 2.9957323 * jax.random.uniform(key_of[2], (NX, NY), jnp.float32) ** steps_of(key_of[2], (NX, NY), ((0, 32), (1, 16)), -0.2, 0.2)), 0.1, 2.0),
        "rows_we": scatter_about(key_of[3], (STEPS, 2, NZ, PY), 1.0, 6.0, ((3, 16),), jnp.float32),
        "rows_sn": scatter_about(key_of[4], (STEPS, 2, NZ, PX), 1.0, 6.0, ((3, 32),), jnp.float32),
        "fill_we": scatter_about(key_of[5], (2, NZ, PY), 1.0, 6.0, ((2, 16),), jnp.float32),
        "fill_sn": scatter_about(key_of[6], (2, NZ, PX), 1.0, 6.0, ((2, 32),), jnp.float32),
        "index_we": plant(jax.random.randint(key_of[7], (NY,), 0, PY - 1), jax.random.fold_in(key_of[7], 1), 0, (PY - 1) - 1).astype(jnp.int32),
        "weight_we": jnp.clip(1.0 * jax.random.uniform(key_of[8], (NY,), jnp.float32) ** steps_of(key_of[8], (NY,), ((0, 16),), -0.2, 0.2), 0.0, 1.0),
        "index_sn": plant(jax.random.randint(key_of[9], (NX,), 0, PX - 1), jax.random.fold_in(key_of[9], 1), 0, (PX - 1) - 1).astype(jnp.int32),
        "weight_sn": jnp.clip(1.0 * jax.random.uniform(key_of[10], (NX,), jnp.float32) ** steps_of(key_of[10], (NX,), ((0, 32),), -0.2, 0.2), 0.0, 1.0),
        "jump": jax.random.randint(key_of[11], (2,), -1, 2).astype(jnp.int32),
    }


def column_solve(explicit, vertical):
    layers = explicit.shape[0]
    factors = []
    sources = []
    for layer_index in range(layers):
        if layer_index == 0 or layer_index == layers - 1:
            diagonal_term = 1.0 + vertical
        else:
            diagonal_term = 1.0 + 2.0 * vertical
        if layer_index == 0:
            pivot_value = diagonal_term
            source_term = explicit[layer_index]
        else:
            pivot_value = diagonal_term + vertical * factors[-1]
            source_term = explicit[layer_index] + vertical * sources[-1]
        factors.append(-vertical / pivot_value)
        sources.append(source_term / pivot_value)
    result = [sources[-1]]
    for layer_index in range(layers - 2, -1, -1):
        result.append(sources[layer_index] - factors[layer_index] * result[-1])
    return jnp.stack(result[::-1], axis=0)


def blend(rows, index, weight):
    lower = rows[..., index]
    upper = rows[..., index + 1]
    return (1.0 - weight) * lower + weight * upper


def advance(field, diffuse, vertical, edge_y, edge_x):
    padded = jnp.pad(field, ((0, 0), (1, 1), (1, 1)))
    padded = padded.at[:, 0, 1:-1].set(edge_y[0])
    padded = padded.at[:, -1, 1:-1].set(edge_y[1])
    padded = padded.at[:, 1:-1, 0].set(edge_x[0])
    padded = padded.at[:, 1:-1, -1].set(edge_x[1])
    center = padded[:, 1:-1, 1:-1]
    laplace = padded[:, 2:, 1:-1] + padded[:, :-2, 1:-1] + padded[:, 1:-1, 2:] + padded[:, 1:-1, :-2] - 4.0 * center
    explicit = center + diffuse * laplace
    return column_solve(explicit, vertical)


def reference(state, diffuse, vertical, rows_we, rows_sn, fill_we, fill_sn, index_we, weight_we, index_sn, weight_sn, jump):
    edge_y = blend(rows_we, index_we, weight_we)
    edge_x = blend(rows_sn, index_sn, weight_sn)
    first = advance(state, diffuse, vertical, edge_y[0], edge_x[0])
    shift_x = jump[0].astype(jnp.int32)
    shift_y = jump[1].astype(jnp.int32)
    padded = jnp.pad(first, ((0, 0), (3, 3), (3, 3)))
    region = lax.dynamic_slice(padded, (jnp.int32(0), 3 + 3 * shift_x, 3 + 3 * shift_y), (NZ, NX, NY))
    source_x = jnp.arange(NX, dtype=jnp.int32) + 3 * shift_x
    source_y = jnp.arange(NY, dtype=jnp.int32) + 3 * shift_y
    coarse_y = jnp.clip(source_y, 0, NY - 1) // 3
    coarse_x = jnp.clip(source_x, 0, NX - 1) // 3
    west = fill_we[0][:, coarse_y][:, None, :]
    east = fill_we[1][:, coarse_y][:, None, :]
    south = fill_sn[0][:, coarse_x][:, :, None]
    north = fill_sn[1][:, coarse_x][:, :, None]
    below_x = (source_x < 0)[None, :, None]
    above_x = (source_x >= NX)[None, :, None]
    below_y = (source_y < 0)[None, None, :]
    above_y = (source_y >= NY)[None, None, :]
    moved = jnp.where(below_x, west, jnp.where(above_x, east, jnp.where(below_y, south, jnp.where(above_y, north, region))))
    second = advance(moved, diffuse, vertical, edge_y[1], edge_x[1])
    return advance(second, diffuse, vertical, edge_y[2], edge_x[2])
```

```python
import functools

import jax
import jax.numpy as jnp
from jax import lax
from jax.experimental import pallas as pl
from jax.experimental.pallas import tpu as pltpu
from jax.sharding import PartitionSpec as P

LV = 16
WX = 48
WY = 384
NG = WY // 128
HX = 8
STATE_ROWS = 6
COEF_ROWS = 5
COEF_AT = LV * STATE_ROWS
VERT_AT = COEF_AT + LV * COEF_ROWS
XROWS = 184


def rounds_of(count):
    if count == 32:
        return [[16], [4, 8, 12], [1, 2, 3]]
    if count == 16:
        return [[8], [2, 4, 6], [1]]
    masks, bit = [], count // 2
    while bit:
        masks.append([bit])
        bit //= 2
    return masks


def masks_of(count):
    have = [0]
    for masks in rounds_of(count):
        have = [m ^ h for m in [0] + masks for h in have]
    return have


def pack_kernel(place, state, diffuse, vertical, filler, interp, xa, xb, y_low, y_high):
    def rows(ref, high):
        at = WX - STATE_ROWS if high else 0
        bt = WX - COEF_ROWS if high else 0
        for l in range(NG):
            lanes = slice(128 * l, 128 * l + 128)
            for k in range(LV):
                ref[l, k * STATE_ROWS : (k + 1) * STATE_ROWS, :] = state[k, at : at + STATE_ROWS, lanes]
                ref[l, COEF_AT + k * COEF_ROWS : COEF_AT + (k + 1) * COEF_ROWS, :] = diffuse[
                    k, bt : bt + COEF_ROWS, lanes
                ]
            ref[l, VERT_AT : VERT_AT + COEF_ROWS, :] = vertical[bt : bt + COEF_ROWS, lanes]
            ref[l, VERT_AT + COEF_ROWS :, :] = jnp.zeros((XROWS - VERT_AT - COEF_ROWS, 128), jnp.float32)

    odd = place[2] % 2 == 1

    @pl.when(odd)
    def _():
        rows(xa, True)
        rows(xb, False)

    @pl.when(jnp.logical_not(odd))
    def _():
        rows(xa, False)
        rows(xb, True)

    lane = lax.broadcasted_iota(jnp.int32, (WX, 128), 1)
    row = lax.broadcasted_iota(jnp.int32, (WX, 128), 0)
    for ref, group, first in ((y_low, 0, 0), (y_high, NG - 1, 120)):
        lanes = slice(128 * group, 128 * group + 128)
        for which, field in enumerate((state, diffuse)):
            total = jnp.zeros((WX, 128), jnp.float32)
            for k in range(LV):
                part = pltpu.roll(field[k, :, lanes], (8 * k - first) % 128, 1)
                total = jnp.where((lane >= 8 * k) & (lane < 8 * k + 8), part, total)
            ref[:, 128 * which : 128 * which + 128] = total
        last = jnp.where(lane < 8, pltpu.roll(vertical[:, lanes], (-first) % 128, 1), 0.0)
        src = filler[:, 0:128]
        last = jnp.where(
            (lane >= 8) & (lane < 16), pltpu.roll(src, (8 - first) % 128, 1), last
        )
        pair = jnp.where(row == 0, interp[0:1, lanes], interp[1:2, lanes])
        last = jnp.where(
            (lane >= 16) & (lane < 24) & (row < 2), pltpu.roll(pair, (16 - first) % 128, 1), last
        )
        ref[:, 256:384] = last


def main_kernel(
    count_x, count_y, masks_y, place, state, diffuse, vertical, ra, rb, from_low, from_high, ca, cb,
    colpack, interp, chain_y, chain_x, colid, filler, out, es, ed, ev, mv, gv, fac, strip, ey, ex, pack, sem,
):
    dx, dy, nx, ny = place[0], place[1], place[2], place[3]
    copies = []
    for which, (src, dst) in enumerate(((state, es), (diffuse, ed))):
        for l in range(NG):
            copy = pltpu.make_async_copy(
                src.at[:, :, pl.ds(128 * l, 128)], dst.at[:, l, pl.ds(HX, WX), :], sem.at[NG * which + l]
            )
            copy.start()
            copies.append(copy)
    odd = nx % 2 == 1
    lane = lax.broadcasted_iota(jnp.int32, (8, 128), 1)
    lane64 = lax.broadcasted_iota(jnp.int32, (64, 128), 1)

    def beyond(at, size, l):
        a, b = ra[l, at : at + size, :], rb[l, at : at + size, :]
        return jnp.where(odd, b, a), jnp.where(odd, a, b)

    for l in range(NG):
        for k in range(LV):
            low, high = beyond(k * STATE_ROWS, STATE_ROWS, l)
            es[k, l, HX - STATE_ROWS : HX, :] = low
            es[k, l, HX + WX : HX + WX + STATE_ROWS, :] = high
            low, high = beyond(COEF_AT + k * COEF_ROWS, COEF_ROWS, l)
            ed[k, l, HX - COEF_ROWS : HX, :] = low
            ed[k, l, HX + WX : HX + WX + COEF_ROWS, :] = high
        low, high = beyond(VERT_AT, COEF_ROWS, l)
        ev[l, HX - COEF_ROWS : HX, :] = low
        ev[l, HX + WX : HX + WX + COEF_ROWS, :] = high
        ev[l, HX : HX + WX, :] = vertical[:, 128 * l : 128 * l + 128]

    low = jnp.where(odd, cb[...], ca[...])
    high = jnp.where(odd, ca[...], cb[...])
    for side, ref in enumerate((from_low, from_high)):
        strip[side, 0:HX, :] = low[8 * side : 8 * side + 8]
        strip[side, HX : HX + WX, :] = ref[...]
        strip[side, HX + WX : 64, :] = high[8 * side : 8 * side + 8]
    pack[0:HX, :] = low[0:8, 256:384]
    pack[HX : HX + WX, :] = colpack[...]
    pack[HX + WX : 64, :] = high[0:8, 256:384]
    for which, dst in enumerate((es, ed)):
        lanes = slice(128 * which, 128 * which + 128)
        for k in range(LV):
            dst[k, NG, 0:64, :] = jnp.where(
                lane64 < 64,
                pltpu.roll(strip[1, :, lanes], (-8 * k) % 128, 1),
                pltpu.roll(strip[0, :, lanes], (120 - 8 * k) % 128, 1),
            )
    ev[NG, 0:64, :] = jnp.where(
        lane64 < 64, strip[1, :, 256:384], pltpu.roll(strip[0, :, 256:384], 120, 1)
    )

    west, east = nx == 0, nx == count_x - 1
    south, north = ny == 0, ny == count_y - 1

    @pl.when(west | east)
    def _():
        lane1 = lax.broadcasted_iota(jnp.int32, (1, 128), 1)
        for l in range(NG + 1):
            got = []
            for item in range(2):
                if l < NG:
                    got.append(interp[item : item + 1, 128 * l : 128 * l + 128])
                else:
                    got.append(
                        jnp.where(
                            lane1 < 64,
                            pltpu.roll(strip[1, HX : HX + 8, 256:384], 112, 1)[item : item + 1],
                            pltpu.roll(strip[0, HX : HX + 8, 256:384], 104, 1)[item : item + 1],
                        )
                    )
            index = jnp.broadcast_to(got[0], (48, 128)).astype(jnp.int32)
            ends = []
            for offset in range(2):
                at = index + offset
                block, inside = at >> 7, at & 127
                total = jnp.zeros((48, 128), jnp.float32)
                for piece, mask in enumerate(masks_y):
                    value = jnp.take_along_axis(chain_y[piece], inside, axis=1, mode="promise_in_bounds")
                    total = jnp.where(block == (ny ^ mask), value, total)
                ends.append(total)
            ey[l] = (1.0 - got[1]) * ends[0] + got[1] * ends[1]

    @pl.when(south | north)
    def _():
        index = pack[:, 64:65].astype(jnp.int32)
        weight = pack[:, 65:66]
        ids = colid[0:1, :]
        spread = jnp.where(ids == index, 1.0 - weight, 0.0) + jnp.where(ids == index + 1, weight, 0.0)
        ex[0:64, :] = jnp.dot(
            spread, chain_x[...], preferred_element_type=jnp.float32, precision=lax.Precision.HIGHEST
        )

    def ghosts(field, step, row_low, row_high, shift):
        @pl.when(west)
        def _():
            for k in range(LV):
                for l in range(NG + 1):
                    field[k, l, row_low : row_low + 1, :] = ey[l, 16 * step + k : 16 * step + k + 1, :]

        @pl.when(east)
        def _():
            for k in range(LV):
                for l in range(NG + 1):
                    field[k, l, row_high : row_high + 1, :] = ey[l, 16 * step + k : 16 * step + k + 1, :]

        @pl.when(south | north)
        def _():
            at = jnp.where(south, 127, 0)
            lanes = lax.broadcasted_iota(jnp.int32, (56, 128), 1)
            for k in range(LV):
                col = ex[shift : shift + 56, 16 * step + k : 16 * step + k + 1]
                field[k, NG, 0:56, :] = jnp.where(lanes == at, col, field[k, NG, 0:56, :])

    def ghost_tail(step):
        @pl.when(south | north)
        def _():
            at = jnp.where(south, 127, 0)
            for k in range(LV):
                col = ex[56:64, 16 * step + k : 16 * step + k + 1]
                es[k, NG, 56:64, :] = jnp.where(lane == at, col, es[k, NG, 56:64, :])

    for copy in copies:
        copy.wait()
    ghosts(es, 0, HX - 1, HX + WX, 0)
    ghost_tail(0)

    def sideways(c):
        lefts = [pltpu.roll(x, 1, 1) for x in c]
        rights = [pltpu.roll(x, 127, 1) for x in c]
        n = len(c)
        left = [jnp.where(lane == 0, lefts[l - 1], lefts[l]) for l in range(n)]
        right = [jnp.where(lane == 127, rights[(l + 1) % n], rights[l]) for l in range(n)]
        return left, right

    def advance(field, at, coef_at, groups, write_source, read_source, write):
        g = [ev[l, pl.ds(coef_at, 8), :] for l in range(groups)]
        factor, source = [None] * groups, [None] * groups
        for k in range(LV):
            c = [field[k, l, pl.ds(at, 8), :] for l in range(NG + 1)]
            left, right = sideways(c)
            for l in range(groups):
                lap = (
                    field[k, l, pl.ds(at + 1, 8), :]
                    + field[k, l, pl.ds(at - 1, 8), :]
                    + right[l]
                    + left[l]
                    - 4.0 * c[l]
                )
                explicit = c[l] + ed[k, l, pl.ds(coef_at, 8), :] * lap
                diagonal = 1.0 + (g[l] if k in (0, LV - 1) else 2.0 * g[l])
                if k > 0:
                    diagonal = diagonal + g[l] * factor[l]
                    explicit = explicit + g[l] * source[l]
                inverse = 1.0 / diagonal
                factor[l] = -g[l] * inverse
                source[l] = explicit * inverse
                fac[k, l] = factor[l]
                if k < LV - 1:
                    write_source(k, l, source[l])
        value = source
        write(LV - 1, value)
        for k in range(LV - 2, -1, -1):
            value = [read_source(k, l) - fac[k, l] * value[l] for l in range(groups)]
            write(k, value)

    turn = (128 - 3 * dy) % 128

    @pl.loop(0, 7)
    def _(t):
        to = pl.multiple_of(8 * t, 8)

        def put(k, l, x):
            mv[k, l, pl.ds(to, 8), :] = x

        def take(k, l):
            return mv[k, l, pl.ds(to, 8), :]

        def moved(k, values):
            turned = [pltpu.roll(x, turn, 1) for x in values]
            for l in range(NG + 1):
                x = jnp.where(lane >= 128 - 3 * dy, turned[(l + 1) % (NG + 1)], turned[l])
                put(k, l, jnp.where(lane < -3 * dy, turned[l - 1], x))

        at = HX - 2 + 3 * dx + 8 * t
        advance(es, at, at, NG + 1, put, take, moved)

    @pl.when((south & (dy < 0)) | (north & (dy > 0)))
    def _():
        row = lax.broadcasted_iota(jnp.int32, (56, 128), 0)
        cell = (((row + 4) * 21846) >> 16) - 2 + dx
        lanes = lax.broadcasted_iota(jnp.int32, (56, 128), 1)
        total = jnp.zeros((56, 128), jnp.float32)
        for q in range(-2, 18):
            r = q + 8 if q < 0 else (q + HX if q < 8 else q + 40)
            total = jnp.where(cell == q, pack[r : r + 1, :], total)

        for is_side, side, l, first in ((south, 0, 0, 0), (north, 1, NG - 1, 125)):

            @pl.when(is_side)
            def _():
                inside = (lanes >= first) & (lanes < first + 3)
                for k in range(LV):
                    n = 96 + 16 * side + k
                    mv[k, l, 0:56, :] = jnp.where(inside, total[:, n : n + 1], mv[k, l, 0:56, :])

    @pl.when((west & (dx < 0)) | (east & (dx > 0)))
    def _():
        lane16 = lax.broadcasted_iota(jnp.int32, (16, 128), 1)
        for is_side, side, first in ((west, 0, 2), (east, 1, 47)):

            @pl.when(is_side)
            def _():
                rows = slice(16 * side, 16 * side + 16)
                own = filler[rows, :]
                ring = jnp.where(
                    lane16 < 64,
                    pltpu.roll(strip[1, HX + 16 * side : HX + 16 * side + 16, 256:384], 120, 1),
                    pltpu.roll(strip[0, HX + 16 * side : HX + 16 * side + 16, 256:384], 112, 1),
                )
                for l in range(NG + 1):
                    column = lane16 + 128 * l
                    if l == NG:
                        column = jnp.where(lane16 < 64, column, lane16 - 128)
                    cell = (((column + 384) * 21846) >> 16) - 128 + dy
                    cell = jnp.clip(cell, -128 * ny, 128 * (count_y - ny) - 1)
                    inside = cell & 127
                    a = jnp.take_along_axis(own, inside, axis=1, mode="promise_in_bounds")
                    b = jnp.take_along_axis(ring, inside, axis=1, mode="promise_in_bounds")
                    ey[l, 0:16, :] = jnp.where((cell >= 0) & (cell < 128), a, b)
                    for k in range(LV):
                        mv[k, l, first : first + 3, :] = jnp.broadcast_to(ey[l, k : k + 1, :], (3, 128))

    ghosts(mv, 1, 1, WX + 2, HX - 2)

    @pl.loop(0, 7)
    def _(t):
        to = pl.multiple_of(8 * t, 8)

        def put(k, l, x):
            gv[k, l, pl.ds(to, 8), :] = x

        def take(k, l):
            return gv[k, l, pl.ds(to, 8), :]

        def keep(k, values):
            for l in range(NG + 1):
                put(k, l, values[l])

        advance(mv, 1 + 8 * t, HX - 1 + 8 * t, NG + 1, put, take, keep)

    ghosts(gv, 2, 0, WX + 1, HX - 1)

    @pl.loop(0, 6)
    def _(t):
        to = pl.multiple_of(8 * t, 8)

        def put(k, l, x):
            out[k, pl.ds(to, 8), 128 * l : 128 * l + 128] = x

        def take(k, l):
            return out[k, pl.ds(to, 8), 128 * l : 128 * l + 128]

        def keep(k, values):
            for l in range(NG):
                put(k, l, values[l])

        advance(gv, 1 + 8 * t, HX + 8 * t, NG, put, take, keep)


def on_device(
    state,
    diffuse,
    vertical,
    rows_we,
    rows_sn,
    fill_we,
    fill_sn,
    index_we,
    weight_we,
    index_sn,
    weight_sn,
    jump,
):
    f32 = jnp.float32
    count_x, count_y = lax.axis_size("nx"), lax.axis_size("ny")
    nx, ny = lax.axis_index("nx"), lax.axis_index("ny")
    both = ("nx", "ny")
    place = jnp.stack([jump[0], jump[1], nx, ny]).astype(jnp.int32)
    odd = nx % 2

    filler = fill_we.reshape(32, 128)
    interp = jnp.stack([index_we.astype(f32), weight_we])
    interp = jnp.pad(interp, ((0, 6), (0, 0)))
    vmem = pl.BlockSpec(memory_space=pltpu.VMEM)
    smem = pl.BlockSpec(memory_space=pltpu.SMEM)
    xa, xb, y_low, y_high = pl.pallas_call(
        pack_kernel,
        out_shape=(
            jax.ShapeDtypeStruct((NG, XROWS, 128), f32),
            jax.ShapeDtypeStruct((NG, XROWS, 128), f32),
            jax.ShapeDtypeStruct((WX, WY), f32),
            jax.ShapeDtypeStruct((WX, WY), f32),
        ),
        in_specs=[smem] + [vmem] * 5,
        out_specs=(vmem,) * 4,
        compiler_params=pltpu.CompilerParams(vmem_limit_bytes=40 << 20),
        name="pack",
    )(place, state, diffuse, vertical, jnp.pad(filler, ((0, 16), (0, 0))), interp)

    pairs_a = [(i, i + 1) for i in range(1, count_x - 1, 2)]
    pairs_a += [(b, a) for a, b in pairs_a]
    pairs_b = [(i, i + 1) for i in range(0, count_x, 2)]
    pairs_b += [(b, a) for a, b in pairs_b]
    up = [(i, i + 1) for i in range(count_y - 1)]
    down = [(b, a) for a, b in up]
    ra = lax.ppermute(xa, "nx", pairs_a)

    chain_x = jnp.where(ny == 0, rows_sn[:, 0], rows_sn[:, 1]).reshape(48, 16)
    chain_x = jnp.pad(chain_x.T, ((0, 0), (0, 80)))[None]
    chain_y = jnp.where(nx == 0, rows_we[:, 0], rows_we[:, 1]).reshape(48, 128)[None]

    def grow(chain, masks, pairs):
        return jnp.concatenate([chain] + [lax.ppermute(chain, both, pairs(m)) for m in masks])

    def pairs_x(mask):
        return [(i * count_y + n, (i ^ mask) * count_y + n) for n in (0, count_y - 1) for i in range(count_x)]

    def pairs_y(mask):
        return [(n * count_y + j, n * count_y + (j ^ mask)) for n in (0, count_x - 1) for j in range(count_y)]

    rb = lax.ppermute(xb, "nx", pairs_b)
    from_low = lax.ppermute(y_high, "ny", up)
    from_high = lax.ppermute(y_low, "ny", down)
    for mx, my in zip(rounds_of(count_x), rounds_of(count_y), strict=True):
        chain_x = grow(chain_x, mx, pairs_x)
        chain_y = grow(chain_y, my, pairs_y)
    masks_x, masks_y = masks_of(count_x), masks_of(count_y)
    chain_x = chain_x.reshape(16 * count_x, 128)
    blocks = nx ^ jnp.array(masks_x, jnp.int32)
    colid = (blocks[:, None] * 16 + jnp.arange(16, dtype=jnp.int32)).reshape(1, -1)
    colid = jnp.broadcast_to(colid, (8, 16 * count_x))

    fill_t = fill_sn.reshape(32, 16).T
    fill_t = jnp.pad(fill_t.reshape(2, 8, 32), ((0, 0), (0, 32), (0, 0))).reshape(80, 32)[:WX]
    colpack = jnp.concatenate(
        [
            jnp.zeros((WX, 64), f32),
            index_sn.astype(f32)[:, None],
            weight_sn[:, None],
            jnp.zeros((WX, 30), f32),
            fill_t,
        ],
        axis=1,
    )

    def corner(start):
        low = lax.dynamic_slice(from_low, (start, 0), (8, WY))
        high = lax.dynamic_slice(from_high, (start, 0), (8, WY))
        own = jnp.pad(lax.dynamic_slice(colpack, (start, 0), (8, 128)), ((0, 0), (256, 0)))
        clear = lax.broadcasted_iota(jnp.int32, (8, WY), 1) < 256 + 64
        return jnp.concatenate([jnp.where(clear, low, own), high])

    ca = lax.ppermute(corner(40 * odd), "nx", pairs_a)
    cb = lax.ppermute(corner(40 - 40 * odd), "nx", pairs_b)

    any_ = pl.BlockSpec(memory_space=pl.ANY)
    return pl.pallas_call(
        functools.partial(main_kernel, count_x, count_y, masks_y),
        out_shape=jax.ShapeDtypeStruct((LV, WX, WY), f32),
        in_specs=[smem, any_, any_] + [vmem] * 13,
        out_specs=vmem,
        scratch_shapes=[
            pltpu.VMEM((LV, NG + 1, 72, 128), f32),
            pltpu.VMEM((LV, NG + 1, 72, 128), f32),
            pltpu.VMEM((NG + 1, 72, 128), f32),
            pltpu.VMEM((LV, NG + 1, 64, 128), f32),
            pltpu.VMEM((LV, NG + 1, 64, 128), f32),
            pltpu.VMEM((LV, NG + 1, 8, 128), f32),
            pltpu.VMEM((2, 64, WY), f32),
            pltpu.VMEM((NG + 1, 48, 128), f32),
            pltpu.VMEM((64, 128), f32),
            pltpu.VMEM((64, 128), f32),
            pltpu.SemaphoreType.DMA((2 * NG,)),
        ],
        compiler_params=pltpu.CompilerParams(vmem_limit_bytes=48 << 20),
        name="steps",
    )(
        place, state, diffuse, vertical, ra, rb, from_low, from_high, ca, cb,
        colpack, interp, chain_y, chain_x, colid, filler,
    )


def solution(mesh):
    return jax.shard_map(
        on_device,
        mesh=mesh,
        in_specs=(
            P(None, "nx", "ny"),
            P(None, "nx", "ny"),
            P("nx", "ny"),
            P(None, None, None, "ny"),
            P(None, None, None, "nx"),
            P(None, None, "ny"),
            P(None, None, "nx"),
            P("ny"),
            P("ny"),
            P("nx"),
            P("nx"),
            P(),
        ),
        out_specs=P(None, "nx", "ny"),
        check_vma=False,
    )
```

```python
import functools

import jax
import jax.numpy as jnp
from jax import lax
from jax.experimental import pallas as pl
from jax.experimental.pallas import tpu as pltpu
from jax.sharding import PartitionSpec as P

LV = 16
WX = 48
WY = 384
NG = WY // 128
HX = 8
STATE_ROWS = 6
COEF_ROWS = 5
COEF_AT = LV * STATE_ROWS
VERT_AT = COEF_AT + LV * COEF_ROWS
XROWS = 184


def rounds_of(count):
    if count == 32:
        return [[16], [4, 8, 12], [1, 2, 3]]
    if count == 16:
        return [[8], [2, 4, 6], [1]]
    return [[2], [1], []]


def masks_of(rounds):
    have = [0]
    for masks in rounds:
        have = [m ^ h for m in [0] + masks for h in have]
    return have


def pack_kernel(
    state_hbm, diffuse_hbm, vertical, rows_we, rows_sn, fill_we, fill_sn, index_we, weight_we, index_sn, weight_sn,
    xa, xb, y_low, y_high, chain_x, chain_y, colpack, interp, state, diffuse, square, sem,
):
    copies = [
        pltpu.make_async_copy(state_hbm, state, sem.at[0]),
        pltpu.make_async_copy(diffuse_hbm, diffuse, sem.at[1]),
    ]
    for copy in copies:
        copy.start()
    nx, ny = lax.axis_index("nx"), lax.axis_index("ny")
    odd = nx % 2 == 1

    side_x = jnp.where(ny == 0, 0, 1)
    side_y = jnp.where(nx == 0, 0, 1)
    lane = lax.broadcasted_iota(jnp.int32, (128, 128), 1)
    square[...] = jnp.zeros((128, 128), jnp.float32)
    for step in range(3):
        chain_y[0, 16 * step : 16 * step + 16, :] = rows_we[step, side_y]
        square[16 * step : 16 * step + 16, 0:16] = rows_sn[step, side_x]
    chain_x[0] = square[...].T[0:16]
    square[0:48, :] = jnp.zeros((48, 128), jnp.float32)
    square[96:112, 0:16] = fill_sn[0]
    square[112:128, 0:16] = fill_sn[1]
    square[64:65, 0:WX] = index_sn[...].astype(jnp.float32).reshape(1, WX)
    square[65:66, 0:WX] = weight_sn[...].reshape(1, WX)
    whole = square[...]
    row = lax.broadcasted_iota(jnp.int32, (128, 128), 0)
    whole = jnp.where((lane < 8) | (row < 96), whole, pltpu.roll(whole, 32, 1))
    colpack[...] = whole.T[0:WX]
    interp[...] = jnp.zeros((8, WY), jnp.float32)
    interp[0:1, :] = index_we[...].astype(jnp.float32).reshape(1, WY)
    interp[1:2, :] = weight_we[...].reshape(1, WY)
    square[0:16, :] = fill_we[0]
    square[16:32, :] = fill_we[1]

    def rows(ref, high):
        at = WX - STATE_ROWS if high else 0
        bt = WX - COEF_ROWS if high else 0
        for l in range(NG):
            lanes = slice(128 * l, 128 * l + 128)
            for k in range(LV):
                ref[l, k * STATE_ROWS : (k + 1) * STATE_ROWS, :] = state[k, at : at + STATE_ROWS, lanes]
                ref[l, COEF_AT + k * COEF_ROWS : COEF_AT + (k + 1) * COEF_ROWS, :] = diffuse[
                    k, bt : bt + COEF_ROWS, lanes
                ]
            ref[l, VERT_AT : VERT_AT + COEF_ROWS, :] = vertical[bt : bt + COEF_ROWS, lanes]
            ref[l, VERT_AT + COEF_ROWS :, :] = jnp.zeros((XROWS - VERT_AT - COEF_ROWS, 128), jnp.float32)

    for copy in copies:
        copy.wait()

    @pl.when(odd)
    def _():
        rows(xa, True)
        rows(xb, False)

    @pl.when(jnp.logical_not(odd))
    def _():
        rows(xa, False)
        rows(xb, True)

    lane = lax.broadcasted_iota(jnp.int32, (WX, 128), 1)
    row = lax.broadcasted_iota(jnp.int32, (WX, 128), 0)
    for ref, group, first in ((y_low, 0, 0), (y_high, NG - 1, 120)):
        lanes = slice(128 * group, 128 * group + 128)
        for which, field in enumerate((state, diffuse)):
            total = jnp.zeros((WX, 128), jnp.float32)
            for k in range(LV):
                part = pltpu.roll(field[k, :, lanes], (8 * k - first) % 128, 1)
                total = jnp.where((lane >= 8 * k) & (lane < 8 * k + 8), part, total)
            ref[:, 128 * which : 128 * which + 128] = total
        last = jnp.where(lane < 8, pltpu.roll(vertical[:, lanes], (-first) % 128, 1), 0.0)
        last = jnp.where(
            (lane >= 8) & (lane < 16), pltpu.roll(square[0:WX, :], (8 - first) % 128, 1), last
        )
        pair = jnp.where(row == 0, interp[0:1, lanes], interp[1:2, lanes])
        last = jnp.where(
            (lane >= 16) & (lane < 24) & (row < 2), pltpu.roll(pair, (16 - first) % 128, 1), last
        )
        ref[:, 256:384] = last


def corner_kernel(from_low, from_high, colpack, ca, cb):
    odd = lax.axis_index("nx") % 2 == 1
    clear = lax.broadcasted_iota(jnp.int32, (8, 128), 1) < 64

    def rows(ref, at):
        ref[0:8, 0:256] = from_low[at : at + 8, 0:256]
        ref[0:8, 256:384] = jnp.where(clear, from_low[at : at + 8, 256:384], colpack[at : at + 8, :])
        ref[8:16, :] = from_high[at : at + 8, :]

    @pl.when(odd)
    def _():
        rows(ca, 40)
        rows(cb, 0)

    @pl.when(jnp.logical_not(odd))
    def _():
        rows(ca, 0)
        rows(cb, 40)


def join_kernel(count_x, count_y, after, *refs):
    ins, (out_x, out_y) = refs[:-2], refs[-2:]
    for out, parts in ((out_x, ins[:count_x]), (out_y, ins[count_x : count_x + count_y])):
        at = 0
        for part in parts:
            out[at : at + part.shape[0]] = part[...]
            at += part.shape[0]


def main_kernel(
    count_x, count_y, plan_x, plan_y, jump, state, diffuse, vertical, ra, rb, from_low, from_high, ca, cb,
    colpack, interp, fill_we, *refs,
):
    chain_x, refs = refs[: len(plan_x)], refs[len(plan_x) :]
    chain_y, refs = refs[: len(plan_y)], refs[len(plan_y) :]
    out, es, ed, ev, mv, gv, fac, strip, ey, ex, pack, sem = refs
    dx, dy = jump[0], jump[1]
    nx, ny = lax.axis_index("nx"), lax.axis_index("ny")
    copies = []
    for which, (src, dst) in enumerate(((state, es), (diffuse, ed))):
        for l in range(NG):
            copy = pltpu.make_async_copy(
                src.at[:, :, pl.ds(128 * l, 128)], dst.at[:, l, pl.ds(HX, WX), :], sem.at[NG * which + l]
            )
            copy.start()
            copies.append(copy)
    odd = nx % 2 == 1
    lane = lax.broadcasted_iota(jnp.int32, (8, 128), 1)
    lane64 = lax.broadcasted_iota(jnp.int32, (64, 128), 1)

    def beyond(at, size, l):
        a, b = ra[l, at : at + size, :], rb[l, at : at + size, :]
        return jnp.where(odd, b, a), jnp.where(odd, a, b)

    for l in range(NG):
        for k in range(LV):
            low, high = beyond(k * STATE_ROWS, STATE_ROWS, l)
            es[k, l, HX - STATE_ROWS : HX, :] = low
            es[k, l, HX + WX : HX + WX + STATE_ROWS, :] = high
            low, high = beyond(COEF_AT + k * COEF_ROWS, COEF_ROWS, l)
            ed[k, l, HX - COEF_ROWS : HX, :] = low
            ed[k, l, HX + WX : HX + WX + COEF_ROWS, :] = high
        low, high = beyond(VERT_AT, COEF_ROWS, l)
        ev[l, HX - COEF_ROWS : HX, :] = low
        ev[l, HX + WX : HX + WX + COEF_ROWS, :] = high
        ev[l, HX : HX + WX, :] = vertical[:, 128 * l : 128 * l + 128]

    low = jnp.where(odd, cb[...], ca[...])
    high = jnp.where(odd, ca[...], cb[...])
    for side, ref in enumerate((from_low, from_high)):
        strip[side, 0:HX, :] = low[8 * side : 8 * side + 8]
        strip[side, HX : HX + WX, :] = ref[...]
        strip[side, HX + WX : 64, :] = high[8 * side : 8 * side + 8]
    pack[0:HX, :] = low[0:8, 256:384]
    pack[HX : HX + WX, :] = colpack[...]
    pack[HX + WX : 64, :] = high[0:8, 256:384]
    for which, dst in enumerate((es, ed)):
        lanes = slice(128 * which, 128 * which + 128)
        for k in range(LV):
            dst[k, NG, 0:64, :] = jnp.where(
                lane64 < 64,
                pltpu.roll(strip[1, :, lanes], (-8 * k) % 128, 1),
                pltpu.roll(strip[0, :, lanes], (120 - 8 * k) % 128, 1),
            )
    ev[NG, 0:64, :] = jnp.where(
        lane64 < 64, strip[1, :, 256:384], pltpu.roll(strip[0, :, 256:384], 120, 1)
    )

    west, east = nx == 0, nx == count_x - 1
    south, north = ny == 0, ny == count_y - 1

    @pl.when(west | east)
    def _():
        lane1 = lax.broadcasted_iota(jnp.int32, (1, 128), 1)
        for l in range(NG + 1):
            got = []
            for item in range(2):
                if l < NG:
                    got.append(interp[item : item + 1, 128 * l : 128 * l + 128])
                else:
                    got.append(
                        jnp.where(
                            lane1 < 64,
                            pltpu.roll(strip[1, HX : HX + 8, 256:384], 112, 1)[item : item + 1],
                            pltpu.roll(strip[0, HX : HX + 8, 256:384], 104, 1)[item : item + 1],
                        )
                    )
            index = jnp.broadcast_to(got[0], (48, 128)).astype(jnp.int32)
            ends = []
            for offset in range(2):
                at = index + offset
                block, inside = at >> 7, at & 127
                total = jnp.zeros((48, 128), jnp.float32)
                for ref, masks in zip(chain_y, plan_y, strict=True):
                    for piece, mask in enumerate(masks):
                        value = jnp.take_along_axis(ref[piece], inside, axis=1, mode="promise_in_bounds")
                        total = jnp.where(block == (ny ^ mask), value, total)
                ends.append(total)
            ey[l] = (1.0 - got[1]) * ends[0] + got[1] * ends[1]

    @pl.when(south | north)
    def _():
        index = pack[:, 64:65].astype(jnp.int32)
        weight = pack[:, 65:66]
        total = jnp.zeros((64, 128), jnp.float32)
        for ref, masks in zip(chain_x, plan_x, strict=True):
            size = 16 * len(masks)
            at = lax.broadcasted_iota(jnp.int32, (1, size), 1)
            ids = at & 15
            for piece, mask in enumerate(masks):
                ids = jnp.where(at >> 4 == piece, ids + 16 * (nx ^ mask), ids)
            spread = jnp.where(ids == index, 1.0 - weight, 0.0) + jnp.where(ids == index + 1, weight, 0.0)
            total += jnp.dot(
                spread,
                ref[...].reshape(size, 128),
                preferred_element_type=jnp.float32,
                precision=lax.Precision.HIGHEST,
            )
        ex[0:64, :] = total

    def ghosts(field, step, row_low, row_high, shift):
        @pl.when(west)
        def _():
            for k in range(LV):
                for l in range(NG + 1):
                    field[k, l, row_low : row_low + 1, :] = ey[l, 16 * step + k : 16 * step + k + 1, :]

        @pl.when(east)
        def _():
            for k in range(LV):
                for l in range(NG + 1):
                    field[k, l, row_high : row_high + 1, :] = ey[l, 16 * step + k : 16 * step + k + 1, :]

        @pl.when(south | north)
        def _():
            at = jnp.where(south, 127, 0)
            lanes = lax.broadcasted_iota(jnp.int32, (56, 128), 1)
            for k in range(LV):
                col = ex[shift : shift + 56, 16 * step + k : 16 * step + k + 1]
                field[k, NG, 0:56, :] = jnp.where(lanes == at, col, field[k, NG, 0:56, :])

    def ghost_tail(step):
        @pl.when(south | north)
        def _():
            at = jnp.where(south, 127, 0)
            for k in range(LV):
                col = ex[56:64, 16 * step + k : 16 * step + k + 1]
                es[k, NG, 56:64, :] = jnp.where(lane == at, col, es[k, NG, 56:64, :])

    for copy in copies:
        copy.wait()
    ghosts(es, 0, HX - 1, HX + WX, 0)
    ghost_tail(0)

    def sideways(c):
        lefts = [pltpu.roll(x, 1, 1) for x in c]
        rights = [pltpu.roll(x, 127, 1) for x in c]
        n = len(c)
        left = [jnp.where(lane == 0, lefts[l - 1], lefts[l]) for l in range(n)]
        right = [jnp.where(lane == 127, rights[(l + 1) % n], rights[l]) for l in range(n)]
        return left, right

    def advance(field, at, coef_at, groups, write_source, read_source, write):
        g = [ev[l, pl.ds(coef_at, 8), :] for l in range(groups)]
        factor, source = [None] * groups, [None] * groups
        for k in range(LV):
            c = [field[k, l, pl.ds(at, 8), :] for l in range(NG + 1)]
            left, right = sideways(c)
            for l in range(groups):
                lap = (
                    field[k, l, pl.ds(at + 1, 8), :]
                    + field[k, l, pl.ds(at - 1, 8), :]
                    + right[l]
                    + left[l]
                    - 4.0 * c[l]
                )
                explicit = c[l] + ed[k, l, pl.ds(coef_at, 8), :] * lap
                diagonal = 1.0 + (g[l] if k in (0, LV - 1) else 2.0 * g[l])
                if k > 0:
                    diagonal = diagonal + g[l] * factor[l]
                    explicit = explicit + g[l] * source[l]
                inverse = 1.0 / diagonal
                factor[l] = -g[l] * inverse
                source[l] = explicit * inverse
                fac[k, l] = factor[l]
                if k < LV - 1:
                    write_source(k, l, source[l])
        value = source
        write(LV - 1, value)
        for k in range(LV - 2, -1, -1):
            value = [read_source(k, l) - fac[k, l] * value[l] for l in range(groups)]
            write(k, value)

    turn = (128 - 3 * dy) % 128

    @pl.loop(0, 7)
    def _(t):
        to = pl.multiple_of(8 * t, 8)

        def put(k, l, x):
            mv[k, l, pl.ds(to, 8), :] = x

        def take(k, l):
            return mv[k, l, pl.ds(to, 8), :]

        def moved(k, values):
            turned = [pltpu.roll(x, turn, 1) for x in values]
            for l in range(NG + 1):
                x = jnp.where(lane >= 128 - 3 * dy, turned[(l + 1) % (NG + 1)], turned[l])
                put(k, l, jnp.where(lane < -3 * dy, turned[l - 1], x))

        at = HX - 2 + 3 * dx + 8 * t
        advance(es, at, at, NG + 1, put, take, moved)

    @pl.when((south & (dy < 0)) | (north & (dy > 0)))
    def _():
        row = lax.broadcasted_iota(jnp.int32, (56, 128), 0)
        cell = (((row + 4) * 21846) >> 16) - 2 + dx
        lanes = lax.broadcasted_iota(jnp.int32, (56, 128), 1)
        total = jnp.zeros((56, 128), jnp.float32)
        for q in range(-2, 18):
            r = q + 8 if q < 0 else (q + HX if q < 8 else q + 40)
            total = jnp.where(cell == q, pack[r : r + 1, :], total)

        for is_side, side, l, first in ((south, 0, 0, 0), (north, 1, NG - 1, 125)):

            @pl.when(is_side)
            def _():
                inside = (lanes >= first) & (lanes < first + 3)
                for k in range(LV):
                    n = 96 + 16 * side + k
                    mv[k, l, 0:56, :] = jnp.where(inside, total[:, n : n + 1], mv[k, l, 0:56, :])

    @pl.when((west & (dx < 0)) | (east & (dx > 0)))
    def _():
        lane16 = lax.broadcasted_iota(jnp.int32, (16, 128), 1)
        for is_side, side, first in ((west, 0, 2), (east, 1, 47)):

            @pl.when(is_side)
            def _():
                own = fill_we[side]
                ring = jnp.where(
                    lane16 < 64,
                    pltpu.roll(strip[1, HX + 16 * side : HX + 16 * side + 16, 256:384], 120, 1),
                    pltpu.roll(strip[0, HX + 16 * side : HX + 16 * side + 16, 256:384], 112, 1),
                )
                for l in range(NG + 1):
                    column = lane16 + 128 * l
                    if l == NG:
                        column = jnp.where(lane16 < 64, column, lane16 - 128)
                    cell = (((column + 384) * 21846) >> 16) - 128 + dy
                    cell = jnp.clip(cell, -128 * ny, 128 * (count_y - ny) - 1)
                    inside = cell & 127
                    a = jnp.take_along_axis(own, inside, axis=1, mode="promise_in_bounds")
                    b = jnp.take_along_axis(ring, inside, axis=1, mode="promise_in_bounds")
                    ey[l, 0:16, :] = jnp.where((cell >= 0) & (cell < 128), a, b)
                    for k in range(LV):
                        mv[k, l, first : first + 3, :] = jnp.broadcast_to(ey[l, k : k + 1, :], (3, 128))

    ghosts(mv, 1, 1, WX + 2, HX - 2)

    @pl.loop(0, 7)
    def _(t):
        to = pl.multiple_of(8 * t, 8)

        def put(k, l, x):
            gv[k, l, pl.ds(to, 8), :] = x

        def take(k, l):
            return gv[k, l, pl.ds(to, 8), :]

        def keep(k, values):
            for l in range(NG + 1):
                put(k, l, values[l])

        advance(mv, 1 + 8 * t, HX - 1 + 8 * t, NG + 1, put, take, keep)

    ghosts(gv, 2, 0, WX + 1, HX - 1)

    @pl.loop(0, 6)
    def _(t):
        to = pl.multiple_of(8 * t, 8)

        def put(k, l, x):
            out[k, pl.ds(to, 8), 128 * l : 128 * l + 128] = x

        def take(k, l):
            return out[k, pl.ds(to, 8), 128 * l : 128 * l + 128]

        def keep(k, values):
            for l in range(NG):
                put(k, l, values[l])

        advance(gv, 1 + 8 * t, HX + 8 * t, NG, put, take, keep)


def on_device(
    state,
    diffuse,
    vertical,
    rows_we,
    rows_sn,
    fill_we,
    fill_sn,
    index_we,
    weight_we,
    index_sn,
    weight_sn,
    jump,
):
    f32 = jnp.float32
    count_x, count_y = lax.axis_size("nx"), lax.axis_size("ny")
    both = ("nx", "ny")
    vmem = pl.BlockSpec(memory_space=pltpu.VMEM)
    smem = pl.BlockSpec(memory_space=pltpu.SMEM)
    hbm = pl.BlockSpec(memory_space=pl.ANY)

    def shape(*dims):
        return jax.ShapeDtypeStruct(dims, f32)

    xa, xb, y_low, y_high, chain_x, chain_y, colpack, interp = pl.pallas_call(
        pack_kernel,
        out_shape=(
            shape(NG, XROWS, 128),
            shape(NG, XROWS, 128),
            shape(WX, WY),
            shape(WX, WY),
            shape(1, 16, 128),
            shape(1, 48, 128),
            shape(WX, 128),
            shape(8, WY),
        ),
        in_specs=[hbm] * 2 + [vmem] * 9,
        out_specs=(vmem,) * 8,
        scratch_shapes=[
            pltpu.VMEM((LV, WX, WY), f32),
            pltpu.VMEM((LV, WX, WY), f32),
            pltpu.VMEM((128, 128), f32),
            pltpu.SemaphoreType.DMA((2,)),
        ],
        compiler_params=pltpu.CompilerParams(vmem_limit_bytes=40 << 20),
        name="pack",
    )(state, diffuse, vertical, rows_we, rows_sn, fill_we, fill_sn, index_we, weight_we, index_sn, weight_sn)

    pairs_a = [(i, i + 1) for i in range(1, count_x - 1, 2)]
    pairs_a += [(b, a) for a, b in pairs_a]
    pairs_b = [(i, i + 1) for i in range(0, count_x, 2)]
    pairs_b += [(b, a) for a, b in pairs_b]
    up = [(i, i + 1) for i in range(count_y - 1)]
    down = [(b, a) for a, b in up]
    rounds_x, rounds_y = rounds_of(count_x), rounds_of(count_y)

    def along_x(chain, masks):
        return [
            lax.ppermute(
                chain,
                both,
                [(i * count_y + n, (i ^ m) * count_y + n) for n in (0, count_y - 1) for i in range(count_x)],
            )
            for m in masks
        ]

    def along_y(chain, masks):
        return [
            lax.ppermute(
                chain,
                both,
                [(n * count_y + j, n * count_y + (j ^ m)) for n in (0, count_x - 1) for j in range(count_y)],
            )
            for m in masks
        ]

    def join(after, parts_x, parts_y, name):
        return pl.pallas_call(
            functools.partial(join_kernel, len(parts_x), len(parts_y)),
            out_shape=(
                shape(sum(p.shape[0] for p in parts_x), 16, 128),
                shape(sum(p.shape[0] for p in parts_y), 48, 128),
            ),
            in_specs=[hbm] + [vmem] * (len(parts_x) + len(parts_y)),
            out_specs=(vmem, vmem),
            name=name,
        )(after, *parts_x, *parts_y)

    parts_x = [chain_x] + along_x(chain_x, rounds_x[0])
    ra = lax.ppermute(xa, "nx", pairs_a)
    parts_y = [chain_y] + along_y(chain_y, rounds_y[0])
    from_low = lax.ppermute(y_high, "ny", up)
    from_high = lax.ppermute(y_low, "ny", down)
    rb = lax.ppermute(xb, "nx", pairs_b)
    ca, cb = pl.pallas_call(
        corner_kernel,
        out_shape=(shape(16, WY), shape(16, WY)),
        in_specs=[vmem] * 3,
        out_specs=(vmem, vmem),
        name="corner",
    )(from_low, from_high, colpack)
    chain_x, chain_y = join(ca, parts_x, parts_y, "join_first")
    parts_x = [chain_x] + along_x(chain_x, rounds_x[1])
    parts_y = [chain_y] + along_y(chain_y, rounds_y[1])
    ra2 = lax.ppermute(ca, "nx", pairs_a)
    rb2 = lax.ppermute(cb, "nx", pairs_b)
    chain_x, chain_y = join(ca, parts_x, parts_y, "join_second")
    parts_x = [chain_x] + along_x(chain_x, rounds_x[2])
    parts_y = [chain_y] + along_y(chain_y, rounds_y[2])
    have_x, have_y = masks_of(rounds_x[:2]), masks_of(rounds_y[:2])
    plan_x = [[m ^ h for h in have_x] for m in [0] + rounds_x[2]]
    plan_y = [[m ^ h for h in have_y] for m in [0] + rounds_y[2]]

    return pl.pallas_call(
        functools.partial(main_kernel, count_x, count_y, plan_x, plan_y),
        out_shape=shape(LV, WX, WY),
        in_specs=[smem, hbm, hbm] + [vmem] * (10 + len(parts_x) + len(parts_y)),
        out_specs=vmem,
        scratch_shapes=[
            pltpu.VMEM((LV, NG + 1, 72, 128), f32),
            pltpu.VMEM((LV, NG + 1, 72, 128), f32),
            pltpu.VMEM((NG + 1, 72, 128), f32),
            pltpu.VMEM((LV, NG + 1, 64, 128), f32),
            pltpu.VMEM((LV, NG + 1, 64, 128), f32),
            pltpu.VMEM((LV, NG + 1, 8, 128), f32),
            pltpu.VMEM((2, 64, WY), f32),
            pltpu.VMEM((NG + 1, 48, 128), f32),
            pltpu.VMEM((64, 128), f32),
            pltpu.VMEM((64, 128), f32),
            pltpu.SemaphoreType.DMA((2 * NG,)),
        ],
        compiler_params=pltpu.CompilerParams(vmem_limit_bytes=48 << 20),
        name="steps",
    )(
        jump, state, diffuse, vertical, ra, rb, from_low, from_high, ra2, rb2,
        colpack, interp, fill_we, *parts_x, *parts_y,
    )


def solution(mesh):
    return jax.shard_map(
        on_device,
        mesh=mesh,
        in_specs=(
            P(None, "nx", "ny"),
            P(None, "nx", "ny"),
            P("nx", "ny"),
            P(None, None, None, "ny"),
            P(None, None, None, "nx"),
            P(None, None, "ny"),
            P(None, None, "nx"),
            P("ny"),
            P("ny"),
            P("nx"),
            P("nx"),
            P(),
        ),
        out_specs=P(None, "nx", "ny"),
        check_vma=False,
    )
```

```python
import functools

import jax
import jax.numpy as jnp
from jax import lax
from jax.experimental import pallas as pl
from jax.experimental.pallas import tpu as pltpu
from jax.sharding import PartitionSpec as P

LV = 16
WX = 48
WY = 384
NG = WY // 128
HX = 8
STATE_ROWS = 6
COEF_ROWS = 5
COEF_AT = LV * STATE_ROWS
VERT_AT = COEF_AT + LV * COEF_ROWS
XROWS = 184
CORNER_AT = NG * XROWS
SENT = CORNER_AT + 16 * NG


def rounds_of(count):
    if count == 32:
        return [[16], [4, 8, 12], [1, 2, 3]]
    if count == 16:
        return [[8], [2, 4, 6], [1]]
    return [[2], [1], []]


def masks_of(rounds):
    have = [0]
    for masks in rounds:
        have = [m ^ h for m in [0] + masks for h in have]
    return have


def pack_kernel(
    state_hbm, diffuse_hbm, vertical_hbm, rows_we_hbm, rows_sn_hbm, fill_we_hbm, fill_sn_hbm,
    index_we_hbm, weight_we_hbm, index_sn_hbm, weight_sn_hbm,
    y_low, y_high, chain_x, chain_y, colpack, interp,
    state, diffuse, vertical, rows_we, rows_sn, fill_we, fill_sn, index_we, weight_we, index_sn, weight_sn,
    square, sem,
):
    nx, ny = lax.axis_index("nx"), lax.axis_index("ny")
    side_x = jnp.where(ny == 0, 0, 1)
    side_y = jnp.where(nx == 0, 0, 1)
    pairs = [
        (rows_we_hbm.at[:, side_y], rows_we),
        (rows_sn_hbm.at[:, side_x], rows_sn),
        (fill_we_hbm, fill_we),
        (fill_sn_hbm, fill_sn),
        (index_we_hbm, index_we),
        (weight_we_hbm, weight_we),
        (index_sn_hbm, index_sn),
        (weight_sn_hbm, weight_sn),
        (vertical_hbm, vertical),
    ]
    for src, dst in ((state_hbm, state), (diffuse_hbm, diffuse)):
        for at, group in enumerate((0, NG - 1)):
            pairs.append((src.at[:, :, pl.ds(128 * group, 128)], dst.at[at]))
    copies = [pltpu.make_async_copy(src, dst, sem.at[n]) for n, (src, dst) in enumerate(pairs)]
    for copy in copies:
        copy.start()
    lane = lax.broadcasted_iota(jnp.int32, (128, 128), 1)
    square[...] = jnp.zeros((128, 128), jnp.float32)
    interp[...] = jnp.zeros((8, WY), jnp.float32)
    for copy in copies[:8]:
        copy.wait()
    for step in range(3):
        chain_y[0, 16 * step : 16 * step + 16, :] = rows_we[step]
        square[16 * step : 16 * step + 16, 0:16] = rows_sn[step]
    chain_x[0] = square[...].T[0:16]
    square[0:48, :] = jnp.zeros((48, 128), jnp.float32)
    square[96:112, 0:16] = fill_sn[0]
    square[112:128, 0:16] = fill_sn[1]
    square[64:65, 0:WX] = index_sn[...].astype(jnp.float32).reshape(1, WX)
    square[65:66, 0:WX] = weight_sn[...].reshape(1, WX)
    whole = square[...]
    row = lax.broadcasted_iota(jnp.int32, (128, 128), 0)
    whole = jnp.where((lane < 8) | (row < 96), whole, pltpu.roll(whole, 32, 1))
    colpack[...] = whole.T[0:WX]
    interp[0:1, :] = index_we[...].astype(jnp.float32).reshape(1, WY)
    interp[1:2, :] = weight_we[...].reshape(1, WY)
    square[0:16, :] = fill_we[0]
    square[16:32, :] = fill_we[1]
    for copy in copies[8:]:
        copy.wait()

    lane = lax.broadcasted_iota(jnp.int32, (WX, 128), 1)
    row = lax.broadcasted_iota(jnp.int32, (WX, 128), 0)
    for at, (ref, group, first) in enumerate(((y_low, 0, 0), (y_high, NG - 1, 120))):
        lanes = slice(128 * group, 128 * group + 128)
        for which, field in enumerate((state, diffuse)):
            total = jnp.zeros((WX, 128), jnp.float32)
            for k in range(LV):
                part = pltpu.roll(field[at, k], (8 * k - first) % 128, 1)
                total = jnp.where((lane >= 8 * k) & (lane < 8 * k + 8), part, total)
            ref[:, 128 * which : 128 * which + 128] = total
        last = jnp.where(lane < 8, pltpu.roll(vertical[:, lanes], (-first) % 128, 1), 0.0)
        last = jnp.where(
            (lane >= 8) & (lane < 16), pltpu.roll(square[0:WX, :], (8 - first) % 128, 1), last
        )
        pair = jnp.where(row == 0, interp[0:1, lanes], interp[1:2, lanes])
        last = jnp.where(
            (lane >= 16) & (lane < 24) & (row < 2), pltpu.roll(pair, (16 - first) % 128, 1), last
        )
        ref[:, 256:384] = last


def border_kernel(
    state_hbm, diffuse_hbm, vertical_hbm, from_low, from_high, colpack, xa, xb, state, diffuse, vertical, sem
):
    copies = [pltpu.make_async_copy(vertical_hbm, vertical, sem.at[4])]
    for n, (src, dst) in enumerate(((state_hbm, state), (diffuse_hbm, diffuse))):
        for side in range(2):
            copies.append(
                pltpu.make_async_copy(src.at[:, pl.ds(40 * side, 8), :], dst.at[side], sem.at[2 * n + side])
            )
    for copy in copies:
        copy.start()
    odd = lax.axis_index("nx") % 2 == 1
    clear = lax.broadcasted_iota(jnp.int32, (8, 128), 1) < 64
    for copy in copies:
        copy.wait()

    def rows(ref, side):
        at = 8 - STATE_ROWS if side else 0
        bt = 8 - COEF_ROWS if side else 0
        for l in range(NG):
            lanes = slice(128 * l, 128 * l + 128)
            base = XROWS * l
            for k in range(LV):
                n = base + k * STATE_ROWS
                ref[n : n + STATE_ROWS, :] = state[side, k, at : at + STATE_ROWS, lanes]
                n = base + COEF_AT + k * COEF_ROWS
                ref[n : n + COEF_ROWS, :] = diffuse[side, k, bt : bt + COEF_ROWS, lanes]
            n = base + VERT_AT
            ref[n : n + COEF_ROWS, :] = vertical[40 * side + bt : 40 * side + bt + COEF_ROWS, lanes]
            ref[n + COEF_ROWS : base + XROWS, :] = jnp.zeros((XROWS - VERT_AT - COEF_ROWS, 128), jnp.float32)
        for which, strips in enumerate((from_low, from_high)):
            for l in range(NG):
                part = strips[40 * side : 40 * side + 8, 128 * l : 128 * l + 128]
                if which == 0 and l == NG - 1:
                    part = jnp.where(clear, part, colpack[40 * side : 40 * side + 8, :])
                n = CORNER_AT + 8 * (NG * which + l)
                ref[n : n + 8, :] = part

    @pl.when(odd)
    def _():
        rows(xa, 1)
        rows(xb, 0)

    @pl.when(jnp.logical_not(odd))
    def _():
        rows(xa, 0)
        rows(xb, 1)


def join_kernel(count_x, count_y, after, *refs):
    ins, (out_x, out_y) = refs[:-2], refs[-2:]
    for out, parts in ((out_x, ins[:count_x]), (out_y, ins[count_x : count_x + count_y])):
        at = 0
        for part in parts:
            out[at : at + part.shape[0]] = part[...]
            at += part.shape[0]


def main_kernel(
    count_x, count_y, plan_x, plan_y, jump, state, diffuse, vertical_hbm, fill_we_hbm, ra, rb, from_low, from_high,
    colpack, interp, *refs,
):
    chain_x, refs = refs[: len(plan_x)], refs[len(plan_x) :]
    chain_y, refs = refs[: len(plan_y)], refs[len(plan_y) :]
    out, es, ed, ev, mv, gv, fac, strip, ey, ex, pack, vertical, fill_we, sem = refs
    dx, dy = jump[0], jump[1]
    nx, ny = lax.axis_index("nx"), lax.axis_index("ny")
    copies = []
    for which, (src, dst) in enumerate(((state, es), (diffuse, ed))):
        for l in range(NG):
            copy = pltpu.make_async_copy(
                src.at[:, :, pl.ds(128 * l, 128)], dst.at[:, l, pl.ds(HX, WX), :], sem.at[NG * which + l]
            )
            copy.start()
            copies.append(copy)
    first_copies = [
        pltpu.make_async_copy(vertical_hbm, vertical, sem.at[2 * NG]),
        pltpu.make_async_copy(fill_we_hbm, fill_we, sem.at[2 * NG + 1]),
    ]
    for copy in first_copies:
        copy.start()
    odd = nx % 2 == 1
    lane = lax.broadcasted_iota(jnp.int32, (8, 128), 1)
    lane64 = lax.broadcasted_iota(jnp.int32, (64, 128), 1)

    def beyond(at, size, l):
        a, b = ra[XROWS * l + at : XROWS * l + at + size, :], rb[XROWS * l + at : XROWS * l + at + size, :]
        return jnp.where(odd, b, a), jnp.where(odd, a, b)

    for copy in first_copies:
        copy.wait()
    for l in range(NG):
        for k in range(LV):
            low, high = beyond(k * STATE_ROWS, STATE_ROWS, l)
            es[k, l, HX - STATE_ROWS : HX, :] = low
            es[k, l, HX + WX : HX + WX + STATE_ROWS, :] = high
            low, high = beyond(COEF_AT + k * COEF_ROWS, COEF_ROWS, l)
            ed[k, l, HX - COEF_ROWS : HX, :] = low
            ed[k, l, HX + WX : HX + WX + COEF_ROWS, :] = high
        low, high = beyond(VERT_AT, COEF_ROWS, l)
        ev[l, HX - COEF_ROWS : HX, :] = low
        ev[l, HX + WX : HX + WX + COEF_ROWS, :] = high
        ev[l, HX : HX + WX, :] = vertical[:, 128 * l : 128 * l + 128]

    def corner(side, l):
        n = CORNER_AT + 8 * (NG * side + l)
        a, b = ra[n : n + 8, :], rb[n : n + 8, :]
        return jnp.where(odd, b, a), jnp.where(odd, a, b)

    for side, ref in enumerate((from_low, from_high)):
        strip[side, HX : HX + WX, :] = ref[...]
        for l in range(NG):
            low, high = corner(side, l)
            strip[side, 0:HX, 128 * l : 128 * l + 128] = low
            strip[side, HX + WX : 64, 128 * l : 128 * l + 128] = high
    low, high = corner(0, NG - 1)
    pack[0:HX, :] = low
    pack[HX : HX + WX, :] = colpack[...]
    pack[HX + WX : 64, :] = high
    for which, dst in enumerate((es, ed)):
        lanes = slice(128 * which, 128 * which + 128)
        for k in range(LV):
            dst[k, NG, 0:64, :] = jnp.where(
                lane64 < 64,
                pltpu.roll(strip[1, :, lanes], (-8 * k) % 128, 1),
                pltpu.roll(strip[0, :, lanes], (120 - 8 * k) % 128, 1),
            )
    ev[NG, 0:64, :] = jnp.where(
        lane64 < 64, strip[1, :, 256:384], pltpu.roll(strip[0, :, 256:384], 120, 1)
    )

    west, east = nx == 0, nx == count_x - 1
    south, north = ny == 0, ny == count_y - 1

    @pl.when(west | east)
    def _():
        lane1 = lax.broadcasted_iota(jnp.int32, (1, 128), 1)
        for l in range(NG + 1):
            got = []
            for item in range(2):
                if l < NG:
                    got.append(interp[item : item + 1, 128 * l : 128 * l + 128])
                else:
                    got.append(
                        jnp.where(
                            lane1 < 64,
                            pltpu.roll(strip[1, HX : HX + 8, 256:384], 112, 1)[item : item + 1],
                            pltpu.roll(strip[0, HX : HX + 8, 256:384], 104, 1)[item : item + 1],
                        )
                    )
            index = jnp.broadcast_to(got[0], (48, 128)).astype(jnp.int32)
            ends = []
            for offset in range(2):
                at = index + offset
                block, inside = at >> 7, at & 127
                total = jnp.zeros((48, 128), jnp.float32)
                for ref, masks in zip(chain_y, plan_y, strict=True):
                    for piece, mask in enumerate(masks):
                        value = jnp.take_along_axis(ref[piece], inside, axis=1, mode="promise_in_bounds")
                        total = jnp.where(block == (ny ^ mask), value, total)
                ends.append(total)
            ey[l] = (1.0 - got[1]) * ends[0] + got[1] * ends[1]

    @pl.when(south | north)
    def _():
        index = pack[:, 64:65].astype(jnp.int32)
        weight = pack[:, 65:66]
        total = jnp.zeros((64, 128), jnp.float32)
        for ref, masks in zip(chain_x, plan_x, strict=True):
            size = 16 * len(masks)
            at = lax.broadcasted_iota(jnp.int32, (1, size), 1)
            ids = at & 15
            for piece, mask in enumerate(masks):
                ids = jnp.where(at >> 4 == piece, ids + 16 * (nx ^ mask), ids)
            spread = jnp.where(ids == index, 1.0 - weight, 0.0) + jnp.where(ids == index + 1, weight, 0.0)
            total += jnp.dot(
                spread,
                ref[...].reshape(size, 128),
                preferred_element_type=jnp.float32,
                precision=lax.Precision.HIGHEST,
            )
        ex[0:64, :] = total

    def ghosts(field, step, row_low, row_high, shift):
        @pl.when(west)
        def _():
            for k in range(LV):
                for l in range(NG + 1):
                    field[k, l, row_low : row_low + 1, :] = ey[l, 16 * step + k : 16 * step + k + 1, :]

        @pl.when(east)
        def _():
            for k in range(LV):
                for l in range(NG + 1):
                    field[k, l, row_high : row_high + 1, :] = ey[l, 16 * step + k : 16 * step + k + 1, :]

        @pl.when(south | north)
        def _():
            at = jnp.where(south, 127, 0)
            lanes = lax.broadcasted_iota(jnp.int32, (56, 128), 1)
            for k in range(LV):
                col = ex[shift : shift + 56, 16 * step + k : 16 * step + k + 1]
                field[k, NG, 0:56, :] = jnp.where(lanes == at, col, field[k, NG, 0:56, :])

    def ghost_tail(step):
        @pl.when(south | north)
        def _():
            at = jnp.where(south, 127, 0)
            for k in range(LV):
                col = ex[56:64, 16 * step + k : 16 * step + k + 1]
                es[k, NG, 56:64, :] = jnp.where(lane == at, col, es[k, NG, 56:64, :])

    for copy in copies:
        copy.wait()
    ghosts(es, 0, HX - 1, HX + WX, 0)
    ghost_tail(0)

    def sideways(c):
        lefts = [pltpu.roll(x, 1, 1) for x in c]
        rights = [pltpu.roll(x, 127, 1) for x in c]
        n = len(c)
        left = [jnp.where(lane == 0, lefts[l - 1], lefts[l]) for l in range(n)]
        right = [jnp.where(lane == 127, rights[(l + 1) % n], rights[l]) for l in range(n)]
        return left, right

    def advance(field, at, coef_at, groups, write_source, read_source, write):
        g = [ev[l, pl.ds(coef_at, 8), :] for l in range(groups)]
        factor, source = [None] * groups, [None] * groups
        for k in range(LV):
            c = [field[k, l, pl.ds(at, 8), :] for l in range(NG + 1)]
            left, right = sideways(c)
            for l in range(groups):
                lap = (
                    field[k, l, pl.ds(at + 1, 8), :]
                    + field[k, l, pl.ds(at - 1, 8), :]
                    + right[l]
                    + left[l]
                    - 4.0 * c[l]
                )
                explicit = c[l] + ed[k, l, pl.ds(coef_at, 8), :] * lap
                diagonal = 1.0 + (g[l] if k in (0, LV - 1) else 2.0 * g[l])
                if k > 0:
                    diagonal = diagonal + g[l] * factor[l]
                    explicit = explicit + g[l] * source[l]
                inverse = 1.0 / diagonal
                factor[l] = -g[l] * inverse
                source[l] = explicit * inverse
                fac[k, l] = factor[l]
                if k < LV - 1:
                    write_source(k, l, source[l])
        value = source
        write(LV - 1, value)
        for k in range(LV - 2, -1, -1):
            value = [read_source(k, l) - fac[k, l] * value[l] for l in range(groups)]
            write(k, value)

    turn = (128 - 3 * dy) % 128

    @pl.loop(0, 7)
    def _(t):
        to = pl.multiple_of(8 * t, 8)

        def put(k, l, x):
            mv[k, l, pl.ds(to, 8), :] = x

        def take(k, l):
            return mv[k, l, pl.ds(to, 8), :]

        def moved(k, values):
            turned = [pltpu.roll(x, turn, 1) for x in values]
            for l in range(NG + 1):
                x = jnp.where(lane >= 128 - 3 * dy, turned[(l + 1) % (NG + 1)], turned[l])
                put(k, l, jnp.where(lane < -3 * dy, turned[l - 1], x))

        at = HX - 2 + 3 * dx + 8 * t
        advance(es, at, at, NG + 1, put, take, moved)

    @pl.when((south & (dy < 0)) | (north & (dy > 0)))
    def _():
        row = lax.broadcasted_iota(jnp.int32, (56, 128), 0)
        cell = (((row + 4) * 21846) >> 16) - 2 + dx
        lanes = lax.broadcasted_iota(jnp.int32, (56, 128), 1)
        total = jnp.zeros((56, 128), jnp.float32)
        for q in range(-2, 18):
            r = q + 8 if q < 0 else (q + HX if q < 8 else q + 40)
            total = jnp.where(cell == q, pack[r : r + 1, :], total)

        for is_side, side, l, first in ((south, 0, 0, 0), (north, 1, NG - 1, 125)):

            @pl.when(is_side)
            def _():
                inside = (lanes >= first) & (lanes < first + 3)
                for k in range(LV):
                    n = 96 + 16 * side + k
                    mv[k, l, 0:56, :] = jnp.where(inside, total[:, n : n + 1], mv[k, l, 0:56, :])

    @pl.when((west & (dx < 0)) | (east & (dx > 0)))
    def _():
        lane16 = lax.broadcasted_iota(jnp.int32, (16, 128), 1)
        for is_side, side, first in ((west, 0, 2), (east, 1, 47)):

            @pl.when(is_side)
            def _():
                own = fill_we[side]
                ring = jnp.where(
                    lane16 < 64,
                    pltpu.roll(strip[1, HX + 16 * side : HX + 16 * side + 16, 256:384], 120, 1),
                    pltpu.roll(strip[0, HX + 16 * side : HX + 16 * side + 16, 256:384], 112, 1),
                )
                for l in range(NG + 1):
                    column = lane16 + 128 * l
                    if l == NG:
                        column = jnp.where(lane16 < 64, column, lane16 - 128)
                    cell = (((column + 384) * 21846) >> 16) - 128 + dy
                    cell = jnp.clip(cell, -128 * ny, 128 * (count_y - ny) - 1)
                    inside = cell & 127
                    a = jnp.take_along_axis(own, inside, axis=1, mode="promise_in_bounds")
                    b = jnp.take_along_axis(ring, inside, axis=1, mode="promise_in_bounds")
                    ey[l, 0:16, :] = jnp.where((cell >= 0) & (cell < 128), a, b)
                    for k in range(LV):
                        mv[k, l, first : first + 3, :] = jnp.broadcast_to(ey[l, k : k + 1, :], (3, 128))

    ghosts(mv, 1, 1, WX + 2, HX - 2)

    @pl.loop(0, 7)
    def _(t):
        to = pl.multiple_of(8 * t, 8)

        def put(k, l, x):
            gv[k, l, pl.ds(to, 8), :] = x

        def take(k, l):
            return gv[k, l, pl.ds(to, 8), :]

        def keep(k, values):
            for l in range(NG + 1):
                put(k, l, values[l])

        advance(mv, 1 + 8 * t, HX - 1 + 8 * t, NG + 1, put, take, keep)

    ghosts(gv, 2, 0, WX + 1, HX - 1)

    @pl.loop(0, 6)
    def _(t):
        to = pl.multiple_of(8 * t, 8)

        def put(k, l, x):
            out[k, pl.ds(to, 8), 128 * l : 128 * l + 128] = x

        def take(k, l):
            return out[k, pl.ds(to, 8), 128 * l : 128 * l + 128]

        def keep(k, values):
            for l in range(NG):
                put(k, l, values[l])

        advance(gv, 1 + 8 * t, HX + 8 * t, NG, put, take, keep)


def on_device(
    state,
    diffuse,
    vertical,
    rows_we,
    rows_sn,
    fill_we,
    fill_sn,
    index_we,
    weight_we,
    index_sn,
    weight_sn,
    jump,
):
    f32 = jnp.float32
    count_x, count_y = lax.axis_size("nx"), lax.axis_size("ny")
    both = ("nx", "ny")
    vmem = pl.BlockSpec(memory_space=pltpu.VMEM)
    smem = pl.BlockSpec(memory_space=pltpu.SMEM)
    hbm = pl.BlockSpec(memory_space=pltpu.HBM)
    any_ = pl.BlockSpec(memory_space=pl.ANY)

    def shape(*dims):
        return jax.ShapeDtypeStruct(dims, f32)

    y_low, y_high, chain_x, chain_y, colpack, interp = pl.pallas_call(
        pack_kernel,
        out_shape=(
            shape(WX, WY),
            shape(WX, WY),
            shape(1, 16, 128),
            shape(1, 48, 128),
            shape(WX, 128),
            shape(8, WY),
        ),
        in_specs=[hbm] * 11,
        out_specs=(vmem,) * 6,
        scratch_shapes=[
            pltpu.VMEM((2, LV, WX, 128), f32),
            pltpu.VMEM((2, LV, WX, 128), f32),
            pltpu.VMEM((WX, WY), f32),
            pltpu.VMEM((3, 16, 128), f32),
            pltpu.VMEM((3, 16, 16), f32),
            pltpu.VMEM((2, 16, 128), f32),
            pltpu.VMEM((2, 16, 16), f32),
            pltpu.VMEM((WY,), jnp.int32),
            pltpu.VMEM((WY,), f32),
            pltpu.VMEM((WX,), jnp.int32),
            pltpu.VMEM((WX,), f32),
            pltpu.VMEM((128, 128), f32),
            pltpu.SemaphoreType.DMA((13,)),
        ],
        compiler_params=pltpu.CompilerParams(vmem_limit_bytes=40 << 20),
        name="pack",
    )(state, diffuse, vertical, rows_we, rows_sn, fill_we, fill_sn, index_we, weight_we, index_sn, weight_sn)

    pairs_a = [(i, i + 1) for i in range(1, count_x - 1, 2)]
    pairs_a += [(b, a) for a, b in pairs_a]
    pairs_b = [(i, i + 1) for i in range(0, count_x, 2)]
    pairs_b += [(b, a) for a, b in pairs_b]
    up = [(i, i + 1) for i in range(count_y - 1)]
    down = [(b, a) for a, b in up]
    rounds_x, rounds_y = rounds_of(count_x), rounds_of(count_y)

    def along_x(chain, masks):
        return [
            lax.ppermute(
                chain,
                both,
                [(i * count_y + n, (i ^ m) * count_y + n) for n in (0, count_y - 1) for i in range(count_x)],
            )
            for m in masks
        ]

    def along_y(chain, masks):
        return [
            lax.ppermute(
                chain,
                both,
                [(n * count_y + j, n * count_y + (j ^ m)) for n in (0, count_x - 1) for j in range(count_y)],
            )
            for m in masks
        ]

    def join(after, parts_x, parts_y, name):
        return pl.pallas_call(
            functools.partial(join_kernel, len(parts_x), len(parts_y)),
            out_shape=(
                shape(sum(p.shape[0] for p in parts_x), 16, 128),
                shape(sum(p.shape[0] for p in parts_y), 48, 128),
            ),
            in_specs=[any_] + [vmem] * (len(parts_x) + len(parts_y)),
            out_specs=(vmem, vmem),
            name=name,
        )(after, *parts_x, *parts_y)

    parts_x = [chain_x] + along_x(chain_x, rounds_x[0])
    parts_y = [chain_y] + along_y(chain_y, rounds_y[0])
    from_low = lax.ppermute(y_high, "ny", up)
    from_high = lax.ppermute(y_low, "ny", down)
    xa, xb = pl.pallas_call(
        border_kernel,
        out_shape=(shape(SENT, 128), shape(SENT, 128)),
        in_specs=[hbm] * 3 + [vmem] * 3,
        out_specs=(vmem, vmem),
        scratch_shapes=[
            pltpu.VMEM((2, LV, 8, WY), f32),
            pltpu.VMEM((2, LV, 8, WY), f32),
            pltpu.VMEM((WX, WY), f32),
            pltpu.SemaphoreType.DMA((5,)),
        ],
        name="border",
    )(state, diffuse, vertical, from_low, from_high, colpack)
    ra = lax.ppermute(xa, "nx", pairs_a)
    rb = lax.ppermute(xb, "nx", pairs_b)
    chain_x, chain_y = join(xa, parts_x, parts_y, "join_first")
    parts_x = [chain_x] + along_x(chain_x, rounds_x[1])
    parts_y = [chain_y] + along_y(chain_y, rounds_y[1])
    chain_x, chain_y = join(xa, parts_x, parts_y, "join_second")
    parts_x = [chain_x] + along_x(chain_x, rounds_x[2])
    parts_y = [chain_y] + along_y(chain_y, rounds_y[2])
    have_x, have_y = masks_of(rounds_x[:2]), masks_of(rounds_y[:2])
    plan_x = [[m ^ h for h in have_x] for m in [0] + rounds_x[2]]
    plan_y = [[m ^ h for h in have_y] for m in [0] + rounds_y[2]]

    return pl.pallas_call(
        functools.partial(main_kernel, count_x, count_y, plan_x, plan_y),
        out_shape=shape(LV, WX, WY),
        in_specs=[smem] + [hbm] * 4 + [vmem] * (6 + len(parts_x) + len(parts_y)),
        out_specs=vmem,
        scratch_shapes=[
            pltpu.VMEM((LV, NG + 1, 72, 128), f32),
            pltpu.VMEM((LV, NG + 1, 72, 128), f32),
            pltpu.VMEM((NG + 1, 72, 128), f32),
            pltpu.VMEM((LV, NG + 1, 64, 128), f32),
            pltpu.VMEM((LV, NG + 1, 64, 128), f32),
            pltpu.VMEM((LV, NG + 1, 8, 128), f32),
            pltpu.VMEM((2, 64, WY), f32),
            pltpu.VMEM((NG + 1, 48, 128), f32),
            pltpu.VMEM((64, 128), f32),
            pltpu.VMEM((64, 128), f32),
            pltpu.VMEM((WX, WY), f32),
            pltpu.VMEM((2, 16, 128), f32),
            pltpu.SemaphoreType.DMA((2 * NG + 2,)),
        ],
        compiler_params=pltpu.CompilerParams(vmem_limit_bytes=48 << 20),
        name="steps",
    )(
        jump, state, diffuse, vertical, fill_we, ra, rb, from_low, from_high,
        colpack, interp, *parts_x, *parts_y,
    )


def solution(mesh):
    return jax.shard_map(
        on_device,
        mesh=mesh,
        in_specs=(
            P(None, "nx", "ny"),
            P(None, "nx", "ny"),
            P("nx", "ny"),
            P(None, None, None, "ny"),
            P(None, None, None, "nx"),
            P(None, None, "ny"),
            P(None, None, "nx"),
            P("ny"),
            P("ny"),
            P("nx"),
            P("nx"),
            P(),
        ),
        out_specs=P(None, "nx", "ny"),
        check_vma=False,
    )
```

```python
import functools

import jax
import jax.numpy as jnp
from jax import lax
from jax.experimental import pallas as pl
from jax.experimental.pallas import tpu as pltpu
from jax.sharding import PartitionSpec as P

LV = 16
WX = 48
WY = 384
NG = WY // 128
HX = 8
STATE_ROWS = 6
COEF_ROWS = 5
COEF_AT = LV * STATE_ROWS
VERT_AT = COEF_AT + LV * COEF_ROWS
XROWS = 184
CORNER_AT = NG * XROWS
SENT = CORNER_AT + 16 * NG


def rounds_of(count):
    if count == 32:
        return [[16], [4, 8, 12], [1, 2, 3]]
    if count == 16:
        return [[8], [2, 4, 6], [1]]
    return [[2], [1], []]


def masks_of(rounds):
    have = [0]
    for masks in rounds:
        have = [m ^ h for m in [0] + masks for h in have]
    return have


def pack_kernel(
    state_hbm, diffuse_hbm, vertical_hbm, rows_we_hbm, rows_sn_hbm, fill_we_hbm, fill_sn_hbm,
    index_we_hbm, weight_we_hbm, index_sn_hbm, weight_sn_hbm,
    y_low, y_high, chain_x, chain_y, colpack, interp,
    state, diffuse, vertical, rows_we, rows_sn, fill_we, fill_sn, index_we, weight_we, index_sn, weight_sn,
    square, sem,
):
    nx, ny = lax.axis_index("nx"), lax.axis_index("ny")
    side_x = jnp.where(ny < lax.axis_size("ny") // 2, 0, 1)
    side_y = jnp.where(nx < lax.axis_size("nx") // 2, 0, 1)
    pairs = [
        (rows_we_hbm.at[:, side_y], rows_we),
        (rows_sn_hbm.at[:, side_x], rows_sn),
        (fill_we_hbm, fill_we),
        (fill_sn_hbm, fill_sn),
        (index_we_hbm, index_we),
        (weight_we_hbm, weight_we),
        (index_sn_hbm, index_sn),
        (weight_sn_hbm, weight_sn),
        (vertical_hbm, vertical),
    ]
    for src, dst in ((state_hbm, state), (diffuse_hbm, diffuse)):
        for at, group in enumerate((0, NG - 1)):
            pairs.append((src.at[:, :, pl.ds(128 * group, 128)], dst.at[at]))
    copies = [pltpu.make_async_copy(src, dst, sem.at[n]) for n, (src, dst) in enumerate(pairs)]
    for copy in copies:
        copy.start()
    lane = lax.broadcasted_iota(jnp.int32, (128, 128), 1)
    square[...] = jnp.zeros((128, 128), jnp.float32)
    interp[...] = jnp.zeros((8, WY), jnp.float32)
    for copy in copies[:8]:
        copy.wait()
    for step in range(3):
        chain_y[0, 16 * step : 16 * step + 16, :] = rows_we[step]
        square[16 * step : 16 * step + 16, 0:16] = rows_sn[step]
    chain_x[0] = square[...].T[0:16]
    square[0:48, :] = jnp.zeros((48, 128), jnp.float32)
    square[96:112, 0:16] = fill_sn[0]
    square[112:128, 0:16] = fill_sn[1]
    square[64:65, 0:WX] = index_sn[...].astype(jnp.float32).reshape(1, WX)
    square[65:66, 0:WX] = weight_sn[...].reshape(1, WX)
    whole = square[...]
    row = lax.broadcasted_iota(jnp.int32, (128, 128), 0)
    whole = jnp.where((lane < 8) | (row < 96), whole, pltpu.roll(whole, 32, 1))
    colpack[...] = whole.T[0:WX]
    interp[0:1, :] = index_we[...].astype(jnp.float32).reshape(1, WY)
    interp[1:2, :] = weight_we[...].reshape(1, WY)
    square[0:16, :] = fill_we[0]
    square[16:32, :] = fill_we[1]
    for copy in copies[8:]:
        copy.wait()

    lane = lax.broadcasted_iota(jnp.int32, (WX, 128), 1)
    row = lax.broadcasted_iota(jnp.int32, (WX, 128), 0)
    for at, (ref, group, first) in enumerate(((y_low, 0, 0), (y_high, NG - 1, 120))):
        lanes = slice(128 * group, 128 * group + 128)
        for which, field in enumerate((state, diffuse)):
            total = jnp.zeros((WX, 128), jnp.float32)
            for k in range(LV):
                part = pltpu.roll(field[at, k], (8 * k - first) % 128, 1)
                total = jnp.where((lane >= 8 * k) & (lane < 8 * k + 8), part, total)
            ref[:, 128 * which : 128 * which + 128] = total
        last = jnp.where(lane < 8, pltpu.roll(vertical[:, lanes], (-first) % 128, 1), 0.0)
        last = jnp.where(
            (lane >= 8) & (lane < 16), pltpu.roll(square[0:WX, :], (8 - first) % 128, 1), last
        )
        pair = jnp.where(row == 0, interp[0:1, lanes], interp[1:2, lanes])
        last = jnp.where(
            (lane >= 16) & (lane < 24) & (row < 2), pltpu.roll(pair, (16 - first) % 128, 1), last
        )
        ref[:, 256:384] = last


def border_kernel(
    after_x, after_y, state_hbm, diffuse_hbm, vertical_hbm, from_low, from_high, colpack,
    xa, xb, state, diffuse, vertical, sem,
):
    copies = [pltpu.make_async_copy(vertical_hbm, vertical, sem.at[4])]
    for n, (src, dst) in enumerate(((state_hbm, state), (diffuse_hbm, diffuse))):
        for side in range(2):
            copies.append(
                pltpu.make_async_copy(src.at[:, pl.ds(40 * side, 8), :], dst.at[side], sem.at[2 * n + side])
            )
    for copy in copies:
        copy.start()
    odd = lax.axis_index("nx") % 2 == 1
    clear = lax.broadcasted_iota(jnp.int32, (8, 128), 1) < 64
    for copy in copies:
        copy.wait()

    def rows(ref, side):
        at = 8 - STATE_ROWS if side else 0
        bt = 8 - COEF_ROWS if side else 0
        for l in range(NG):
            lanes = slice(128 * l, 128 * l + 128)
            base = XROWS * l
            for k in range(LV):
                n = base + k * STATE_ROWS
                ref[n : n + STATE_ROWS, :] = state[side, k, at : at + STATE_ROWS, lanes]
                n = base + COEF_AT + k * COEF_ROWS
                ref[n : n + COEF_ROWS, :] = diffuse[side, k, bt : bt + COEF_ROWS, lanes]
            n = base + VERT_AT
            ref[n : n + COEF_ROWS, :] = vertical[40 * side + bt : 40 * side + bt + COEF_ROWS, lanes]
            ref[n + COEF_ROWS : base + XROWS, :] = jnp.zeros((XROWS - VERT_AT - COEF_ROWS, 128), jnp.float32)
        for which, strips in enumerate((from_low, from_high)):
            for l in range(NG):
                part = strips[40 * side : 40 * side + 8, 128 * l : 128 * l + 128]
                if which == 0 and l == NG - 1:
                    part = jnp.where(clear, part, colpack[40 * side : 40 * side + 8, :])
                n = CORNER_AT + 8 * (NG * which + l)
                ref[n : n + 8, :] = part

    @pl.when(odd)
    def _():
        rows(xa, 1)
        rows(xb, 0)

    @pl.when(jnp.logical_not(odd))
    def _():
        rows(xa, 0)
        rows(xb, 1)


def join_kernel(count_x, count_y, *refs):
    ins, (out_x, out_y) = refs[:-2], refs[-2:]
    for out, parts in ((out_x, ins[:count_x]), (out_y, ins[count_x : count_x + count_y])):
        at = 0
        for part in parts:
            out[at : at + part.shape[0]] = part[...]
            at += part.shape[0]


def edge_kernel(count_x, count_y, plan_x, plan_y, ra, rb, from_low, from_high, colpack, interp, *refs):
    chain_x, refs = refs[: len(plan_x)], refs[len(plan_x) :]
    chain_y, refs = refs[: len(plan_y)], refs[len(plan_y) :]
    edges, pack = refs
    nx, ny = lax.axis_index("nx"), lax.axis_index("ny")
    odd = nx % 2 == 1
    border_x = (nx == 0) | (nx == count_x - 1)
    border_y = (ny == 0) | (ny == count_y - 1)
    inner_x = (nx == 1) | (nx == count_x - 2)
    inner_y = (ny == 1) | (ny == count_y - 2)

    @pl.when((border_x & jnp.logical_not(inner_y)) | (inner_x & inner_y))
    def _():
        lane1 = lax.broadcasted_iota(jnp.int32, (1, 128), 1)
        for l in range(NG + 1):
            got = []
            for item in range(2):
                if l < NG:
                    got.append(interp[item : item + 1, 128 * l : 128 * l + 128])
                else:
                    got.append(
                        jnp.where(
                            lane1 < 64,
                            pltpu.roll(from_high[0:8, 256:384], 112, 1)[item : item + 1],
                            pltpu.roll(from_low[0:8, 256:384], 104, 1)[item : item + 1],
                        )
                    )
            index = jnp.broadcast_to(got[0], (48, 128)).astype(jnp.int32)
            ends = []
            for offset in range(2):
                at = index + offset
                block, inside = at >> 7, at & 127
                total = jnp.zeros((48, 128), jnp.float32)
                for ref, masks in zip(chain_y, plan_y, strict=True):
                    for piece, mask in enumerate(masks):
                        value = jnp.take_along_axis(ref[piece], inside, axis=1, mode="promise_in_bounds")
                        total = jnp.where(block == (ny ^ mask), value, total)
                ends.append(total)
            edges[64 + 48 * l : 112 + 48 * l, :] = (1.0 - got[1]) * ends[0] + got[1] * ends[1]

    @pl.when((border_y & jnp.logical_not(border_x)) | (border_x & inner_y))
    def _():
        n = CORNER_AT + 8 * (NG - 1)
        a, b = ra[n : n + 8, :], rb[n : n + 8, :]
        pack[0:HX, :] = jnp.where(odd, b, a)
        pack[HX : HX + WX, :] = colpack[...]
        pack[HX + WX : 64, :] = jnp.where(odd, a, b)
        index = pack[:, 64:65].astype(jnp.int32)
        weight = pack[:, 65:66]
        total = jnp.zeros((64, 128), jnp.float32)
        for ref, masks in zip(chain_x, plan_x, strict=True):
            size = 16 * len(masks)
            at = lax.broadcasted_iota(jnp.int32, (1, size), 1)
            ids = at & 15
            for piece, mask in enumerate(masks):
                ids = jnp.where(at >> 4 == piece, ids + 16 * (nx ^ mask), ids)
            spread = jnp.where(ids == index, 1.0 - weight, 0.0) + jnp.where(ids == index + 1, weight, 0.0)
            total += jnp.dot(
                spread,
                ref[...].reshape(size, 128),
                preferred_element_type=jnp.float32,
                precision=lax.Precision.HIGHEST,
            )
        edges[0:64, :] = total


def main_kernel(
    count_x, count_y, jump, state, diffuse, vertical_hbm, fill_we_hbm, ra, rb, from_low, from_high,
    colpack, edges, brought_ref,
    out, es, ed, ev, mv, gv, fac, strip, ey, ex, pack, vertical, fill_we, sem,
):
    dx, dy = jump[0], jump[1]
    nx, ny = lax.axis_index("nx"), lax.axis_index("ny")
    copies = []
    for which, (src, dst) in enumerate(((state, es), (diffuse, ed))):
        for l in range(NG):
            copy = pltpu.make_async_copy(
                src.at[:, :, pl.ds(128 * l, 128)], dst.at[:, l, pl.ds(HX, WX), :], sem.at[NG * which + l]
            )
            copy.start()
            copies.append(copy)
    first_copies = [
        pltpu.make_async_copy(vertical_hbm, vertical, sem.at[2 * NG]),
        pltpu.make_async_copy(fill_we_hbm, fill_we, sem.at[2 * NG + 1]),
    ]
    for copy in first_copies:
        copy.start()
    odd = nx % 2 == 1
    lane = lax.broadcasted_iota(jnp.int32, (8, 128), 1)
    lane64 = lax.broadcasted_iota(jnp.int32, (64, 128), 1)

    def beyond(at, size, l):
        a, b = ra[XROWS * l + at : XROWS * l + at + size, :], rb[XROWS * l + at : XROWS * l + at + size, :]
        return jnp.where(odd, b, a), jnp.where(odd, a, b)

    for copy in first_copies:
        copy.wait()
    for l in range(NG):
        for k in range(LV):
            low, high = beyond(k * STATE_ROWS, STATE_ROWS, l)
            es[k, l, HX - STATE_ROWS : HX, :] = low
            es[k, l, HX + WX : HX + WX + STATE_ROWS, :] = high
            low, high = beyond(COEF_AT + k * COEF_ROWS, COEF_ROWS, l)
            ed[k, l, HX - COEF_ROWS : HX, :] = low
            ed[k, l, HX + WX : HX + WX + COEF_ROWS, :] = high
        low, high = beyond(VERT_AT, COEF_ROWS, l)
        ev[l, HX - COEF_ROWS : HX, :] = low
        ev[l, HX + WX : HX + WX + COEF_ROWS, :] = high
        ev[l, HX : HX + WX, :] = vertical[:, 128 * l : 128 * l + 128]

    def corner(side, l):
        n = CORNER_AT + 8 * (NG * side + l)
        a, b = ra[n : n + 8, :], rb[n : n + 8, :]
        return jnp.where(odd, b, a), jnp.where(odd, a, b)

    for side, ref in enumerate((from_low, from_high)):
        strip[side, HX : HX + WX, :] = ref[...]
        for l in range(NG):
            low, high = corner(side, l)
            strip[side, 0:HX, 128 * l : 128 * l + 128] = low
            strip[side, HX + WX : 64, 128 * l : 128 * l + 128] = high
    low, high = corner(0, NG - 1)
    pack[0:HX, :] = low
    pack[HX : HX + WX, :] = colpack[...]
    pack[HX + WX : 64, :] = high
    for which, dst in enumerate((es, ed)):
        lanes = slice(128 * which, 128 * which + 128)
        for k in range(LV):
            dst[k, NG, 0:64, :] = jnp.where(
                lane64 < 64,
                pltpu.roll(strip[1, :, lanes], (-8 * k) % 128, 1),
                pltpu.roll(strip[0, :, lanes], (120 - 8 * k) % 128, 1),
            )
    ev[NG, 0:64, :] = jnp.where(
        lane64 < 64, strip[1, :, 256:384], pltpu.roll(strip[0, :, 256:384], 120, 1)
    )

    west, east = nx == 0, nx == count_x - 1
    south, north = ny == 0, ny == count_y - 1

    @pl.when(west | east)
    def _():
        brought = (ny == 1) | (ny == count_y - 2)
        for l in range(NG + 1):
            rows = slice(64 + 48 * l, 112 + 48 * l)
            ey[l] = jnp.where(brought, brought_ref[rows, :], edges[rows, :])

    @pl.when(south | north)
    def _():
        ex[...] = jnp.where(west | east, brought_ref[0:64, :], edges[0:64, :])

    def ghosts(field, step, row_low, row_high, shift):
        @pl.when(west)
        def _():
            for k in range(LV):
                for l in range(NG + 1):
                    field[k, l, row_low : row_low + 1, :] = ey[l, 16 * step + k : 16 * step + k + 1, :]

        @pl.when(east)
        def _():
            for k in range(LV):
                for l in range(NG + 1):
                    field[k, l, row_high : row_high + 1, :] = ey[l, 16 * step + k : 16 * step + k + 1, :]

        @pl.when(south | north)
        def _():
            at = jnp.where(south, 127, 0)
            lanes = lax.broadcasted_iota(jnp.int32, (56, 128), 1)
            for k in range(LV):
                col = ex[shift : shift + 56, 16 * step + k : 16 * step + k + 1]
                field[k, NG, 0:56, :] = jnp.where(lanes == at, col, field[k, NG, 0:56, :])

    def ghost_tail(step):
        @pl.when(south | north)
        def _():
            at = jnp.where(south, 127, 0)
            for k in range(LV):
                col = ex[56:64, 16 * step + k : 16 * step + k + 1]
                es[k, NG, 56:64, :] = jnp.where(lane == at, col, es[k, NG, 56:64, :])

    for copy in copies:
        copy.wait()
    ghosts(es, 0, HX - 1, HX + WX, 0)
    ghost_tail(0)

    def sideways(c):
        lefts = [pltpu.roll(x, 1, 1) for x in c]
        rights = [pltpu.roll(x, 127, 1) for x in c]
        n = len(c)
        left = [jnp.where(lane == 0, lefts[l - 1], lefts[l]) for l in range(n)]
        right = [jnp.where(lane == 127, rights[(l + 1) % n], rights[l]) for l in range(n)]
        return left, right

    def advance(field, at, coef_at, groups, write_source, read_source, write):
        g = [ev[l, pl.ds(coef_at, 8), :] for l in range(groups)]
        factor, source = [None] * groups, [None] * groups
        for k in range(LV):
            c = [field[k, l, pl.ds(at, 8), :] for l in range(NG + 1)]
            left, right = sideways(c)
            for l in range(groups):
                lap = (
                    field[k, l, pl.ds(at + 1, 8), :]
                    + field[k, l, pl.ds(at - 1, 8), :]
                    + right[l]
                    + left[l]
                    - 4.0 * c[l]
                )
                explicit = c[l] + ed[k, l, pl.ds(coef_at, 8), :] * lap
                diagonal = 1.0 + (g[l] if k in (0, LV - 1) else 2.0 * g[l])
                if k > 0:
                    diagonal = diagonal + g[l] * factor[l]
                    explicit = explicit + g[l] * source[l]
                inverse = 1.0 / diagonal
                factor[l] = -g[l] * inverse
                source[l] = explicit * inverse
                fac[k, l] = factor[l]
                if k < LV - 1:
                    write_source(k, l, source[l])
        value = source
        write(LV - 1, value)
        for k in range(LV - 2, -1, -1):
            value = [read_source(k, l) - fac[k, l] * value[l] for l in range(groups)]
            write(k, value)

    turn = (128 - 3 * dy) % 128

    @pl.loop(0, 7)
    def _(t):
        to = pl.multiple_of(8 * t, 8)

        def put(k, l, x):
            mv[k, l, pl.ds(to, 8), :] = x

        def take(k, l):
            return mv[k, l, pl.ds(to, 8), :]

        def moved(k, values):
            turned = [pltpu.roll(x, turn, 1) for x in values]
            for l in range(NG + 1):
                x = jnp.where(lane >= 128 - 3 * dy, turned[(l + 1) % (NG + 1)], turned[l])
                put(k, l, jnp.where(lane < -3 * dy, turned[l - 1], x))

        at = HX - 2 + 3 * dx + 8 * t
        advance(es, at, at, NG + 1, put, take, moved)

    @pl.when((south & (dy < 0)) | (north & (dy > 0)))
    def _():
        row = lax.broadcasted_iota(jnp.int32, (56, 128), 0)
        cell = (((row + 4) * 21846) >> 16) - 2 + dx
        lanes = lax.broadcasted_iota(jnp.int32, (56, 128), 1)
        total = jnp.zeros((56, 128), jnp.float32)
        for q in range(-2, 18):
            r = q + 8 if q < 0 else (q + HX if q < 8 else q + 40)
            total = jnp.where(cell == q, pack[r : r + 1, :], total)

        for is_side, side, l, first in ((south, 0, 0, 0), (north, 1, NG - 1, 125)):

            @pl.when(is_side)
            def _():
                inside = (lanes >= first) & (lanes < first + 3)
                for k in range(LV):
                    n = 96 + 16 * side + k
                    mv[k, l, 0:56, :] = jnp.where(inside, total[:, n : n + 1], mv[k, l, 0:56, :])

    @pl.when((west & (dx < 0)) | (east & (dx > 0)))
    def _():
        lane16 = lax.broadcasted_iota(jnp.int32, (16, 128), 1)
        for is_side, side, first in ((west, 0, 2), (east, 1, 47)):

            @pl.when(is_side)
            def _():
                own = fill_we[side]
                ring = jnp.where(
                    lane16 < 64,
                    pltpu.roll(strip[1, HX + 16 * side : HX + 16 * side + 16, 256:384], 120, 1),
                    pltpu.roll(strip[0, HX + 16 * side : HX + 16 * side + 16, 256:384], 112, 1),
                )
                for l in range(NG + 1):
                    column = lane16 + 128 * l
                    if l == NG:
                        column = jnp.where(lane16 < 64, column, lane16 - 128)
                    cell = (((column + 384) * 21846) >> 16) - 128 + dy
                    cell = jnp.clip(cell, -128 * ny, 128 * (count_y - ny) - 1)
                    inside = cell & 127
                    a = jnp.take_along_axis(own, inside, axis=1, mode="promise_in_bounds")
                    b = jnp.take_along_axis(ring, inside, axis=1, mode="promise_in_bounds")
                    ey[l, 0:16, :] = jnp.where((cell >= 0) & (cell < 128), a, b)
                    for k in range(LV):
                        mv[k, l, first : first + 3, :] = jnp.broadcast_to(ey[l, k : k + 1, :], (3, 128))

    ghosts(mv, 1, 1, WX + 2, HX - 2)

    @pl.loop(0, 7)
    def _(t):
        to = pl.multiple_of(8 * t, 8)

        def put(k, l, x):
            gv[k, l, pl.ds(to, 8), :] = x

        def take(k, l):
            return gv[k, l, pl.ds(to, 8), :]

        def keep(k, values):
            for l in range(NG + 1):
                put(k, l, values[l])

        advance(mv, 1 + 8 * t, HX - 1 + 8 * t, NG + 1, put, take, keep)

    ghosts(gv, 2, 0, WX + 1, HX - 1)

    @pl.loop(0, 6)
    def _(t):
        to = pl.multiple_of(8 * t, 8)

        def put(k, l, x):
            out[k, pl.ds(to, 8), 128 * l : 128 * l + 128] = x

        def take(k, l):
            return out[k, pl.ds(to, 8), 128 * l : 128 * l + 128]

        def keep(k, values):
            for l in range(NG):
                put(k, l, values[l])

        advance(gv, 1 + 8 * t, HX + 8 * t, NG, put, take, keep)


def on_device(
    state,
    diffuse,
    vertical,
    rows_we,
    rows_sn,
    fill_we,
    fill_sn,
    index_we,
    weight_we,
    index_sn,
    weight_sn,
    jump,
):
    f32 = jnp.float32
    count_x, count_y = lax.axis_size("nx"), lax.axis_size("ny")
    both = ("nx", "ny")
    vmem = pl.BlockSpec(memory_space=pltpu.VMEM)
    smem = pl.BlockSpec(memory_space=pltpu.SMEM)
    hbm = pl.BlockSpec(memory_space=pltpu.HBM)
    any_ = pl.BlockSpec(memory_space=pl.ANY)

    def shape(*dims):
        return jax.ShapeDtypeStruct(dims, f32)

    state, diffuse, vertical, rows_we, rows_sn, fill_we, fill_sn, index_we, weight_we, index_sn, weight_sn = (
        pltpu.with_memory_space_constraint(x, pltpu.HBM)
        for x in (
            state, diffuse, vertical, rows_we, rows_sn, fill_we, fill_sn, index_we, weight_we, index_sn, weight_sn
        )
    )
    y_low, y_high, chain_x, chain_y, colpack, interp = pl.pallas_call(
        pack_kernel,
        out_shape=(
            shape(WX, WY),
            shape(WX, WY),
            shape(1, 16, 128),
            shape(1, 48, 128),
            shape(WX, 128),
            shape(8, WY),
        ),
        in_specs=[hbm] * 11,
        out_specs=(vmem,) * 6,
        scratch_shapes=[
            pltpu.VMEM((2, LV, WX, 128), f32),
            pltpu.VMEM((2, LV, WX, 128), f32),
            pltpu.VMEM((WX, WY), f32),
            pltpu.VMEM((3, 16, 128), f32),
            pltpu.VMEM((3, 16, 16), f32),
            pltpu.VMEM((2, 16, 128), f32),
            pltpu.VMEM((2, 16, 16), f32),
            pltpu.VMEM((WY,), jnp.int32),
            pltpu.VMEM((WY,), f32),
            pltpu.VMEM((WX,), jnp.int32),
            pltpu.VMEM((WX,), f32),
            pltpu.VMEM((128, 128), f32),
            pltpu.SemaphoreType.DMA((13,)),
        ],
        compiler_params=pltpu.CompilerParams(vmem_limit_bytes=16 << 20),
        name="pack",
    )(state, diffuse, vertical, rows_we, rows_sn, fill_we, fill_sn, index_we, weight_we, index_sn, weight_sn)

    pairs_a = [(i, i + 1) for i in range(1, count_x - 1, 2)]
    pairs_a += [(b, a) for a, b in pairs_a]
    pairs_b = [(i, i + 1) for i in range(0, count_x, 2)]
    pairs_b += [(b, a) for a, b in pairs_b]
    up = [(i, i + 1) for i in range(count_y - 1)]
    down = [(b, a) for a, b in up]
    rounds_x, rounds_y = rounds_of(count_x), rounds_of(count_y)

    def place(i, j):
        return i * count_y + j

    last_x, last_y = count_x - 1, count_y - 1
    set_x = [
        [place(i, (1 if i in (0, last_x) else 0) if side == 0 else (last_y - 1 if i in (0, last_x) else last_y))
         for i in range(count_x)]
        for side in range(2)
    ]
    set_y = [
        [place((1 if j in (1, last_y - 1) else 0) if side == 0 else (last_x - 1 if j in (1, last_y - 1) else last_x), j)
         for j in range(count_y)]
        for side in range(2)
    ]
    bring = []
    for i, step in ((0, 1), (last_x, -1)):
        for j, other in ((0, 1), (last_y, last_y - 1)):
            bring.append((place(i, other), place(i, j)))
            bring.append((place(i + step, other), place(i, other)))

    def along(sets, chain, masks):
        return [
            lax.ppermute(chain, both, [(own[n], own[n ^ m]) for own in sets for n in range(len(own))]) for m in masks
        ]

    along_x, along_y = functools.partial(along, set_x), functools.partial(along, set_y)

    def join(parts_x, parts_y, name):
        return pl.pallas_call(
            functools.partial(join_kernel, len(parts_x), len(parts_y)),
            out_shape=(
                shape(sum(p.shape[0] for p in parts_x), 16, 128),
                shape(sum(p.shape[0] for p in parts_y), 48, 128),
            ),
            in_specs=[vmem] * (len(parts_x) + len(parts_y)),
            out_specs=(vmem, vmem),
            compiler_params=pltpu.CompilerParams(vmem_limit_bytes=8 << 20),
            name=name,
        )(*parts_x, *parts_y)

    parts_x = [chain_x] + along_x(chain_x, rounds_x[0])
    parts_y = [chain_y] + along_y(chain_y, rounds_y[0])
    from_low = lax.ppermute(y_high, "ny", up)
    from_high = lax.ppermute(y_low, "ny", down)
    xa, xb = pl.pallas_call(
        border_kernel,
        out_shape=(shape(SENT, 128), shape(SENT, 128)),
        in_specs=[any_] * 2 + [hbm] * 3 + [vmem] * 3,
        out_specs=(vmem, vmem),
        scratch_shapes=[
            pltpu.VMEM((2, LV, 8, WY), f32),
            pltpu.VMEM((2, LV, 8, WY), f32),
            pltpu.VMEM((WX, WY), f32),
            pltpu.SemaphoreType.DMA((5,)),
        ],
        compiler_params=pltpu.CompilerParams(vmem_limit_bytes=8 << 20),
        name="border",
    )(parts_x[-1], parts_y[-1], state, diffuse, vertical, from_low, from_high, colpack)
    ra = lax.ppermute(xa, "nx", pairs_a)
    rb = lax.ppermute(xb, "nx", pairs_b)
    chain_x, chain_y = join(parts_x, parts_y, "join_first")
    parts_x = [chain_x] + along_x(chain_x, rounds_x[1])
    parts_y = [chain_y] + along_y(chain_y, rounds_y[1])
    chain_x, chain_y = join(parts_x, parts_y, "join_second")
    parts_x = [chain_x] + along_x(chain_x, rounds_x[2])
    parts_y = [chain_y] + along_y(chain_y, rounds_y[2])
    have_x, have_y = masks_of(rounds_x[:2]), masks_of(rounds_y[:2])
    plan_x = [[m ^ h for h in have_x] for m in [0] + rounds_x[2]]
    plan_y = [[m ^ h for h in have_y] for m in [0] + rounds_y[2]]

    edges = pl.pallas_call(
        functools.partial(edge_kernel, count_x, count_y, plan_x, plan_y),
        out_shape=shape(256, 128),
        in_specs=[vmem] * (6 + len(parts_x) + len(parts_y)),
        out_specs=vmem,
        scratch_shapes=[pltpu.VMEM((64, 128), f32)],
        compiler_params=pltpu.CompilerParams(vmem_limit_bytes=8 << 20),
        name="edges",
    )(ra, rb, from_low, from_high, colpack, interp, *parts_x, *parts_y)
    brought = lax.ppermute(edges, both, bring)

    return pl.pallas_call(
        functools.partial(main_kernel, count_x, count_y),
        out_shape=shape(LV, WX, WY),
        in_specs=[smem] + [hbm] * 4 + [vmem] * 7,
        out_specs=vmem,
        scratch_shapes=[
            pltpu.VMEM((LV, NG + 1, 72, 128), f32),
            pltpu.VMEM((LV, NG + 1, 72, 128), f32),
            pltpu.VMEM((NG + 1, 72, 128), f32),
            pltpu.VMEM((LV, NG + 1, 64, 128), f32),
            pltpu.VMEM((LV, NG + 1, 64, 128), f32),
            pltpu.VMEM((LV, NG + 1, 8, 128), f32),
            pltpu.VMEM((2, 64, WY), f32),
            pltpu.VMEM((NG + 1, 48, 128), f32),
            pltpu.VMEM((64, 128), f32),
            pltpu.VMEM((64, 128), f32),
            pltpu.VMEM((WX, WY), f32),
            pltpu.VMEM((2, 16, 128), f32),
            pltpu.SemaphoreType.DMA((2 * NG + 2,)),
        ],
        compiler_params=pltpu.CompilerParams(vmem_limit_bytes=22 << 20),
        name="steps",
    )(
        jump, state, diffuse, vertical, fill_we, ra, rb, from_low, from_high,
        colpack, edges, brought,
    )


def solution(mesh):
    return jax.shard_map(
        on_device,
        mesh=mesh,
        in_specs=(
            P(None, "nx", "ny"),
            P(None, "nx", "ny"),
            P("nx", "ny"),
            P(None, None, None, "ny"),
            P(None, None, None, "nx"),
            P(None, None, "ny"),
            P(None, None, "nx"),
            P("ny"),
            P("ny"),
            P("nx"),
            P("nx"),
            P(),
        ),
        out_specs=P(None, "nx", "ny"),
        check_vma=False,
    )
```

```python
import functools

import jax
import jax.numpy as jnp
from jax import lax
from jax.experimental import pallas as pl
from jax.experimental.pallas import tpu as pltpu
from jax.sharding import PartitionSpec as P

LV = 16
WX = 48
WY = 384
NG = WY // 128
HX = 8
STATE_ROWS = 6
COEF_ROWS = 5
COEF_AT = LV * STATE_ROWS
VERT_AT = COEF_AT + LV * COEF_ROWS
XROWS = 184
CORNER_AT = NG * XROWS
FIRST = 10
SENT = CORNER_AT + 16 * NG


def rounds_of(count):
    if count == 32:
        return [[16], [4, 8, 12], [1, 2, 3]]
    if count == 16:
        return [[8], [2, 4, 6], [1]]
    return [[2], [1], []]


def masks_of(rounds):
    have = [0]
    for masks in rounds:
        have = [m ^ h for m in [0] + masks for h in have]
    return have


def pack_kernel(
    state_hbm, diffuse_hbm, vertical_hbm, rows_we_hbm, rows_sn_hbm, fill_we_hbm, fill_sn_hbm,
    index_we_hbm, weight_we_hbm, index_sn_hbm, weight_sn_hbm,
    y_low, y_high, chain_x, chain_y, colpack, interp,
    state, diffuse, vertical, rows_we, rows_sn, fill_we, fill_sn, index_we, weight_we, index_sn, weight_sn,
    square, sem,
):
    nx, ny = lax.axis_index("nx"), lax.axis_index("ny")
    side_x = jnp.where(ny < lax.axis_size("ny") // 2, 0, 1)
    side_y = jnp.where(nx < lax.axis_size("nx") // 2, 0, 1)
    pairs = [
        (rows_we_hbm.at[:, side_y], rows_we),
        (rows_sn_hbm.at[:, side_x], rows_sn),
        (fill_we_hbm, fill_we),
        (fill_sn_hbm, fill_sn),
        (index_we_hbm, index_we),
        (weight_we_hbm, weight_we),
        (index_sn_hbm, index_sn),
        (weight_sn_hbm, weight_sn),
        (vertical_hbm, vertical),
    ]
    for src, dst in ((state_hbm, state), (diffuse_hbm, diffuse)):
        for at, group in enumerate((0, NG - 1)):
            pairs.append((src.at[:, :, pl.ds(128 * group, 128)], dst.at[at]))
    copies = [pltpu.make_async_copy(src, dst, sem.at[n]) for n, (src, dst) in enumerate(pairs)]
    for copy in copies:
        copy.start()
    lane = lax.broadcasted_iota(jnp.int32, (128, 128), 1)
    square[...] = jnp.zeros((128, 128), jnp.float32)
    interp[...] = jnp.zeros((8, WY), jnp.float32)
    for copy in copies[:8]:
        copy.wait()
    for step in range(3):
        chain_y[0, 16 * step : 16 * step + 16, :] = rows_we[step]
        square[16 * step : 16 * step + 16, 0:16] = rows_sn[step]
    chain_x[...] = jnp.zeros((FIRST, 16, 128), jnp.float32)
    chain_x[0] = square[...].T[0:16]
    square[0:48, :] = jnp.zeros((48, 128), jnp.float32)
    square[96:112, 0:16] = fill_sn[0]
    square[112:128, 0:16] = fill_sn[1]
    square[64:65, 0:WX] = index_sn[...].astype(jnp.float32).reshape(1, WX)
    square[65:66, 0:WX] = weight_sn[...].reshape(1, WX)
    whole = square[...]
    row = lax.broadcasted_iota(jnp.int32, (128, 128), 0)
    whole = jnp.where((lane < 8) | (row < 96), whole, pltpu.roll(whole, 32, 1))
    colpack[...] = whole.T[0:WX]
    interp[0:1, :] = index_we[...].astype(jnp.float32).reshape(1, WY)
    interp[1:2, :] = weight_we[...].reshape(1, WY)
    square[0:16, :] = fill_we[0]
    square[16:32, :] = fill_we[1]
    for copy in copies[8:]:
        copy.wait()

    lane = lax.broadcasted_iota(jnp.int32, (WX, 128), 1)
    row = lax.broadcasted_iota(jnp.int32, (WX, 128), 0)
    for at, (ref, group, first) in enumerate(((y_low, 0, 0), (y_high, NG - 1, 120))):
        lanes = slice(128 * group, 128 * group + 128)
        for which, field in enumerate((state, diffuse)):
            total = jnp.zeros((WX, 128), jnp.float32)
            for k in range(LV):
                part = pltpu.roll(field[at, k], (8 * k - first) % 128, 1)
                total = jnp.where((lane >= 8 * k) & (lane < 8 * k + 8), part, total)
            ref[:, 128 * which : 128 * which + 128] = total
        last = jnp.where(lane < 8, pltpu.roll(vertical[:, lanes], (-first) % 128, 1), 0.0)
        last = jnp.where(
            (lane >= 8) & (lane < 16), pltpu.roll(square[0:WX, :], (8 - first) % 128, 1), last
        )
        pair = jnp.where(row == 0, interp[0:1, lanes], interp[1:2, lanes])
        last = jnp.where(
            (lane >= 16) & (lane < 24) & (row < 2), pltpu.roll(pair, (16 - first) % 128, 1), last
        )
        ref[:, 256:384] = last


def border_kernel(
    after_x, after_y, state_hbm, diffuse_hbm, vertical_hbm, from_low, from_high, colpack,
    xa, xb, state, diffuse, vertical, sem,
):
    copies = [pltpu.make_async_copy(vertical_hbm, vertical, sem.at[4])]
    for n, (src, dst) in enumerate(((state_hbm, state), (diffuse_hbm, diffuse))):
        for side in range(2):
            copies.append(
                pltpu.make_async_copy(src.at[:, pl.ds(40 * side, 8), :], dst.at[side], sem.at[2 * n + side])
            )
    for copy in copies:
        copy.start()
    odd = lax.axis_index("nx") % 2 == 1
    clear = lax.broadcasted_iota(jnp.int32, (8, 128), 1) < 64
    for copy in copies:
        copy.wait()

    def rows(ref, side):
        at = 8 - STATE_ROWS if side else 0
        bt = 8 - COEF_ROWS if side else 0
        for l in range(NG):
            lanes = slice(128 * l, 128 * l + 128)
            base = XROWS * l
            for k in range(LV):
                n = base + k * STATE_ROWS
                ref[n : n + STATE_ROWS, :] = state[side, k, at : at + STATE_ROWS, lanes]
                n = base + COEF_AT + k * COEF_ROWS
                ref[n : n + COEF_ROWS, :] = diffuse[side, k, bt : bt + COEF_ROWS, lanes]
            n = base + VERT_AT
            ref[n : n + COEF_ROWS, :] = vertical[40 * side + bt : 40 * side + bt + COEF_ROWS, lanes]
            ref[n + COEF_ROWS : base + XROWS, :] = jnp.zeros((XROWS - VERT_AT - COEF_ROWS, 128), jnp.float32)
        for which, strips in enumerate((from_low, from_high)):
            for l in range(NG):
                part = strips[40 * side : 40 * side + 8, 128 * l : 128 * l + 128]
                if which == 0 and l == NG - 1:
                    part = jnp.where(clear, part, colpack[40 * side : 40 * side + 8, :])
                n = CORNER_AT + 8 * (NG * which + l)
                ref[n : n + 8, :] = part

    @pl.when(odd)
    def _():
        rows(xa, 1)
        rows(xb, 0)

    @pl.when(jnp.logical_not(odd))
    def _():
        rows(xa, 0)
        rows(xb, 1)


def join_kernel(count_x, count_y, *refs):
    ins, (out_x, out_y) = refs[:-2], refs[-2:]
    for out, parts in ((out_x, ins[:count_x]), (out_y, ins[count_x : count_x + count_y])):
        at = 0
        for part in parts:
            size = 1 if part.shape[0] == FIRST else part.shape[0]
            out[at : at + size] = part[0:size]
            at += size


def edge_kernel(count_x, count_y, plan_x, plan_y, pack, from_low, from_high, interp, *refs):
    chain_x, refs = refs[: len(plan_x)], refs[len(plan_x) :]
    chain_y, refs = refs[: len(plan_y)], refs[len(plan_y) :]
    (edges,) = refs
    nx, ny = lax.axis_index("nx"), lax.axis_index("ny")
    border_x = (nx == 0) | (nx == count_x - 1)
    border_y = (ny == 0) | (ny == count_y - 1)
    inner_x = (nx == 1) | (nx == count_x - 2)
    inner_y = (ny == 1) | (ny == count_y - 2)

    @pl.when((border_x & jnp.logical_not(inner_y)) | (inner_x & inner_y))
    def _():
        lane1 = lax.broadcasted_iota(jnp.int32, (1, 128), 1)
        for l in range(NG + 1):
            got = []
            for item in range(2):
                if l < NG:
                    got.append(interp[item : item + 1, 128 * l : 128 * l + 128])
                else:
                    got.append(
                        jnp.where(
                            lane1 < 64,
                            pltpu.roll(from_high[0:8, 256:384], 112, 1)[item : item + 1],
                            pltpu.roll(from_low[0:8, 256:384], 104, 1)[item : item + 1],
                        )
                    )
            index = jnp.broadcast_to(got[0], (48, 128)).astype(jnp.int32)
            ends = []
            for offset in range(2):
                at = index + offset
                block, inside = at >> 7, at & 127
                total = jnp.zeros((48, 128), jnp.float32)
                for ref, masks in zip(chain_y, plan_y, strict=True):
                    for piece, mask in enumerate(masks):
                        value = jnp.take_along_axis(ref[piece], inside, axis=1, mode="promise_in_bounds")
                        total = jnp.where(block == (ny ^ mask), value, total)
                ends.append(total)
            edges[64 + 48 * l : 112 + 48 * l, :] = (1.0 - got[1]) * ends[0] + got[1] * ends[1]

    @pl.when((border_y & jnp.logical_not(border_x)) | (border_x & inner_y))
    def _():
        index = pack[:, 64:65].astype(jnp.int32)
        weight = pack[:, 65:66]
        total = jnp.zeros((64, 128), jnp.float32)
        for ref, masks in zip(chain_x, plan_x, strict=True):
            size = 16 * len(masks)
            at = lax.broadcasted_iota(jnp.int32, (1, size), 1)
            ids = at & 15
            for piece, mask in enumerate(masks):
                ids = jnp.where(at >> 4 == piece, ids + 16 * (nx ^ mask), ids)
            spread = jnp.where(ids == index, 1.0 - weight, 0.0) + jnp.where(ids == index + 1, weight, 0.0)
            total += jnp.dot(
                spread,
                ref[...].reshape(size, 128),
                preferred_element_type=jnp.float32,
                precision=lax.Precision.HIGHEST,
            )
        edges[0:64, :] = total


def prepare_kernel(
    state, diffuse, vertical_hbm, ra, rb, from_low, from_high, colpack, es, ed, ev, inv, pack, strip, vertical, sem
):
    nx = lax.axis_index("nx")
    copies = []
    for which, (src, dst) in enumerate(((state, es), (diffuse, ed))):
        for l in range(NG):
            copy = pltpu.make_async_copy(
                src.at[:, :, pl.ds(128 * l, 128)], dst.at[:, l, pl.ds(HX, WX), :], sem.at[NG * which + l]
            )
            copy.start()
            copies.append(copy)
    first_copies = [
        pltpu.make_async_copy(vertical_hbm, vertical, sem.at[2 * NG]),
    ]
    for copy in first_copies:
        copy.start()
    odd = nx % 2 == 1
    lane64 = lax.broadcasted_iota(jnp.int32, (64, 128), 1)

    def beyond(at, size, l):
        a, b = ra[XROWS * l + at : XROWS * l + at + size, :], rb[XROWS * l + at : XROWS * l + at + size, :]
        return jnp.where(odd, b, a), jnp.where(odd, a, b)

    for copy in first_copies:
        copy.wait()
    for l in range(NG):
        for k in range(LV):
            low, high = beyond(k * STATE_ROWS, STATE_ROWS, l)
            es[k, l, HX - STATE_ROWS : HX, :] = low
            es[k, l, HX + WX : HX + WX + STATE_ROWS, :] = high
            low, high = beyond(COEF_AT + k * COEF_ROWS, COEF_ROWS, l)
            ed[k, l, HX - COEF_ROWS : HX, :] = low
            ed[k, l, HX + WX : HX + WX + COEF_ROWS, :] = high
        low, high = beyond(VERT_AT, COEF_ROWS, l)
        ev[l, HX - COEF_ROWS : HX, :] = low
        ev[l, HX + WX : HX + WX + COEF_ROWS, :] = high
        ev[l, HX : HX + WX, :] = vertical[:, 128 * l : 128 * l + 128]

    def corner(side, l):
        n = CORNER_AT + 8 * (NG * side + l)
        a, b = ra[n : n + 8, :], rb[n : n + 8, :]
        return jnp.where(odd, b, a), jnp.where(odd, a, b)

    for side, ref in enumerate((from_low, from_high)):
        strip[side, HX : HX + WX, :] = ref[...]
        for l in range(NG):
            low, high = corner(side, l)
            strip[side, 0:HX, 128 * l : 128 * l + 128] = low
            strip[side, HX + WX : 64, 128 * l : 128 * l + 128] = high
    low, high = corner(0, NG - 1)
    pack[0:HX, :] = low
    pack[HX : HX + WX, :] = colpack[...]
    pack[HX + WX : 64, :] = high
    for which, dst in enumerate((es, ed)):
        lanes = slice(128 * which, 128 * which + 128)
        for k in range(LV):
            dst[k, NG, 0:64, :] = jnp.where(
                lane64 < 64,
                pltpu.roll(strip[1, :, lanes], (-8 * k) % 128, 1),
                pltpu.roll(strip[0, :, lanes], (120 - 8 * k) % 128, 1),
            )
    ev[NG, 0:64, :] = jnp.where(
        lane64 < 64, strip[1, :, 256:384], pltpu.roll(strip[0, :, 256:384], 120, 1)
    )


    @pl.loop(0, 8)
    def _(t):
        rows = pl.ds(pl.multiple_of(8 * t, 8), 8)
        for l in range(NG + 1):
            g = ev[l, rows, :]
            inverse = 1.0 / (1.0 + g)
            inv[0, l, rows, :] = inverse
            for k in range(1, LV):
                diagonal = 1.0 + (g if k == LV - 1 else 2.0 * g)
                inverse = 1.0 / (diagonal - g * (g * inverse))
                inv[k, l, rows, :] = inverse

    for copy in copies:
        copy.wait()


def main_kernel(
    count_x, count_y, jump, fill_we_hbm, from_low, from_high, es_in, ed, ev, inv, pack, edges, brought_ref,
    out, es, mv, gv, ey, ex, fill_we, sem,
):
    dx, dy = jump[0], jump[1]
    nx, ny = lax.axis_index("nx"), lax.axis_index("ny")
    lane = lax.broadcasted_iota(jnp.int32, (8, 128), 1)
    fetch = pltpu.make_async_copy(fill_we_hbm, fill_we, sem)
    fetch.start()
    west, east = nx == 0, nx == count_x - 1
    south, north = ny == 0, ny == count_y - 1

    @pl.when(west | east)
    def _():
        brought = (ny == 1) | (ny == count_y - 2)
        for l in range(NG + 1):
            rows = slice(64 + 48 * l, 112 + 48 * l)
            ey[l] = jnp.where(brought, brought_ref[rows, :], edges[rows, :])

    @pl.when(south | north)
    def _():
        ex[...] = jnp.where(west | east, brought_ref[0:64, :], edges[0:64, :])

    def ghosts(field, step, row_low, row_high, shift):
        @pl.when(west)
        def _():
            for k in range(LV):
                for l in range(NG + 1):
                    field[k, l, row_low : row_low + 1, :] = ey[l, 16 * step + k : 16 * step + k + 1, :]

        @pl.when(east)
        def _():
            for k in range(LV):
                for l in range(NG + 1):
                    field[k, l, row_high : row_high + 1, :] = ey[l, 16 * step + k : 16 * step + k + 1, :]

        @pl.when(south | north)
        def _():
            at = jnp.where(south, 127, 0)
            lanes = lax.broadcasted_iota(jnp.int32, (56, 128), 1)
            for k in range(LV):
                col = ex[shift : shift + 56, 16 * step + k : 16 * step + k + 1]
                field[k, NG, 0:56, :] = jnp.where(lanes == at, col, field[k, NG, 0:56, :])

    def ghost_tail(step):
        @pl.when(south | north)
        def _():
            at = jnp.where(south, 127, 0)
            for k in range(LV):
                col = ex[56:64, 16 * step + k : 16 * step + k + 1]
                es[k, NG, 56:64, :] = jnp.where(lane == at, col, es[k, NG, 56:64, :])

    ghosts(es, 0, HX - 1, HX + WX, 0)
    ghost_tail(0)

    def sideways(c):
        lefts = [pltpu.roll(x, 1, 1) for x in c]
        rights = [pltpu.roll(x, 127, 1) for x in c]
        n = len(c)
        left = [jnp.where(lane == 0, lefts[l - 1], lefts[l]) for l in range(n)]
        right = [jnp.where(lane == 127, rights[(l + 1) % n], rights[l]) for l in range(n)]
        return left, right

    def advance(field, at, coef_at, groups, write_source, read_source, write):
        g = [ev[l, pl.ds(coef_at, 8), :] for l in range(groups)]
        source = [None] * groups
        for k in range(LV):
            c = [field[k, l, pl.ds(at, 8), :] for l in range(NG + 1)]
            left, right = sideways(c)
            for l in range(groups):
                lap = (
                    field[k, l, pl.ds(at + 1, 8), :]
                    + field[k, l, pl.ds(at - 1, 8), :]
                    + right[l]
                    + left[l]
                    - 4.0 * c[l]
                )
                explicit = c[l] + ed[k, l, pl.ds(coef_at, 8), :] * lap
                if k > 0:
                    explicit = explicit + g[l] * source[l]
                source[l] = explicit * inv[k, l, pl.ds(coef_at, 8), :]
                if k < LV - 1:
                    write_source(k, l, source[l])
        value = source
        write(LV - 1, value)
        for k in range(LV - 2, -1, -1):
            value = [
                read_source(k, l) + (g[l] * inv[k, l, pl.ds(coef_at, 8), :]) * value[l] for l in range(groups)
            ]
            write(k, value)

    turn = (128 - 3 * dy) % 128

    @pl.loop(0, 7)
    def _(t):
        to = pl.multiple_of(8 * t, 8)

        def put(k, l, x):
            mv[k, l, pl.ds(to, 8), :] = x

        def take(k, l):
            return mv[k, l, pl.ds(to, 8), :]

        def moved(k, values):
            turned = [pltpu.roll(x, turn, 1) for x in values]
            for l in range(NG + 1):
                x = jnp.where(lane >= 128 - 3 * dy, turned[(l + 1) % (NG + 1)], turned[l])
                put(k, l, jnp.where(lane < -3 * dy, turned[l - 1], x))

        at = HX - 2 + 3 * dx + 8 * t
        advance(es, at, at, NG + 1, put, take, moved)

    @pl.when((south & (dy < 0)) | (north & (dy > 0)))
    def _():
        row = lax.broadcasted_iota(jnp.int32, (56, 128), 0)
        cell = (((row + 4) * 21846) >> 16) - 2 + dx
        lanes = lax.broadcasted_iota(jnp.int32, (56, 128), 1)
        total = jnp.zeros((56, 128), jnp.float32)
        for q in range(-2, 18):
            r = q + 8 if q < 0 else (q + HX if q < 8 else q + 40)
            total = jnp.where(cell == q, pack[r : r + 1, :], total)

        for is_side, side, l, first in ((south, 0, 0, 0), (north, 1, NG - 1, 125)):

            @pl.when(is_side)
            def _():
                inside = (lanes >= first) & (lanes < first + 3)
                for k in range(LV):
                    n = 96 + 16 * side + k
                    mv[k, l, 0:56, :] = jnp.where(inside, total[:, n : n + 1], mv[k, l, 0:56, :])

    fetch.wait()

    @pl.when((west & (dx < 0)) | (east & (dx > 0)))
    def _():
        lane16 = lax.broadcasted_iota(jnp.int32, (16, 128), 1)
        for is_side, side, first in ((west, 0, 2), (east, 1, 47)):

            @pl.when(is_side)
            def _():
                own = fill_we[side]
                ring = jnp.where(
                    lane16 < 64,
                    pltpu.roll(from_high[16 * side : 16 * side + 16, 256:384], 120, 1),
                    pltpu.roll(from_low[16 * side : 16 * side + 16, 256:384], 112, 1),
                )
                for l in range(NG + 1):
                    column = lane16 + 128 * l
                    if l == NG:
                        column = jnp.where(lane16 < 64, column, lane16 - 128)
                    cell = (((column + 384) * 21846) >> 16) - 128 + dy
                    cell = jnp.clip(cell, -128 * ny, 128 * (count_y - ny) - 1)
                    inside = cell & 127
                    a = jnp.take_along_axis(own, inside, axis=1, mode="promise_in_bounds")
                    b = jnp.take_along_axis(ring, inside, axis=1, mode="promise_in_bounds")
                    ey[l, 0:16, :] = jnp.where((cell >= 0) & (cell < 128), a, b)
                    for k in range(LV):
                        mv[k, l, first : first + 3, :] = jnp.broadcast_to(ey[l, k : k + 1, :], (3, 128))

    ghosts(mv, 1, 1, WX + 2, HX - 2)

    @pl.loop(0, 7)
    def _(t):
        to = pl.multiple_of(8 * t, 8)

        def put(k, l, x):
            gv[k, l, pl.ds(to, 8), :] = x

        def take(k, l):
            return gv[k, l, pl.ds(to, 8), :]

        def keep(k, values):
            for l in range(NG + 1):
                put(k, l, values[l])

        advance(mv, 1 + 8 * t, HX - 1 + 8 * t, NG + 1, put, take, keep)

    ghosts(gv, 2, 0, WX + 1, HX - 1)

    @pl.loop(0, 6)
    def _(t):
        to = pl.multiple_of(8 * t, 8)

        def put(k, l, x):
            out[k, pl.ds(to, 8), 128 * l : 128 * l + 128] = x

        def take(k, l):
            return out[k, pl.ds(to, 8), 128 * l : 128 * l + 128]

        def keep(k, values):
            for l in range(NG):
                put(k, l, values[l])

        advance(gv, 1 + 8 * t, HX + 8 * t, NG, put, take, keep)


def on_device(
    state,
    diffuse,
    vertical,
    rows_we,
    rows_sn,
    fill_we,
    fill_sn,
    index_we,
    weight_we,
    index_sn,
    weight_sn,
    jump,
):
    f32 = jnp.float32
    count_x, count_y = lax.axis_size("nx"), lax.axis_size("ny")
    both = ("nx", "ny")
    vmem = pl.BlockSpec(memory_space=pltpu.VMEM)
    smem = pl.BlockSpec(memory_space=pltpu.SMEM)
    hbm = pl.BlockSpec(memory_space=pltpu.HBM)
    any_ = pl.BlockSpec(memory_space=pl.ANY)

    def shape(*dims):
        return jax.ShapeDtypeStruct(dims, f32)

    state, diffuse, vertical, rows_we, rows_sn, fill_we, fill_sn, index_we, weight_we, index_sn, weight_sn = (
        pltpu.with_memory_space_constraint(x, pltpu.HBM)
        for x in (
            state, diffuse, vertical, rows_we, rows_sn, fill_we, fill_sn, index_we, weight_we, index_sn, weight_sn
        )
    )
    y_low, y_high, chain_x, chain_y, colpack, interp = pl.pallas_call(
        pack_kernel,
        out_shape=(
            shape(WX, WY),
            shape(WX, WY),
            shape(FIRST, 16, 128),
            shape(1, 48, 128),
            shape(WX, 128),
            shape(8, WY),
        ),
        in_specs=[hbm] * 11,
        out_specs=(vmem,) * 6,
        scratch_shapes=[
            pltpu.VMEM((2, LV, WX, 128), f32),
            pltpu.VMEM((2, LV, WX, 128), f32),
            pltpu.VMEM((WX, WY), f32),
            pltpu.VMEM((3, 16, 128), f32),
            pltpu.VMEM((3, 16, 16), f32),
            pltpu.VMEM((2, 16, 128), f32),
            pltpu.VMEM((2, 16, 16), f32),
            pltpu.VMEM((WY,), jnp.int32),
            pltpu.VMEM((WY,), f32),
            pltpu.VMEM((WX,), jnp.int32),
            pltpu.VMEM((WX,), f32),
            pltpu.VMEM((128, 128), f32),
            pltpu.SemaphoreType.DMA((13,)),
        ],
        compiler_params=pltpu.CompilerParams(vmem_limit_bytes=16 << 20),
        name="pack",
    )(state, diffuse, vertical, rows_we, rows_sn, fill_we, fill_sn, index_we, weight_we, index_sn, weight_sn)

    pairs_a = [(i, i + 1) for i in range(1, count_x - 1, 2)]
    pairs_a += [(b, a) for a, b in pairs_a]
    pairs_b = [(i, i + 1) for i in range(0, count_x, 2)]
    pairs_b += [(b, a) for a, b in pairs_b]
    up = [(i, i + 1) for i in range(count_y - 1)]
    down = [(b, a) for a, b in up]
    rounds_x, rounds_y = rounds_of(count_x), rounds_of(count_y)

    def place(i, j):
        return i * count_y + j

    last_x, last_y = count_x - 1, count_y - 1
    set_x = [
        [place(i, (1 if i in (0, last_x) else 0) if side == 0 else (last_y - 1 if i in (0, last_x) else last_y))
         for i in range(count_x)]
        for side in range(2)
    ]
    set_y = [
        [place((1 if j in (1, last_y - 1) else 0) if side == 0 else (last_x - 1 if j in (1, last_y - 1) else last_x), j)
         for j in range(count_y)]
        for side in range(2)
    ]
    bring = []
    for i, step in ((0, 1), (last_x, -1)):
        for j, other in ((0, 1), (last_y, last_y - 1)):
            bring.append((place(i, other), place(i, j)))
            bring.append((place(i + step, other), place(i, other)))

    def along(sets, chain, masks):
        return [
            lax.ppermute(chain, both, [(own[n], own[n ^ m]) for own in sets for n in range(len(own))]) for m in masks
        ]

    along_x, along_y = functools.partial(along, set_x), functools.partial(along, set_y)

    def join(parts_x, parts_y, size_x, size_y, name):
        return pl.pallas_call(
            functools.partial(join_kernel, len(parts_x), len(parts_y)),
            out_shape=(
                shape(size_x, 16, 128),
                shape(size_y, 48, 128),
            ),
            in_specs=[vmem] * (len(parts_x) + len(parts_y)),
            out_specs=(vmem, vmem),
            compiler_params=pltpu.CompilerParams(vmem_limit_bytes=8 << 20),
            name=name,
        )(*parts_x, *parts_y)

    parts_x = [chain_x] + along_x(chain_x, rounds_x[0])
    parts_y = [chain_y] + along_y(chain_y, rounds_y[0])
    from_low = lax.ppermute(y_high, "ny", up)
    from_high = lax.ppermute(y_low, "ny", down)
    xa, xb = pl.pallas_call(
        border_kernel,
        out_shape=(shape(SENT, 128), shape(SENT, 128)),
        in_specs=[any_] * 2 + [hbm] * 3 + [vmem] * 3,
        out_specs=(vmem, vmem),
        scratch_shapes=[
            pltpu.VMEM((2, LV, 8, WY), f32),
            pltpu.VMEM((2, LV, 8, WY), f32),
            pltpu.VMEM((WX, WY), f32),
            pltpu.SemaphoreType.DMA((5,)),
        ],
        compiler_params=pltpu.CompilerParams(vmem_limit_bytes=8 << 20),
        name="border",
    )(parts_x[-1], parts_y[-1], state, diffuse, vertical, from_low, from_high, colpack)
    ra = lax.ppermute(xa, "nx", pairs_a)
    rb = lax.ppermute(xb, "nx", pairs_b)
    chain_x, chain_y = join(parts_x, parts_y, len(masks_of(rounds_x[:1])), len(masks_of(rounds_y[:1])), "join_first")
    parts_x = [chain_x] + along_x(chain_x, rounds_x[1])
    parts_y = [chain_y] + along_y(chain_y, rounds_y[1])
    chain_x, chain_y = join(parts_x, parts_y, len(masks_of(rounds_x[:2])), len(masks_of(rounds_y[:2])), "join_second")
    parts_x = [chain_x] + along_x(chain_x, rounds_x[2])
    parts_y = [chain_y] + along_y(chain_y, rounds_y[2])
    big = (LV, NG + 1, 72, 128)
    es, ed, ev, inv, pack = pl.pallas_call(
        prepare_kernel,
        out_shape=(shape(*big), shape(*big), shape(NG + 1, 72, 128), shape(*big), shape(64, 128)),
        in_specs=[hbm] * 3 + [vmem] * 5,
        out_specs=(vmem,) * 5,
        scratch_shapes=[
            pltpu.VMEM((2, 64, WY), f32),
            pltpu.VMEM((WX, WY), f32),
            pltpu.SemaphoreType.DMA((2 * NG + 1,)),
        ],
        compiler_params=pltpu.CompilerParams(vmem_limit_bytes=12 << 20),
        name="prepare",
    )(state, diffuse, vertical, ra, rb, from_low, from_high, colpack)
    have_x, have_y = masks_of(rounds_x[:2]), masks_of(rounds_y[:2])
    plan_x = [[m ^ h for h in have_x] for m in [0] + rounds_x[2]]
    plan_y = [[m ^ h for h in have_y] for m in [0] + rounds_y[2]]

    edges = pl.pallas_call(
        functools.partial(edge_kernel, count_x, count_y, plan_x, plan_y),
        out_shape=shape(256, 128),
        in_specs=[vmem] * (4 + len(parts_x) + len(parts_y)),
        out_specs=vmem,
        compiler_params=pltpu.CompilerParams(vmem_limit_bytes=8 << 20),
        name="edges",
    )(pack, from_low, from_high, interp, *parts_x, *parts_y)
    brought = lax.ppermute(edges, both, bring)

    return pl.pallas_call(
        functools.partial(main_kernel, count_x, count_y),
        out_shape=(shape(LV, WX, WY), shape(*big)),
        in_specs=[smem, hbm] + [vmem] * 9,
        out_specs=(vmem, vmem),
        scratch_shapes=[
            pltpu.VMEM((LV, NG + 1, 64, 128), f32),
            pltpu.VMEM((LV, NG + 1, 64, 128), f32),
            pltpu.VMEM((NG + 1, 48, 128), f32),
            pltpu.VMEM((64, 128), f32),
            pltpu.VMEM((2, 16, 128), f32),
            pltpu.SemaphoreType.DMA,
        ],
        input_output_aliases={4: 1},
        compiler_params=pltpu.CompilerParams(vmem_limit_bytes=20 << 20),
        name="steps",
    )(jump, fill_we, from_low, from_high, es, ed, ev, inv, pack, edges, brought)[0]


def solution(mesh):
    return jax.shard_map(
        on_device,
        mesh=mesh,
        in_specs=(
            P(None, "nx", "ny"),
            P(None, "nx", "ny"),
            P("nx", "ny"),
            P(None, None, None, "ny"),
            P(None, None, None, "nx"),
            P(None, None, "ny"),
            P(None, None, "nx"),
            P("ny"),
            P("ny"),
            P("nx"),
            P("nx"),
            P(),
        ),
        out_specs=P(None, "nx", "ny"),
        check_vma=False,
    )
```

```python
import functools

import jax
import jax.numpy as jnp
from jax import lax
from jax.experimental import pallas as pl
from jax.experimental.pallas import tpu as pltpu
from jax.sharding import PartitionSpec as P

LV = 16
WX = 48
WY = 384
NG = WY // 128
HX = 8
STATE_ROWS = 6
COEF_ROWS = 5
COEF_AT = LV * STATE_ROWS
VERT_AT = COEF_AT + LV * COEF_ROWS
XROWS = 184
CORNER_AT = NG * XROWS
FIRST = 10
SENT = CORNER_AT + 16 * NG


def rounds_of(count):
    if count == 32:
        return [[16], [4, 8, 12], [1, 2, 3]]
    if count == 16:
        return [[8], [2, 4, 6], [1]]
    return [[2], [1], []]


def masks_of(rounds):
    have = [0]
    for masks in rounds:
        have = [m ^ h for m in [0] + masks for h in have]
    return have


def pack_kernel(
    state_hbm, diffuse_hbm, vertical_hbm, rows_we_hbm, rows_sn_hbm, fill_we_hbm, fill_sn_hbm,
    index_we_hbm, weight_we_hbm, index_sn_hbm, weight_sn_hbm,
    y_low, y_high, chain_x, chain_y, colpack, interp,
    state, diffuse, vertical, rows_we, rows_sn, fill_we, fill_sn, index_we, weight_we, index_sn, weight_sn,
    square, sem,
):
    nx, ny = lax.axis_index("nx"), lax.axis_index("ny")
    side_x = jnp.where(ny < lax.axis_size("ny") // 2, 0, 1)
    side_y = jnp.where(nx < lax.axis_size("nx") // 2, 0, 1)
    pairs = [
        (rows_we_hbm.at[:, side_y], rows_we),
        (rows_sn_hbm.at[:, side_x], rows_sn),
        (fill_we_hbm, fill_we),
        (fill_sn_hbm, fill_sn),
        (index_we_hbm, index_we),
        (weight_we_hbm, weight_we),
        (index_sn_hbm, index_sn),
        (weight_sn_hbm, weight_sn),
        (vertical_hbm, vertical),
    ]
    for src, dst in ((state_hbm, state), (diffuse_hbm, diffuse)):
        for at, group in enumerate((0, NG - 1)):
            pairs.append((src.at[:, :, pl.ds(128 * group, 128)], dst.at[at]))
    copies = [pltpu.make_async_copy(src, dst, sem.at[n]) for n, (src, dst) in enumerate(pairs)]
    for copy in copies:
        copy.start()
    lane = lax.broadcasted_iota(jnp.int32, (128, 128), 1)
    square[...] = jnp.zeros((128, 128), jnp.float32)
    interp[...] = jnp.zeros((8, WY), jnp.float32)
    for copy in copies[:8]:
        copy.wait()
    for step in range(3):
        chain_y[0, 16 * step : 16 * step + 16, :] = rows_we[step]
        square[16 * step : 16 * step + 16, 0:16] = rows_sn[step]
    chain_x[...] = jnp.zeros((FIRST, 16, 128), jnp.float32)
    chain_x[0] = square[...].T[0:16]
    square[0:48, :] = jnp.zeros((48, 128), jnp.float32)
    square[96:112, 0:16] = fill_sn[0]
    square[112:128, 0:16] = fill_sn[1]
    square[64:65, 0:WX] = index_sn[...].astype(jnp.float32).reshape(1, WX)
    square[65:66, 0:WX] = weight_sn[...].reshape(1, WX)
    whole = square[...]
    row = lax.broadcasted_iota(jnp.int32, (128, 128), 0)
    whole = jnp.where((lane < 8) | (row < 96), whole, pltpu.roll(whole, 32, 1))
    colpack[...] = whole.T[0:WX]
    interp[0:1, :] = index_we[...].astype(jnp.float32).reshape(1, WY)
    interp[1:2, :] = weight_we[...].reshape(1, WY)
    square[0:16, :] = fill_we[0]
    square[16:32, :] = fill_we[1]
    for copy in copies[8:]:
        copy.wait()

    lane = lax.broadcasted_iota(jnp.int32, (WX, 128), 1)
    row = lax.broadcasted_iota(jnp.int32, (WX, 128), 0)
    for at, (ref, group, first) in enumerate(((y_low, 0, 0), (y_high, NG - 1, 120))):
        lanes = slice(128 * group, 128 * group + 128)
        for which, field in enumerate((state, diffuse)):
            total = jnp.zeros((WX, 128), jnp.float32)
            for k in range(LV):
                part = pltpu.roll(field[at, k], (8 * k - first) % 128, 1)
                total = jnp.where((lane >= 8 * k) & (lane < 8 * k + 8), part, total)
            ref[:, 128 * which : 128 * which + 128] = total
        last = jnp.where(lane < 8, pltpu.roll(vertical[:, lanes], (-first) % 128, 1), 0.0)
        last = jnp.where(
            (lane >= 8) & (lane < 16), pltpu.roll(square[0:WX, :], (8 - first) % 128, 1), last
        )
        pair = jnp.where(row == 0, interp[0:1, lanes], interp[1:2, lanes])
        last = jnp.where(
            (lane >= 16) & (lane < 24) & (row < 2), pltpu.roll(pair, (16 - first) % 128, 1), last
        )
        ref[:, 256:384] = last


def border_kernel(
    after_x, after_y, state_hbm, diffuse_hbm, vertical_hbm, from_low, from_high, colpack,
    xa, xb, state, diffuse, vertical, sem,
):
    copies = [pltpu.make_async_copy(vertical_hbm, vertical, sem.at[4])]
    for n, (src, dst) in enumerate(((state_hbm, state), (diffuse_hbm, diffuse))):
        for side in range(2):
            copies.append(
                pltpu.make_async_copy(src.at[:, pl.ds(40 * side, 8), :], dst.at[side], sem.at[2 * n + side])
            )
    for copy in copies:
        copy.start()
    odd = lax.axis_index("nx") % 2 == 1
    clear = lax.broadcasted_iota(jnp.int32, (8, 128), 1) < 64
    for copy in copies:
        copy.wait()

    def rows(ref, side):
        at = 8 - STATE_ROWS if side else 0
        bt = 8 - COEF_ROWS if side else 0
        for l in range(NG):
            lanes = slice(128 * l, 128 * l + 128)
            base = XROWS * l
            for k in range(LV):
                n = base + k * STATE_ROWS
                ref[n : n + STATE_ROWS, :] = state[side, k, at : at + STATE_ROWS, lanes]
                n = base + COEF_AT + k * COEF_ROWS
                ref[n : n + COEF_ROWS, :] = diffuse[side, k, bt : bt + COEF_ROWS, lanes]
            n = base + VERT_AT
            ref[n : n + COEF_ROWS, :] = vertical[40 * side + bt : 40 * side + bt + COEF_ROWS, lanes]
            ref[n + COEF_ROWS : base + XROWS, :] = jnp.zeros((XROWS - VERT_AT - COEF_ROWS, 128), jnp.float32)
        for which, strips in enumerate((from_low, from_high)):
            for l in range(NG):
                part = strips[40 * side : 40 * side + 8, 128 * l : 128 * l + 128]
                if which == 0 and l == NG - 1:
                    part = jnp.where(clear, part, colpack[40 * side : 40 * side + 8, :])
                n = CORNER_AT + 8 * (NG * which + l)
                ref[n : n + 8, :] = part

    @pl.when(odd)
    def _():
        rows(xa, 1)
        rows(xb, 0)

    @pl.when(jnp.logical_not(odd))
    def _():
        rows(xa, 0)
        rows(xb, 1)


def join_kernel(count_x, count_y, *refs):
    ins, (out_x, out_y) = refs[:-2], refs[-2:]
    for out, parts in ((out_x, ins[:count_x]), (out_y, ins[count_x : count_x + count_y])):
        at = 0
        for part in parts:
            size = 1 if part.shape[0] == FIRST else part.shape[0]
            out[at : at + size] = part[0:size]
            at += size


def edge_kernel(count_x, count_y, plan_x, plan_y, pack, from_low, from_high, interp, *refs):
    chain_x, refs = refs[: len(plan_x)], refs[len(plan_x) :]
    chain_y, refs = refs[: len(plan_y)], refs[len(plan_y) :]
    (edges,) = refs
    nx, ny = lax.axis_index("nx"), lax.axis_index("ny")
    border_x = (nx == 0) | (nx == count_x - 1)
    border_y = (ny == 0) | (ny == count_y - 1)
    inner_x = (nx == 1) | (nx == count_x - 2)
    inner_y = (ny == 1) | (ny == count_y - 2)

    @pl.when((border_x & jnp.logical_not(inner_y)) | (inner_x & inner_y))
    def _():
        lane1 = lax.broadcasted_iota(jnp.int32, (1, 128), 1)
        for l in range(NG + 1):
            got = []
            for item in range(2):
                if l < NG:
                    got.append(interp[item : item + 1, 128 * l : 128 * l + 128])
                else:
                    got.append(
                        jnp.where(
                            lane1 < 64,
                            pltpu.roll(from_high[0:8, 256:384], 112, 1)[item : item + 1],
                            pltpu.roll(from_low[0:8, 256:384], 104, 1)[item : item + 1],
                        )
                    )
            index = jnp.broadcast_to(got[0], (48, 128)).astype(jnp.int32)
            ends = []
            for offset in range(2):
                at = index + offset
                block, inside = at >> 7, at & 127
                total = jnp.zeros((48, 128), jnp.float32)
                for ref, masks in zip(chain_y, plan_y, strict=True):
                    for piece, mask in enumerate(masks):
                        value = jnp.take_along_axis(ref[piece], inside, axis=1, mode="promise_in_bounds")
                        total = jnp.where(block == (ny ^ mask), value, total)
                ends.append(total)
            edges[64 + 48 * l : 112 + 48 * l, :] = (1.0 - got[1]) * ends[0] + got[1] * ends[1]

    @pl.when((border_y & jnp.logical_not(border_x)) | (border_x & inner_y))
    def _():
        index = pack[:, 64:65].astype(jnp.int32)
        weight = pack[:, 65:66]
        total = jnp.zeros((64, 128), jnp.float32)
        for ref, masks in zip(chain_x, plan_x, strict=True):
            size = 16 * len(masks)
            at = lax.broadcasted_iota(jnp.int32, (1, size), 1)
            ids = at & 15
            for piece, mask in enumerate(masks):
                ids = jnp.where(at >> 4 == piece, ids + 16 * (nx ^ mask), ids)
            spread = jnp.where(ids == index, 1.0 - weight, 0.0) + jnp.where(ids == index + 1, weight, 0.0)
            total += jnp.dot(
                spread,
                ref[...].reshape(size, 128),
                preferred_element_type=jnp.float32,
                precision=lax.Precision.HIGHEST,
            )
        edges[0:64, :] = total


def prepare_kernel(
    state, diffuse, vertical_hbm, ra, rb, from_low, from_high, colpack, es, ed, ev, inv, pack, strip, vertical, sem
):
    nx = lax.axis_index("nx")
    copies = []
    for which, (src, dst) in enumerate(((state, es), (diffuse, ed))):
        for l in range(NG):
            copy = pltpu.make_async_copy(
                src.at[:, :, pl.ds(128 * l, 128)], dst.at[:, l, pl.ds(HX, WX), :], sem.at[NG * which + l]
            )
            copy.start()
            copies.append(copy)
    first_copies = [
        pltpu.make_async_copy(vertical_hbm, vertical, sem.at[2 * NG]),
    ]
    for copy in first_copies:
        copy.start()
    odd = nx % 2 == 1
    lane64 = lax.broadcasted_iota(jnp.int32, (64, 128), 1)

    def beyond(at, size, l):
        a, b = ra[XROWS * l + at : XROWS * l + at + size, :], rb[XROWS * l + at : XROWS * l + at + size, :]
        return jnp.where(odd, b, a), jnp.where(odd, a, b)

    for copy in first_copies:
        copy.wait()
    for l in range(NG):
        for k in range(LV):
            low, high = beyond(k * STATE_ROWS, STATE_ROWS, l)
            es[k, l, HX - STATE_ROWS : HX, :] = low
            es[k, l, HX + WX : HX + WX + STATE_ROWS, :] = high
            low, high = beyond(COEF_AT + k * COEF_ROWS, COEF_ROWS, l)
            ed[k, l, HX - COEF_ROWS : HX, :] = low
            ed[k, l, HX + WX : HX + WX + COEF_ROWS, :] = high
        low, high = beyond(VERT_AT, COEF_ROWS, l)
        ev[l, HX - COEF_ROWS : HX, :] = low
        ev[l, HX + WX : HX + WX + COEF_ROWS, :] = high
        ev[l, HX : HX + WX, :] = vertical[:, 128 * l : 128 * l + 128]

    def corner(side, l):
        n = CORNER_AT + 8 * (NG * side + l)
        a, b = ra[n : n + 8, :], rb[n : n + 8, :]
        return jnp.where(odd, b, a), jnp.where(odd, a, b)

    for side, ref in enumerate((from_low, from_high)):
        strip[side, HX : HX + WX, :] = ref[...]
        for l in range(NG):
            low, high = corner(side, l)
            strip[side, 0:HX, 128 * l : 128 * l + 128] = low
            strip[side, HX + WX : 64, 128 * l : 128 * l + 128] = high
    low, high = corner(0, NG - 1)
    pack[0:HX, :] = low
    pack[HX : HX + WX, :] = colpack[...]
    pack[HX + WX : 64, :] = high
    for which, dst in enumerate((es, ed)):
        lanes = slice(128 * which, 128 * which + 128)
        for k in range(LV):
            dst[k, NG, 0:64, :] = jnp.where(
                lane64 < 64,
                pltpu.roll(strip[1, :, lanes], (-8 * k) % 128, 1),
                pltpu.roll(strip[0, :, lanes], (120 - 8 * k) % 128, 1),
            )
    ev[NG, 0:64, :] = jnp.where(
        lane64 < 64, strip[1, :, 256:384], pltpu.roll(strip[0, :, 256:384], 120, 1)
    )


    @pl.loop(0, 8, unroll=True)
    def _(t):
        rows = pl.ds(pl.multiple_of(8 * t, 8), 8)
        for l in range(NG + 1):
            g = ev[l, rows, :]
            inverse = 1.0 / (1.0 + g)
            inv[0, l, rows, :] = inverse
            for k in range(1, LV):
                diagonal = 1.0 + (g if k == LV - 1 else 2.0 * g)
                inverse = 1.0 / (diagonal - g * (g * inverse))
                inv[k, l, rows, :] = inverse

    for copy in copies:
        copy.wait()


def main_kernel(
    count_x, count_y, jump, fill_we_hbm, from_low, from_high, es_in, ed, ev, inv, pack, edges, brought_ref,
    out, es, mv, gv, ey, ex, fill_we, sem,
):
    dx, dy = jump[0], jump[1]
    nx, ny = lax.axis_index("nx"), lax.axis_index("ny")
    lane = lax.broadcasted_iota(jnp.int32, (8, 128), 1)
    fetch = pltpu.make_async_copy(fill_we_hbm, fill_we, sem)
    fetch.start()
    west, east = nx == 0, nx == count_x - 1
    south, north = ny == 0, ny == count_y - 1

    @pl.when(west | east)
    def _():
        brought = (ny == 1) | (ny == count_y - 2)
        for l in range(NG + 1):
            rows = slice(64 + 48 * l, 112 + 48 * l)
            ey[l] = jnp.where(brought, brought_ref[rows, :], edges[rows, :])

    @pl.when(south | north)
    def _():
        ex[...] = jnp.where(west | east, brought_ref[0:64, :], edges[0:64, :])

    def ghosts(field, step, row_low, row_high, shift):
        @pl.when(west)
        def _():
            for k in range(LV):
                for l in range(NG + 1):
                    field[k, l, row_low : row_low + 1, :] = ey[l, 16 * step + k : 16 * step + k + 1, :]

        @pl.when(east)
        def _():
            for k in range(LV):
                for l in range(NG + 1):
                    field[k, l, row_high : row_high + 1, :] = ey[l, 16 * step + k : 16 * step + k + 1, :]

        @pl.when(south | north)
        def _():
            at = jnp.where(south, 127, 0)
            lanes = lax.broadcasted_iota(jnp.int32, (56, 128), 1)
            for k in range(LV):
                col = ex[shift : shift + 56, 16 * step + k : 16 * step + k + 1]
                field[k, NG, 0:56, :] = jnp.where(lanes == at, col, field[k, NG, 0:56, :])

    def ghost_tail(step):
        @pl.when(south | north)
        def _():
            at = jnp.where(south, 127, 0)
            for k in range(LV):
                col = ex[56:64, 16 * step + k : 16 * step + k + 1]
                es[k, NG, 56:64, :] = jnp.where(lane == at, col, es[k, NG, 56:64, :])

    ghosts(es, 0, HX - 1, HX + WX, 0)
    ghost_tail(0)

    def sideways(c):
        lefts = [pltpu.roll(x, 1, 1) for x in c]
        rights = [pltpu.roll(x, 127, 1) for x in c]
        n = len(c)
        left = [jnp.where(lane == 0, lefts[l - 1], lefts[l]) for l in range(n)]
        right = [jnp.where(lane == 127, rights[(l + 1) % n], rights[l]) for l in range(n)]
        return left, right

    def advance(field, at, coef_at, groups, write_source, read_source, write):
        g = [ev[l, pl.ds(coef_at, 8), :] for l in range(groups)]
        source = [None] * groups
        for k in range(LV):
            c = [field[k, l, pl.ds(at, 8), :] for l in range(NG + 1)]
            left, right = sideways(c)
            for l in range(groups):
                lap = (
                    field[k, l, pl.ds(at + 1, 8), :]
                    + field[k, l, pl.ds(at - 1, 8), :]
                    + right[l]
                    + left[l]
                    - 4.0 * c[l]
                )
                explicit = c[l] + ed[k, l, pl.ds(coef_at, 8), :] * lap
                if k > 0:
                    explicit = explicit + g[l] * source[l]
                source[l] = explicit * inv[k, l, pl.ds(coef_at, 8), :]
                if k < LV - 1:
                    write_source(k, l, source[l])
        value = source
        write(LV - 1, value)
        for k in range(LV - 2, -1, -1):
            value = [
                read_source(k, l) + (g[l] * inv[k, l, pl.ds(coef_at, 8), :]) * value[l] for l in range(groups)
            ]
            write(k, value)

    turn = (128 - 3 * dy) % 128

    @pl.loop(0, 7, unroll=True)
    def _(t):
        to = pl.multiple_of(8 * t, 8)

        def put(k, l, x):
            mv[k, l, pl.ds(to, 8), :] = x

        def take(k, l):
            return mv[k, l, pl.ds(to, 8), :]

        def moved(k, values):
            turned = [pltpu.roll(x, turn, 1) for x in values]
            for l in range(NG + 1):
                x = jnp.where(lane >= 128 - 3 * dy, turned[(l + 1) % (NG + 1)], turned[l])
                put(k, l, jnp.where(lane < -3 * dy, turned[l - 1], x))

        at = HX - 2 + 3 * dx + 8 * t
        advance(es, at, at, NG + 1, put, take, moved)

    @pl.when((south & (dy < 0)) | (north & (dy > 0)))
    def _():
        row = lax.broadcasted_iota(jnp.int32, (56, 128), 0)
        cell = (((row + 4) * 21846) >> 16) - 2 + dx
        lanes = lax.broadcasted_iota(jnp.int32, (56, 128), 1)
        total = jnp.zeros((56, 128), jnp.float32)
        for q in range(-2, 18):
            r = q + 8 if q < 0 else (q + HX if q < 8 else q + 40)
            total = jnp.where(cell == q, pack[r : r + 1, :], total)

        for is_side, side, l, first in ((south, 0, 0, 0), (north, 1, NG - 1, 125)):

            @pl.when(is_side)
            def _():
                inside = (lanes >= first) & (lanes < first + 3)
                for k in range(LV):
                    n = 96 + 16 * side + k
                    mv[k, l, 0:56, :] = jnp.where(inside, total[:, n : n + 1], mv[k, l, 0:56, :])

    fetch.wait()

    @pl.when((west & (dx < 0)) | (east & (dx > 0)))
    def _():
        lane16 = lax.broadcasted_iota(jnp.int32, (16, 128), 1)
        for is_side, side, first in ((west, 0, 2), (east, 1, 47)):

            @pl.when(is_side)
            def _():
                own = fill_we[side]
                ring = jnp.where(
                    lane16 < 64,
                    pltpu.roll(from_high[16 * side : 16 * side + 16, 256:384], 120, 1),
                    pltpu.roll(from_low[16 * side : 16 * side + 16, 256:384], 112, 1),
                )
                for l in range(NG + 1):
                    column = lane16 + 128 * l
                    if l == NG:
                        column = jnp.where(lane16 < 64, column, lane16 - 128)
                    cell = (((column + 384) * 21846) >> 16) - 128 + dy
                    cell = jnp.clip(cell, -128 * ny, 128 * (count_y - ny) - 1)
                    inside = cell & 127
                    a = jnp.take_along_axis(own, inside, axis=1, mode="promise_in_bounds")
                    b = jnp.take_along_axis(ring, inside, axis=1, mode="promise_in_bounds")
                    ey[l, 0:16, :] = jnp.where((cell >= 0) & (cell < 128), a, b)
                    for k in range(LV):
                        mv[k, l, first : first + 3, :] = jnp.broadcast_to(ey[l, k : k + 1, :], (3, 128))

    ghosts(mv, 1, 1, WX + 2, HX - 2)

    @pl.loop(0, 7, unroll=True)
    def _(t):
        to = pl.multiple_of(8 * t, 8)

        def put(k, l, x):
            gv[k, l, pl.ds(to, 8), :] = x

        def take(k, l):
            return gv[k, l, pl.ds(to, 8), :]

        def keep(k, values):
            for l in range(NG + 1):
                put(k, l, values[l])

        advance(mv, 1 + 8 * t, HX - 1 + 8 * t, NG + 1, put, take, keep)

    ghosts(gv, 2, 0, WX + 1, HX - 1)

    @pl.loop(0, 6, unroll=True)
    def _(t):
        to = pl.multiple_of(8 * t, 8)

        def put(k, l, x):
            out[k, pl.ds(to, 8), 128 * l : 128 * l + 128] = x

        def take(k, l):
            return out[k, pl.ds(to, 8), 128 * l : 128 * l + 128]

        def keep(k, values):
            for l in range(NG):
                put(k, l, values[l])

        advance(gv, 1 + 8 * t, HX + 8 * t, NG, put, take, keep)


def on_device(
    state,
    diffuse,
    vertical,
    rows_we,
    rows_sn,
    fill_we,
    fill_sn,
    index_we,
    weight_we,
    index_sn,
    weight_sn,
    jump,
):
    f32 = jnp.float32
    count_x, count_y = lax.axis_size("nx"), lax.axis_size("ny")
    both = ("nx", "ny")
    vmem = pl.BlockSpec(memory_space=pltpu.VMEM)
    smem = pl.BlockSpec(memory_space=pltpu.SMEM)
    hbm = pl.BlockSpec(memory_space=pltpu.HBM)
    any_ = pl.BlockSpec(memory_space=pl.ANY)

    def shape(*dims):
        return jax.ShapeDtypeStruct(dims, f32)

    state, diffuse, vertical, rows_we, rows_sn, fill_we, fill_sn, index_we, weight_we, index_sn, weight_sn = (
        pltpu.with_memory_space_constraint(x, pltpu.HBM)
        for x in (
            state, diffuse, vertical, rows_we, rows_sn, fill_we, fill_sn, index_we, weight_we, index_sn, weight_sn
        )
    )
    y_low, y_high, chain_x, chain_y, colpack, interp = pl.pallas_call(
        pack_kernel,
        out_shape=(
            shape(WX, WY),
            shape(WX, WY),
            shape(FIRST, 16, 128),
            shape(1, 48, 128),
            shape(WX, 128),
            shape(8, WY),
        ),
        in_specs=[hbm] * 11,
        out_specs=(vmem,) * 6,
        scratch_shapes=[
            pltpu.VMEM((2, LV, WX, 128), f32),
            pltpu.VMEM((2, LV, WX, 128), f32),
            pltpu.VMEM((WX, WY), f32),
            pltpu.VMEM((3, 16, 128), f32),
            pltpu.VMEM((3, 16, 16), f32),
            pltpu.VMEM((2, 16, 128), f32),
            pltpu.VMEM((2, 16, 16), f32),
            pltpu.VMEM((WY,), jnp.int32),
            pltpu.VMEM((WY,), f32),
            pltpu.VMEM((WX,), jnp.int32),
            pltpu.VMEM((WX,), f32),
            pltpu.VMEM((128, 128), f32),
            pltpu.SemaphoreType.DMA((13,)),
        ],
        compiler_params=pltpu.CompilerParams(vmem_limit_bytes=16 << 20),
        name="pack",
    )(state, diffuse, vertical, rows_we, rows_sn, fill_we, fill_sn, index_we, weight_we, index_sn, weight_sn)

    pairs_a = [(i, i + 1) for i in range(1, count_x - 1, 2)]
    pairs_a += [(b, a) for a, b in pairs_a]
    pairs_b = [(i, i + 1) for i in range(0, count_x, 2)]
    pairs_b += [(b, a) for a, b in pairs_b]
    up = [(i, i + 1) for i in range(count_y - 1)]
    down = [(b, a) for a, b in up]
    rounds_x, rounds_y = rounds_of(count_x), rounds_of(count_y)

    def place(i, j):
        return i * count_y + j

    last_x, last_y = count_x - 1, count_y - 1
    set_x = [
        [place(i, (1 if i in (0, last_x) else 0) if side == 0 else (last_y - 1 if i in (0, last_x) else last_y))
         for i in range(count_x)]
        for side in range(2)
    ]
    set_y = [
        [place((1 if j in (1, last_y - 1) else 0) if side == 0 else (last_x - 1 if j in (1, last_y - 1) else last_x), j)
         for j in range(count_y)]
        for side in range(2)
    ]
    bring = []
    for i, step in ((0, 1), (last_x, -1)):
        for j, other in ((0, 1), (last_y, last_y - 1)):
            bring.append((place(i, other), place(i, j)))
            bring.append((place(i + step, other), place(i, other)))

    def along(sets, chain, masks):
        return [
            lax.ppermute(chain, both, [(own[n], own[n ^ m]) for own in sets for n in range(len(own))]) for m in masks
        ]

    along_x, along_y = functools.partial(along, set_x), functools.partial(along, set_y)

    def join(parts_x, parts_y, size_x, size_y, name):
        return pl.pallas_call(
            functools.partial(join_kernel, len(parts_x), len(parts_y)),
            out_shape=(
                shape(size_x, 16, 128),
                shape(size_y, 48, 128),
            ),
            in_specs=[vmem] * (len(parts_x) + len(parts_y)),
            out_specs=(vmem, vmem),
            compiler_params=pltpu.CompilerParams(vmem_limit_bytes=8 << 20),
            name=name,
        )(*parts_x, *parts_y)

    parts_x = [chain_x] + along_x(chain_x, rounds_x[0])
    parts_y = [chain_y] + along_y(chain_y, rounds_y[0])
    from_low = lax.ppermute(y_high, "ny", up)
    from_high = lax.ppermute(y_low, "ny", down)
    xa, xb = pl.pallas_call(
        border_kernel,
        out_shape=(shape(SENT, 128), shape(SENT, 128)),
        in_specs=[any_] * 2 + [hbm] * 3 + [vmem] * 3,
        out_specs=(vmem, vmem),
        scratch_shapes=[
            pltpu.VMEM((2, LV, 8, WY), f32),
            pltpu.VMEM((2, LV, 8, WY), f32),
            pltpu.VMEM((WX, WY), f32),
            pltpu.SemaphoreType.DMA((5,)),
        ],
        compiler_params=pltpu.CompilerParams(vmem_limit_bytes=8 << 20),
        name="border",
    )(parts_x[-1], parts_y[-1], state, diffuse, vertical, from_low, from_high, colpack)
    ra = lax.ppermute(xa, "nx", pairs_a)
    rb = lax.ppermute(xb, "nx", pairs_b)
    chain_x, chain_y = join(parts_x, parts_y, len(masks_of(rounds_x[:1])), len(masks_of(rounds_y[:1])), "join_first")
    parts_x = [chain_x] + along_x(chain_x, rounds_x[1])
    parts_y = [chain_y] + along_y(chain_y, rounds_y[1])
    chain_x, chain_y = join(parts_x, parts_y, len(masks_of(rounds_x[:2])), len(masks_of(rounds_y[:2])), "join_second")
    parts_x = [chain_x] + along_x(chain_x, rounds_x[2])
    parts_y = [chain_y] + along_y(chain_y, rounds_y[2])
    big = (LV, NG + 1, 72, 128)
    es, ed, ev, inv, pack = pl.pallas_call(
        prepare_kernel,
        out_shape=(shape(*big), shape(*big), shape(NG + 1, 72, 128), shape(*big), shape(64, 128)),
        in_specs=[hbm] * 3 + [vmem] * 5,
        out_specs=(vmem,) * 5,
        scratch_shapes=[
            pltpu.VMEM((2, 64, WY), f32),
            pltpu.VMEM((WX, WY), f32),
            pltpu.SemaphoreType.DMA((2 * NG + 1,)),
        ],
        compiler_params=pltpu.CompilerParams(vmem_limit_bytes=12 << 20),
        name="prepare",
    )(state, diffuse, vertical, ra, rb, from_low, from_high, colpack)
    have_x, have_y = masks_of(rounds_x[:2]), masks_of(rounds_y[:2])
    plan_x = [[m ^ h for h in have_x] for m in [0] + rounds_x[2]]
    plan_y = [[m ^ h for h in have_y] for m in [0] + rounds_y[2]]

    edges = pl.pallas_call(
        functools.partial(edge_kernel, count_x, count_y, plan_x, plan_y),
        out_shape=shape(256, 128),
        in_specs=[vmem] * (4 + len(parts_x) + len(parts_y)),
        out_specs=vmem,
        compiler_params=pltpu.CompilerParams(vmem_limit_bytes=8 << 20),
        name="edges",
    )(pack, from_low, from_high, interp, *parts_x, *parts_y)
    brought = lax.ppermute(edges, both, bring)

    return pl.pallas_call(
        functools.partial(main_kernel, count_x, count_y),
        out_shape=(shape(LV, WX, WY), shape(*big)),
        in_specs=[smem, hbm] + [vmem] * 9,
        out_specs=(vmem, vmem),
        scratch_shapes=[
            pltpu.VMEM((LV, NG + 1, 64, 128), f32),
            pltpu.VMEM((LV, NG + 1, 64, 128), f32),
            pltpu.VMEM((NG + 1, 48, 128), f32),
            pltpu.VMEM((64, 128), f32),
            pltpu.VMEM((2, 16, 128), f32),
            pltpu.SemaphoreType.DMA,
        ],
        input_output_aliases={4: 1},
        compiler_params=pltpu.CompilerParams(vmem_limit_bytes=20 << 20),
        name="steps",
    )(jump, fill_we, from_low, from_high, es, ed, ev, inv, pack, edges, brought)[0]


def solution(mesh):
    return jax.shard_map(
        on_device,
        mesh=mesh,
        in_specs=(
            P(None, "nx", "ny"),
            P(None, "nx", "ny"),
            P("nx", "ny"),
            P(None, None, None, "ny"),
            P(None, None, None, "nx"),
            P(None, None, "ny"),
            P(None, None, "nx"),
            P("ny"),
            P("ny"),
            P("nx"),
            P("nx"),
            P(),
        ),
        out_specs=P(None, "nx", "ny"),
        check_vma=False,
    )
```

```python
import functools

import jax
import jax.numpy as jnp
from jax import lax
from jax.experimental import pallas as pl
from jax.experimental.pallas import tpu as pltpu
from jax.sharding import PartitionSpec as P

LV = 16
WX = 48
WY = 384
NG = WY // 128
HX = 8
STATE_ROWS = 6
COEF_ROWS = 5
COEF_AT = LV * STATE_ROWS
VERT_AT = COEF_AT + LV * COEF_ROWS
XROWS = 184
CORNER_AT = NG * XROWS
FIRST = 10
SENT = CORNER_AT + 16 * NG


def rounds_of(count):
    if count == 32:
        return [[16], [4, 8, 12], [1, 2, 3]]
    if count == 16:
        return [[8], [2, 4, 6], [1]]
    return [[2], [1], []]


def masks_of(rounds):
    have = [0]
    for masks in rounds:
        have = [m ^ h for m in [0] + masks for h in have]
    return have


def pack_kernel(
    state_hbm, diffuse_hbm, vertical_hbm, rows_we_hbm, rows_sn_hbm, fill_we_hbm, fill_sn_hbm,
    index_we_hbm, weight_we_hbm, index_sn_hbm, weight_sn_hbm,
    y_low, y_high, chain_x, chain_y, colpack, interp,
    state, diffuse, vertical, rows_we, rows_sn, fill_we, fill_sn, index_we, weight_we, index_sn, weight_sn,
    square, sem,
):
    nx, ny = lax.axis_index("nx"), lax.axis_index("ny")
    side_x = jnp.where(ny < lax.axis_size("ny") // 2, 0, 1)
    side_y = jnp.where(nx < lax.axis_size("nx") // 2, 0, 1)
    pairs = [
        (rows_we_hbm.at[:, side_y], rows_we),
        (rows_sn_hbm.at[:, side_x], rows_sn),
        (fill_we_hbm, fill_we),
        (fill_sn_hbm, fill_sn),
        (index_we_hbm, index_we),
        (weight_we_hbm, weight_we),
        (index_sn_hbm, index_sn),
        (weight_sn_hbm, weight_sn),
        (vertical_hbm, vertical),
    ]
    for src, dst in ((state_hbm, state), (diffuse_hbm, diffuse)):
        for at, group in enumerate((0, NG - 1)):
            pairs.append((src.at[:, :, pl.ds(128 * group, 128)], dst.at[at]))
    copies = [pltpu.make_async_copy(src, dst, sem.at[n]) for n, (src, dst) in enumerate(pairs)]
    for copy in copies:
        copy.start()
    lane = lax.broadcasted_iota(jnp.int32, (128, 128), 1)
    square[...] = jnp.zeros((128, 128), jnp.float32)
    interp[...] = jnp.zeros((8, WY), jnp.float32)
    for copy in copies[:8]:
        copy.wait()
    for step in range(3):
        chain_y[0, 16 * step : 16 * step + 16, :] = rows_we[step]
        square[16 * step : 16 * step + 16, 0:16] = rows_sn[step]
    chain_x[...] = jnp.zeros((FIRST, 16, 128), jnp.float32)
    chain_x[0] = square[...].T[0:16]
    square[0:48, :] = jnp.zeros((48, 128), jnp.float32)
    square[96:112, 0:16] = fill_sn[0]
    square[112:128, 0:16] = fill_sn[1]
    square[64:65, 0:WX] = index_sn[...].astype(jnp.float32).reshape(1, WX)
    square[65:66, 0:WX] = weight_sn[...].reshape(1, WX)
    whole = square[...]
    row = lax.broadcasted_iota(jnp.int32, (128, 128), 0)
    whole = jnp.where((lane < 8) | (row < 96), whole, pltpu.roll(whole, 32, 1))
    colpack[...] = whole.T[0:WX]
    interp[0:1, :] = index_we[...].astype(jnp.float32).reshape(1, WY)
    interp[1:2, :] = weight_we[...].reshape(1, WY)
    square[0:16, :] = fill_we[0]
    square[16:32, :] = fill_we[1]
    for copy in copies[8:]:
        copy.wait()

    lane = lax.broadcasted_iota(jnp.int32, (WX, 128), 1)
    row = lax.broadcasted_iota(jnp.int32, (WX, 128), 0)
    for at, (ref, group, first) in enumerate(((y_low, 0, 0), (y_high, NG - 1, 120))):
        lanes = slice(128 * group, 128 * group + 128)
        for which, field in enumerate((state, diffuse)):
            total = jnp.zeros((WX, 128), jnp.float32)
            for k in range(LV):
                part = pltpu.roll(field[at, k], (8 * k - first) % 128, 1)
                total = jnp.where((lane >= 8 * k) & (lane < 8 * k + 8), part, total)
            ref[:, 128 * which : 128 * which + 128] = total
        last = jnp.where(lane < 8, pltpu.roll(vertical[:, lanes], (-first) % 128, 1), 0.0)
        last = jnp.where(
            (lane >= 8) & (lane < 16), pltpu.roll(square[0:WX, :], (8 - first) % 128, 1), last
        )
        pair = jnp.where(row == 0, interp[0:1, lanes], interp[1:2, lanes])
        last = jnp.where(
            (lane >= 16) & (lane < 24) & (row < 2), pltpu.roll(pair, (16 - first) % 128, 1), last
        )
        ref[:, 256:384] = last


def border_kernel(
    after_x, after_y, state_hbm, diffuse_hbm, vertical_hbm, from_low, from_high, colpack,
    xa, xb, state, diffuse, vertical, sem,
):
    copies = [pltpu.make_async_copy(vertical_hbm, vertical, sem.at[4])]
    for n, (src, dst) in enumerate(((state_hbm, state), (diffuse_hbm, diffuse))):
        for side in range(2):
            copies.append(
                pltpu.make_async_copy(src.at[:, pl.ds(40 * side, 8), :], dst.at[side], sem.at[2 * n + side])
            )
    for copy in copies:
        copy.start()
    odd = lax.axis_index("nx") % 2 == 1
    clear = lax.broadcasted_iota(jnp.int32, (8, 128), 1) < 64
    for copy in copies:
        copy.wait()

    def rows(ref, side):
        at = 8 - STATE_ROWS if side else 0
        bt = 8 - COEF_ROWS if side else 0
        for l in range(NG):
            lanes = slice(128 * l, 128 * l + 128)
            base = XROWS * l
            for k in range(LV):
                n = base + k * STATE_ROWS
                ref[n : n + STATE_ROWS, :] = state[side, k, at : at + STATE_ROWS, lanes]
                n = base + COEF_AT + k * COEF_ROWS
                ref[n : n + COEF_ROWS, :] = diffuse[side, k, bt : bt + COEF_ROWS, lanes]
            n = base + VERT_AT
            ref[n : n + COEF_ROWS, :] = vertical[40 * side + bt : 40 * side + bt + COEF_ROWS, lanes]
            ref[n + COEF_ROWS : base + XROWS, :] = jnp.zeros((XROWS - VERT_AT - COEF_ROWS, 128), jnp.float32)
        for which, strips in enumerate((from_low, from_high)):
            for l in range(NG):
                part = strips[40 * side : 40 * side + 8, 128 * l : 128 * l + 128]
                if which == 0 and l == NG - 1:
                    part = jnp.where(clear, part, colpack[40 * side : 40 * side + 8, :])
                n = CORNER_AT + 8 * (NG * which + l)
                ref[n : n + 8, :] = part

    @pl.when(odd)
    def _():
        rows(xa, 1)
        rows(xb, 0)

    @pl.when(jnp.logical_not(odd))
    def _():
        rows(xa, 0)
        rows(xb, 1)


def join_kernel(count_x, count_y, *refs):
    ins, (out_x, out_y) = refs[:-2], refs[-2:]
    for out, parts in ((out_x, ins[:count_x]), (out_y, ins[count_x : count_x + count_y])):
        at = 0
        for part in parts:
            size = 1 if part.shape[0] == FIRST else part.shape[0]
            out[at : at + size] = part[0:size]
            at += size


def edge_kernel(count_x, count_y, plan_x, plan_y, pack, from_low, from_high, interp, *refs):
    chain_x, refs = refs[: len(plan_x)], refs[len(plan_x) :]
    chain_y, refs = refs[: len(plan_y)], refs[len(plan_y) :]
    (edges,) = refs
    nx, ny = lax.axis_index("nx"), lax.axis_index("ny")
    border_x = (nx == 0) | (nx == count_x - 1)
    border_y = (ny == 0) | (ny == count_y - 1)
    inner_x = (nx == 1) | (nx == count_x - 2)
    inner_y = (ny == 1) | (ny == count_y - 2)

    @pl.when((border_x & jnp.logical_not(inner_y)) | (inner_x & inner_y))
    def _():
        lane1 = lax.broadcasted_iota(jnp.int32, (1, 128), 1)
        for l in range(NG + 1):
            got = []
            for item in range(2):
                if l < NG:
                    got.append(interp[item : item + 1, 128 * l : 128 * l + 128])
                else:
                    got.append(
                        jnp.where(
                            lane1 < 64,
                            pltpu.roll(from_high[0:8, 256:384], 112, 1)[item : item + 1],
                            pltpu.roll(from_low[0:8, 256:384], 104, 1)[item : item + 1],
                        )
                    )
            index = jnp.broadcast_to(got[0], (48, 128)).astype(jnp.int32)
            ends = []
            for offset in range(2):
                at = index + offset
                block, inside = at >> 7, at & 127
                total = jnp.zeros((48, 128), jnp.float32)
                for ref, masks in zip(chain_y, plan_y, strict=True):
                    for piece, mask in enumerate(masks):
                        value = jnp.take_along_axis(ref[piece], inside, axis=1, mode="promise_in_bounds")
                        total = jnp.where(block == (ny ^ mask), value, total)
                ends.append(total)
            edges[64 + 48 * l : 112 + 48 * l, :] = (1.0 - got[1]) * ends[0] + got[1] * ends[1]

    @pl.when((border_y & jnp.logical_not(border_x)) | (border_x & inner_y))
    def _():
        index = pack[:, 64:65].astype(jnp.int32)
        weight = pack[:, 65:66]
        total = jnp.zeros((64, 128), jnp.float32)
        for ref, masks in zip(chain_x, plan_x, strict=True):
            size = 16 * len(masks)
            at = lax.broadcasted_iota(jnp.int32, (1, size), 1)
            ids = at & 15
            for piece, mask in enumerate(masks):
                ids = jnp.where(at >> 4 == piece, ids + 16 * (nx ^ mask), ids)
            spread = jnp.where(ids == index, 1.0 - weight, 0.0) + jnp.where(ids == index + 1, weight, 0.0)
            total += jnp.dot(
                spread,
                ref[...].reshape(size, 128),
                preferred_element_type=jnp.float32,
                precision=lax.Precision.HIGHEST,
            )
        edges[0:64, :] = total


def prepare_kernel(
    state, diffuse, vertical_hbm, ra, rb, from_low, from_high, colpack, es, ed, ev, inv, pack, strip, vertical, sem
):
    nx = lax.axis_index("nx")
    copies = []
    for which, (src, dst) in enumerate(((state, es), (diffuse, ed))):
        for l in range(NG):
            copy = pltpu.make_async_copy(
                src.at[:, :, pl.ds(128 * l, 128)], dst.at[:, l, pl.ds(HX, WX), :], sem.at[NG * which + l]
            )
            copy.start()
            copies.append(copy)
    first_copies = [
        pltpu.make_async_copy(vertical_hbm, vertical, sem.at[2 * NG]),
    ]
    for copy in first_copies:
        copy.start()
    odd = nx % 2 == 1
    lane64 = lax.broadcasted_iota(jnp.int32, (64, 128), 1)

    def beyond(at, size, l):
        a, b = ra[XROWS * l + at : XROWS * l + at + size, :], rb[XROWS * l + at : XROWS * l + at + size, :]
        return jnp.where(odd, b, a), jnp.where(odd, a, b)

    for copy in first_copies:
        copy.wait()
    for l in range(NG):
        for k in range(LV):
            low, high = beyond(k * STATE_ROWS, STATE_ROWS, l)
            es[k, l, HX - STATE_ROWS : HX, :] = low
            es[k, l, HX + WX : HX + WX + STATE_ROWS, :] = high
            low, high = beyond(COEF_AT + k * COEF_ROWS, COEF_ROWS, l)
            ed[k, l, HX - COEF_ROWS : HX, :] = low
            ed[k, l, HX + WX : HX + WX + COEF_ROWS, :] = high
        low, high = beyond(VERT_AT, COEF_ROWS, l)
        ev[l, HX - COEF_ROWS : HX, :] = low
        ev[l, HX + WX : HX + WX + COEF_ROWS, :] = high
        ev[l, HX : HX + WX, :] = vertical[:, 128 * l : 128 * l + 128]

    def corner(side, l):
        n = CORNER_AT + 8 * (NG * side + l)
        a, b = ra[n : n + 8, :], rb[n : n + 8, :]
        return jnp.where(odd, b, a), jnp.where(odd, a, b)

    for side, ref in enumerate((from_low, from_high)):
        strip[side, HX : HX + WX, :] = ref[...]
        for l in range(NG):
            low, high = corner(side, l)
            strip[side, 0:HX, 128 * l : 128 * l + 128] = low
            strip[side, HX + WX : 64, 128 * l : 128 * l + 128] = high
    low, high = corner(0, NG - 1)
    pack[0:HX, :] = low
    pack[HX : HX + WX, :] = colpack[...]
    pack[HX + WX : 64, :] = high
    for which, dst in enumerate((es, ed)):
        lanes = slice(128 * which, 128 * which + 128)
        for k in range(LV):
            dst[k, NG, 0:64, :] = jnp.where(
                lane64 < 64,
                pltpu.roll(strip[1, :, lanes], (-8 * k) % 128, 1),
                pltpu.roll(strip[0, :, lanes], (120 - 8 * k) % 128, 1),
            )
    ev[NG, 0:64, :] = jnp.where(
        lane64 < 64, strip[1, :, 256:384], pltpu.roll(strip[0, :, 256:384], 120, 1)
    )


    @pl.loop(0, 8, unroll=True)
    def _(t):
        rows = pl.ds(pl.multiple_of(8 * t, 8), 8)
        for l in range(NG + 1):
            g = ev[l, rows, :]
            inverse = 1.0 / (1.0 + g)
            inv[0, l, rows, :] = inverse
            for k in range(1, LV):
                diagonal = 1.0 + (g if k == LV - 1 else 2.0 * g)
                inverse = 1.0 / (diagonal - g * (g * inverse))
                inv[k, l, rows, :] = inverse

    for copy in copies:
        copy.wait()


def main_kernel(
    count_x, count_y, jump, fill_we_hbm, from_low, from_high, es_in, ed, ev, inv, pack, edges, brought_ref,
    out, es, mv, gv, ey, ex, fill_we, sem,
):
    dx, dy = jump[0], jump[1]
    nx, ny = lax.axis_index("nx"), lax.axis_index("ny")
    lane = lax.broadcasted_iota(jnp.int32, (8, 128), 1)
    fetch = pltpu.make_async_copy(fill_we_hbm, fill_we, sem)
    fetch.start()
    west, east = nx == 0, nx == count_x - 1
    south, north = ny == 0, ny == count_y - 1

    @pl.when(west | east)
    def _():
        brought = (ny == 1) | (ny == count_y - 2)
        for l in range(NG + 1):
            rows = slice(64 + 48 * l, 112 + 48 * l)
            ey[l] = jnp.where(brought, brought_ref[rows, :], edges[rows, :])

    @pl.when(south | north)
    def _():
        ex[...] = jnp.where(west | east, brought_ref[0:64, :], edges[0:64, :])

    def ghosts(field, step, row_low, row_high, shift):
        @pl.when(west)
        def _():
            for k in range(LV):
                for l in range(NG + 1):
                    field[k, l, row_low : row_low + 1, :] = ey[l, 16 * step + k : 16 * step + k + 1, :]

        @pl.when(east)
        def _():
            for k in range(LV):
                for l in range(NG + 1):
                    field[k, l, row_high : row_high + 1, :] = ey[l, 16 * step + k : 16 * step + k + 1, :]

        @pl.when(south | north)
        def _():
            at = jnp.where(south, 127, 0)
            lanes = lax.broadcasted_iota(jnp.int32, (56, 128), 1)
            for k in range(LV):
                col = ex[shift : shift + 56, 16 * step + k : 16 * step + k + 1]
                field[k, NG, 0:56, :] = jnp.where(lanes == at, col, field[k, NG, 0:56, :])

    def ghost_tail(step):
        @pl.when(south | north)
        def _():
            at = jnp.where(south, 127, 0)
            for k in range(LV):
                col = ex[56:64, 16 * step + k : 16 * step + k + 1]
                es[k, NG, 56:64, :] = jnp.where(lane == at, col, es[k, NG, 56:64, :])

    ghosts(es, 0, HX - 1, HX + WX, 0)
    ghost_tail(0)

    def sideways(c):
        lefts = [pltpu.roll(x, 1, 1) for x in c]
        rights = [pltpu.roll(x, 127, 1) for x in c]
        n = len(c)
        left = [jnp.where(lane == 0, lefts[l - 1], lefts[l]) for l in range(n)]
        right = [jnp.where(lane == 127, rights[(l + 1) % n], rights[l]) for l in range(n)]
        return left, right

    def advance(field, at, coef_at, groups, write_source, read_source, write):
        g = [ev[l, pl.ds(coef_at, 8), :] for l in range(groups)]
        source = [None] * groups
        for k in range(LV):
            c = [field[k, l, pl.ds(at, 8), :] for l in range(NG + 1)]
            left, right = sideways(c)
            for l in range(groups):
                lap = (
                    field[k, l, pl.ds(at + 1, 8), :]
                    + field[k, l, pl.ds(at - 1, 8), :]
                    + right[l]
                    + left[l]
                    - 4.0 * c[l]
                )
                explicit = c[l] + ed[k, l, pl.ds(coef_at, 8), :] * lap
                if k > 0:
                    explicit = explicit + g[l] * source[l]
                source[l] = explicit * inv[k, l, pl.ds(coef_at, 8), :]
                if k < LV - 1:
                    write_source(k, l, source[l])
        value = source
        write(LV - 1, value)
        for k in range(LV - 2, -1, -1):
            value = [
                read_source(k, l) + (g[l] * inv[k, l, pl.ds(coef_at, 8), :]) * value[l] for l in range(groups)
            ]
            write(k, value)

    turn = (128 - 3 * dy) % 128

    @pl.loop(0, 7, unroll=True)
    def _(t):
        to = pl.multiple_of(8 * t, 8)

        def put(k, l, x):
            mv[k, l, pl.ds(to, 8), :] = x

        def take(k, l):
            return mv[k, l, pl.ds(to, 8), :]

        def moved(k, values):
            turned = [pltpu.roll(x, turn, 1) for x in values]
            for l in range(NG + 1):
                x = jnp.where(lane >= 128 - 3 * dy, turned[(l + 1) % (NG + 1)], turned[l])
                put(k, l, jnp.where(lane < -3 * dy, turned[l - 1], x))

        at = HX - 2 + 3 * dx + 8 * t
        advance(es, at, at, NG + 1, put, take, moved)

    @pl.when((south & (dy < 0)) | (north & (dy > 0)))
    def _():
        row = lax.broadcasted_iota(jnp.int32, (56, 128), 0)
        cell = (((row + 4) * 21846) >> 16) - 2 + dx
        lanes = lax.broadcasted_iota(jnp.int32, (56, 128), 1)
        total = jnp.zeros((56, 128), jnp.float32)
        for q in range(-2, 18):
            r = q + 8 if q < 0 else (q + HX if q < 8 else q + 40)
            total = jnp.where(cell == q, pack[r : r + 1, :], total)

        for is_side, side, l, first in ((south, 0, 0, 0), (north, 1, NG - 1, 125)):

            @pl.when(is_side)
            def _():
                inside = (lanes >= first) & (lanes < first + 3)
                for k in range(LV):
                    n = 96 + 16 * side + k
                    mv[k, l, 0:56, :] = jnp.where(inside, total[:, n : n + 1], mv[k, l, 0:56, :])

    fetch.wait()

    @pl.when((west & (dx < 0)) | (east & (dx > 0)))
    def _():
        lane16 = lax.broadcasted_iota(jnp.int32, (16, 128), 1)
        for is_side, side, first in ((west, 0, 2), (east, 1, 47)):

            @pl.when(is_side)
            def _():
                own = fill_we[side]
                ring = jnp.where(
                    lane16 < 64,
                    pltpu.roll(from_high[16 * side : 16 * side + 16, 256:384], 120, 1),
                    pltpu.roll(from_low[16 * side : 16 * side + 16, 256:384], 112, 1),
                )
                for l in range(NG + 1):
                    column = lane16 + 128 * l
                    if l == NG:
                        column = jnp.where(lane16 < 64, column, lane16 - 128)
                    cell = (((column + 384) * 21846) >> 16) - 128 + dy
                    cell = jnp.clip(cell, -128 * ny, 128 * (count_y - ny) - 1)
                    inside = cell & 127
                    a = jnp.take_along_axis(own, inside, axis=1, mode="promise_in_bounds")
                    b = jnp.take_along_axis(ring, inside, axis=1, mode="promise_in_bounds")
                    ey[l, 0:16, :] = jnp.where((cell >= 0) & (cell < 128), a, b)
                    for k in range(LV):
                        mv[k, l, first : first + 3, :] = jnp.broadcast_to(ey[l, k : k + 1, :], (3, 128))

    ghosts(mv, 1, 1, WX + 2, HX - 2)

    @pl.loop(0, 7, unroll=True)
    def _(t):
        to = pl.multiple_of(8 * t, 8)

        def put(k, l, x):
            gv[k, l, pl.ds(to, 8), :] = x

        def take(k, l):
            return gv[k, l, pl.ds(to, 8), :]

        def keep(k, values):
            for l in range(NG + 1):
                put(k, l, values[l])

        advance(mv, 1 + 8 * t, HX - 1 + 8 * t, NG + 1, put, take, keep)

    ghosts(gv, 2, 0, WX + 1, HX - 1)

    @pl.loop(0, 6, unroll=True)
    def _(t):
        to = pl.multiple_of(8 * t, 8)

        def put(k, l, x):
            out[k, pl.ds(to, 8), 128 * l : 128 * l + 128] = x

        def take(k, l):
            return out[k, pl.ds(to, 8), 128 * l : 128 * l + 128]

        def keep(k, values):
            for l in range(NG):
                put(k, l, values[l])

        advance(gv, 1 + 8 * t, HX + 8 * t, NG, put, take, keep)


def on_device(
    state,
    diffuse,
    vertical,
    rows_we,
    rows_sn,
    fill_we,
    fill_sn,
    index_we,
    weight_we,
    index_sn,
    weight_sn,
    jump,
):
    f32 = jnp.float32
    count_x, count_y = lax.axis_size("nx"), lax.axis_size("ny")
    both = ("nx", "ny")
    vmem = pl.BlockSpec(memory_space=pltpu.VMEM)
    smem = pl.BlockSpec(memory_space=pltpu.SMEM)
    hbm = pl.BlockSpec(memory_space=pltpu.HBM)
    any_ = pl.BlockSpec(memory_space=pl.ANY)

    def shape(*dims):
        return jax.ShapeDtypeStruct(dims, f32)

    state, diffuse, vertical, rows_we, rows_sn, fill_we, fill_sn, index_we, weight_we, index_sn, weight_sn = (
        pltpu.with_memory_space_constraint(x, pltpu.HBM)
        for x in (
            state, diffuse, vertical, rows_we, rows_sn, fill_we, fill_sn, index_we, weight_we, index_sn, weight_sn
        )
    )
    y_low, y_high, chain_x, chain_y, colpack, interp = pl.pallas_call(
        pack_kernel,
        out_shape=(
            shape(WX, WY),
            shape(WX, WY),
            shape(FIRST, 16, 128),
            shape(1, 48, 128),
            shape(WX, 128),
            shape(8, WY),
        ),
        in_specs=[hbm] * 11,
        out_specs=(vmem,) * 6,
        scratch_shapes=[
            pltpu.VMEM((2, LV, WX, 128), f32),
            pltpu.VMEM((2, LV, WX, 128), f32),
            pltpu.VMEM((WX, WY), f32),
            pltpu.VMEM((3, 16, 128), f32),
            pltpu.VMEM((3, 16, 16), f32),
            pltpu.VMEM((2, 16, 128), f32),
            pltpu.VMEM((2, 16, 16), f32),
            pltpu.VMEM((WY,), jnp.int32),
            pltpu.VMEM((WY,), f32),
            pltpu.VMEM((WX,), jnp.int32),
            pltpu.VMEM((WX,), f32),
            pltpu.VMEM((128, 128), f32),
            pltpu.SemaphoreType.DMA((13,)),
        ],
        compiler_params=pltpu.CompilerParams(vmem_limit_bytes=16 << 20),
        name="pack",
    )(state, diffuse, vertical, rows_we, rows_sn, fill_we, fill_sn, index_we, weight_we, index_sn, weight_sn)

    pairs_a = [(i, i + 1) for i in range(1, count_x - 1, 2)]
    pairs_a += [(b, a) for a, b in pairs_a]
    pairs_b = [(i, i + 1) for i in range(0, count_x, 2)]
    pairs_b += [(b, a) for a, b in pairs_b]
    up = [(i, i + 1) for i in range(count_y - 1)]
    down = [(b, a) for a, b in up]
    rounds_x, rounds_y = rounds_of(count_x), rounds_of(count_y)

    def place(i, j):
        return i * count_y + j

    last_x, last_y = count_x - 1, count_y - 1
    set_x = [
        [place(i, (1 if i in (0, last_x) else 0) if side == 0 else (last_y - 1 if i in (0, last_x) else last_y))
         for i in range(count_x)]
        for side in range(2)
    ]
    set_y = [
        [place((1 if j in (1, last_y - 1) else 0) if side == 0 else (last_x - 1 if j in (1, last_y - 1) else last_x), j)
         for j in range(count_y)]
        for side in range(2)
    ]
    bring = []
    for i, step in ((0, 1), (last_x, -1)):
        for j, other in ((0, 1), (last_y, last_y - 1)):
            bring.append((place(i, other), place(i, j)))
            bring.append((place(i + step, other), place(i, other)))

    def along(sets, chain, masks):
        return [
            lax.ppermute(chain, both, [(own[n], own[n ^ m]) for own in sets for n in range(len(own))]) for m in masks
        ]

    along_x, along_y = functools.partial(along, set_x), functools.partial(along, set_y)

    def join(parts_x, parts_y, size_x, size_y, name):
        return pl.pallas_call(
            functools.partial(join_kernel, len(parts_x), len(parts_y)),
            out_shape=(
                shape(size_x, 16, 128),
                shape(size_y, 48, 128),
            ),
            in_specs=[vmem] * (len(parts_x) + len(parts_y)),
            out_specs=(vmem, vmem),
            compiler_params=pltpu.CompilerParams(vmem_limit_bytes=8 << 20),
            name=name,
        )(*parts_x, *parts_y)

    parts_x = [chain_x] + along_x(chain_x, rounds_x[0])
    parts_y = [chain_y] + along_y(chain_y, rounds_y[0])
    from_low = lax.ppermute(y_high, "ny", up)
    from_high = lax.ppermute(y_low, "ny", down)
    xa, xb = pl.pallas_call(
        border_kernel,
        out_shape=(shape(SENT, 128), shape(SENT, 128)),
        in_specs=[any_] * 2 + [hbm] * 3 + [vmem] * 3,
        out_specs=(vmem, vmem),
        scratch_shapes=[
            pltpu.VMEM((2, LV, 8, WY), f32),
            pltpu.VMEM((2, LV, 8, WY), f32),
            pltpu.VMEM((WX, WY), f32),
            pltpu.SemaphoreType.DMA((5,)),
        ],
        compiler_params=pltpu.CompilerParams(vmem_limit_bytes=8 << 20),
        name="border",
    )(parts_x[-1], colpack, state, diffuse, vertical, from_low, from_high, colpack)
    ra = lax.ppermute(xa, "nx", pairs_a)
    rb = lax.ppermute(xb, "nx", pairs_b)
    chain_x, chain_y = join(parts_x, parts_y, len(masks_of(rounds_x[:1])), len(masks_of(rounds_y[:1])), "join_first")
    parts_x = [chain_x] + along_x(chain_x, rounds_x[1])
    parts_y = [chain_y] + along_y(chain_y, rounds_y[1])
    chain_x, chain_y = join(parts_x, parts_y, len(masks_of(rounds_x[:2])), len(masks_of(rounds_y[:2])), "join_second")
    parts_x = [chain_x] + along_x(chain_x, rounds_x[2])
    parts_y = [chain_y] + along_y(chain_y, rounds_y[2])
    big = (LV, NG + 1, 72, 128)
    es, ed, ev, inv, pack = pl.pallas_call(
        prepare_kernel,
        out_shape=(shape(*big), shape(*big), shape(NG + 1, 72, 128), shape(*big), shape(64, 128)),
        in_specs=[hbm] * 3 + [vmem] * 5,
        out_specs=(vmem,) * 5,
        scratch_shapes=[
            pltpu.VMEM((2, 64, WY), f32),
            pltpu.VMEM((WX, WY), f32),
            pltpu.SemaphoreType.DMA((2 * NG + 1,)),
        ],
        compiler_params=pltpu.CompilerParams(vmem_limit_bytes=12 << 20),
        name="prepare",
    )(state, diffuse, vertical, ra, rb, from_low, from_high, colpack)
    have_x, have_y = masks_of(rounds_x[:2]), masks_of(rounds_y[:2])
    plan_x = [[m ^ h for h in have_x] for m in [0] + rounds_x[2]]
    plan_y = [[m ^ h for h in have_y] for m in [0] + rounds_y[2]]

    edges = pl.pallas_call(
        functools.partial(edge_kernel, count_x, count_y, plan_x, plan_y),
        out_shape=shape(256, 128),
        in_specs=[vmem] * (4 + len(parts_x) + len(parts_y)),
        out_specs=vmem,
        compiler_params=pltpu.CompilerParams(vmem_limit_bytes=8 << 20),
        name="edges",
    )(pack, from_low, from_high, interp, *parts_x, *parts_y)
    brought = lax.ppermute(edges, both, bring)

    return pl.pallas_call(
        functools.partial(main_kernel, count_x, count_y),
        out_shape=(shape(LV, WX, WY), shape(*big)),
        in_specs=[smem, hbm] + [vmem] * 9,
        out_specs=(vmem, vmem),
        scratch_shapes=[
            pltpu.VMEM((LV, NG + 1, 64, 128), f32),
            pltpu.VMEM((LV, NG + 1, 64, 128), f32),
            pltpu.VMEM((NG + 1, 48, 128), f32),
            pltpu.VMEM((64, 128), f32),
            pltpu.VMEM((2, 16, 128), f32),
            pltpu.SemaphoreType.DMA,
        ],
        input_output_aliases={4: 1},
        compiler_params=pltpu.CompilerParams(vmem_limit_bytes=20 << 20),
        name="steps",
    )(jump, fill_we, from_low, from_high, es, ed, ev, inv, pack, edges, brought)[0]


def solution(mesh):
    return jax.shard_map(
        on_device,
        mesh=mesh,
        in_specs=(
            P(None, "nx", "ny"),
            P(None, "nx", "ny"),
            P("nx", "ny"),
            P(None, None, None, "ny"),
            P(None, None, None, "nx"),
            P(None, None, "ny"),
            P(None, None, "nx"),
            P("ny"),
            P("ny"),
            P("nx"),
            P("nx"),
            P(),
        ),
        out_specs=P(None, "nx", "ny"),
        check_vma=False,
    )
```
